32 devices in a mesh: fsdp: 4 (over z), ctx: 4 (over y, core), tp: 2 (over x).
Axes of the slice: x: 2, y: 2, z: 4, core: 2. Of those that a mesh axis runs over, the one named last changes fastest.
Arguments:
- block_in: bfloat16 [8, 2048, 768], P('fsdp', 'ctx'), may hold values from -6 to 6
- cotangent: bfloat16 [8, 2048, 768], P('fsdp', 'ctx'), may hold values from -6 to 6
- prev_logits: float32 [8, 2048, 8], P('fsdp', 'ctx'), may hold values from -3 to 3
- routes: int32 [8, 2048, 2], P('fsdp', 'ctx'), may hold values from 0 to 7, all different within a row; in each aligned block of 512 rows (0 to 511, 512 to 1023, ..., all dimensions but the last counted through in order) at most 192 rows name the same one
- segments: int32 [8, 2048], P('fsdp', 'ctx'), may hold values from 0 to 4, as said below
- w_query: float32 [768, 768], P('fsdp', 'tp'), may hold values from -0.3125 to 0.3125
- w_key: float32 [768, 768], P('fsdp', 'tp'), may hold values from -0.3125 to 0.3125
- w_value: float32 [768, 768], P('fsdp', 'tp'), may hold values from -0.21875 to 0.21875
- w_out: float32 [768, 768], P('fsdp', 'tp'), may hold values from -0.875 to 0.875
- w_gate: float32 [4, 768, 2048], P(None, 'fsdp', 'tp'), may hold values from -0.21875 to 0.21875
- w_up: float32 [4, 768, 2048], P(None, 'fsdp', 'tp'), may hold values from -0.21875 to 0.21875
- w_down: float32 [4, 768, 2048], P(None, 'fsdp', 'tp'), may hold values from -0.125 to 0.125
- router: float32 [768, 8], P('fsdp'), may hold values from -0.125 to 0.125
- const_proj: float32 [768, 4], P('fsdp'), may hold values from -0.21875 to 0.21875
- const_vec: float32 [768, 2], P('fsdp'), may hold values from -5 to 5
- norm_attn: float32 [768], P('fsdp'), may hold values from 0.5 to 1.5
- norm_moe: float32 [768], P('fsdp'), may hold values from 0.5 to 1.5
Outputs:
- layer_out: bfloat16 [8, 2048, 768], P('fsdp', 'ctx')
- grad_input: float32 [8, 2048, 768], P('fsdp', 'ctx')
- grad_query: float32 [768, 768], P('fsdp', 'tp')
- grad_key: float32 [768, 768], P('fsdp', 'tp')
- grad_value: float32 [768, 768], P('fsdp', 'tp')
- grad_out: float32 [768, 768], P('fsdp', 'tp')
- grad_gate: float32 [4, 768, 2048], P(None, 'fsdp', 'tp')
- grad_up: float32 [4, 768, 2048], P(None, 'fsdp', 'tp')
- grad_down: float32 [4, 768, 2048], P(None, 'fsdp', 'tp')
- grad_router: float32 [768, 8], P('fsdp')
- grad_const_proj: float32 [768, 4], P('fsdp')
- grad_const_vec: float32 [768, 2], P('fsdp')
- grad_norm_attn: float32 [768], P('fsdp')
- grad_norm_moe: float32 [768], P('fsdp')
The draws below stay inside these ranges and needn't reach their ends.
Inputs may be any that keep to these rules, and one draw needn't show every extreme that they name: `routes`: each token names two different targets: 0 to 3 the feed-forward experts, 4 the zero expert, 5 the copy expert, 6 and 7 the constant experts. In each aligned block of 512 tokens (the positions of one sequence on one index of ctx) no target is named by more than 192 tokens, a bound that some block reaches. `segments`: along each sequence the numbers start at 0 and never fall; equal numbers form one document. One document of each sequence starts within its first 512 positions and ends within its last 512.
All inputs are finite; a program needn't handle non-finite values.
Results may differ from the reference program's by a relative error of at most 0.02.
The reference program's roundings to bfloat16 on the way count: a program that leaves them out, or rounds other values in their place, can miss the bound.
Values may be sent and summed in bfloat16 or wider, within the bound.
No kernel may reach another device: no remote copies, remote signals or barrier semaphores. Data moves between devices by JAX's collectives and lax.ppermute only.
A program may use at most 256 MiB of HBM per device.

```python
import math
import jax
import jax.numpy as jnp
import numpy as np
from jax import lax

D = 768
HEADS = 12
HD = 64
FF = 2048
EXPERTS = 4
ALL = 8
SHARD_LEN = 512
NSEQ = 8
SEQ = 2048
WINDOW = 1024
MOST = 192
N_CTX = 4


def cut_sequence(key):
    pieces = jax.random.split(key, 4)
    first_cut = jax.random.randint(pieces[0], (), 1, SHARD_LEN // 2 + 1, dtype=jnp.int32)
    long_start = first_cut + 1 + jax.random.randint(pieces[1], (), 0, SHARD_LEN - 1 - first_cut, dtype=jnp.int32)
    long_end = jax.random.randint(pieces[2], (), SEQ - SHARD_LEN + 1, SEQ - SHARD_LEN // 2 + 1, dtype=jnp.int32)
    last_cut = long_end + 1 + jax.random.randint(pieces[3], (), 0, SEQ - 1 - long_end, dtype=jnp.int32)
    places = jnp.arange(SEQ, dtype=jnp.int32)
    return (places >= first_cut).astype(jnp.int32) + (places >= long_start).astype(jnp.int32) + (places >= long_end).astype(jnp.int32) + (places >= last_cut).astype(jnp.int32)


def draw_segments(key, part):
    key = jax.random.fold_in(key, 7)
    return jax.vmap(cut_sequence)(jax.random.split(key, NSEQ))


def block_levels(stream_key, shape, cuts, smallest, high):
    gain, own = 1.0, jax.random.fold_in(stream_key, 6)
    for dim, blocks in cuts:
        draws = jnp.exp(jax.random.uniform(jax.random.fold_in(own, dim), (blocks,), jnp.float32, smallest / len(cuts), high / len(cuts)))
        gain = gain * jnp.repeat(draws, shape[dim] // blocks).reshape([-1 if axis == dim else 1 for axis in range(len(shape))])
    return gain


def routed_block(own_key, own, number, rows, count, top, bound, slope):
    order = jax.random.permutation(own_key, count)
    heavy_load, common = shares(count, rows * top, bound, slope, True), shares(count, rows * top, bound, slope, False)
    places = jnp.arange(count)

    def named(tallies, turn):
        used = int((tallies > 0).sum())
        fixed = max(1, used // 4)
        shifted = fixed + (places - fixed + turn * (used - fixed)) % max(1, count - fixed)
        return jnp.zeros((count,), jnp.int32).at[order[jnp.where(places < fixed, places, shifted)]].set(jnp.asarray(tallies, jnp.int32))

    tallies = jnp.where(number % 4 == 0, named(heavy_load, number // 4), named(common, number - number // 4 - 1))
    mixed = jax.random.permutation(jax.random.fold_in(own, 3), count)
    source_of, taker = mixed[0:count // 2 * 2:2], mixed[1:count // 2 * 2:2]
    slack = jnp.minimum(tallies[source_of] - 1, bound - tallies[taker]) // 2
    slack = jnp.where((source_of == order[0]) | (taker == order[0]) | (tallies[taker] == 0), 0, jnp.maximum(slack, 0))
    shifted = jax.random.randint(jax.random.fold_in(own, 4), (count // 2,), 0, 1 << 20) % (slack + 1)
    tallies = tallies.at[source_of].add(-shifted).at[taker].add(shifted)
    members = jnp.searchsorted(jnp.cumsum(tallies), jnp.arange(rows * top), side="right").astype(jnp.int32)
    table = members.reshape(top, rows).T
    table = table[jax.random.permutation(jax.random.fold_in(own, 1), rows)]
    turn = jax.random.randint(jax.random.fold_in(own, 2), (rows, 1), 0, top)
    return jnp.take_along_axis(table, (jnp.arange(top)[None, :] + turn) % top, axis=1)


def shares(amount, total, most, skew, full):
    loads = [(1 << 20) // math.isqrt(rank ** skew) + 1 for rank in range(1, amount + 1)]
    largest = most if full else min(most, max(-(-total // amount), total * loads[0] // sum(loads)))
    least = 1 if total - largest >= amount - 1 else 0
    counts, surplus = [largest] + [least] * (amount - 1), total - largest - least * (amount - 1)
    while surplus > 0:
        movable = [i for i in range(1, amount) if counts[i] < largest] or [i for i in range(1, amount) if counts[i] < most]
        whole, remaining = sum([loads[i] for i in movable]), surplus
        for i in movable:
            more = min(most - counts[i], max(1, remaining * loads[i] // whole), surplus)
            counts[i] = counts[i] + more
            surplus = surplus - more
    return np.array(counts)


def scatter_about(rng, shape, scale, most, shards=(), kind=jnp.bfloat16):
    drawn = scale * jax.random.normal(rng, shape, jnp.float32)
    if shards:
        drawn = drawn * block_levels(rng, shape, shards, -0.22, 0.18)
    return jnp.clip(drawn, -most, most).astype(kind)


def setup_inputs(seed: int = 0) -> dict:
    key_of = jax.random.split(jax.random.key(seed), 18)
    block_in = scatter_about(key_of[0], (NSEQ, SEQ, D), 1.0, 6.0, ((0, 4), (1, 4)))
    cotangent = scatter_about(key_of[1], (NSEQ, SEQ, D), 1.0, 6.0, ((0, 4), (1, 4)))
    prev_logits = scatter_about(key_of[2], (NSEQ, SEQ, ALL), 0.4, 3.0, ((0, 4), (1, 4)), jnp.float32)
    routes_keys = jax.random.split(jax.random.fold_in(key_of[3], 1), NSEQ * SEQ // SHARD_LEN)
    routes_turns = jax.random.permutation(jax.random.fold_in(key_of[3], 3), NSEQ * SEQ // SHARD_LEN)
    routes = jax.vmap(lambda own, number: routed_block(jax.random.fold_in(key_of[3], 2), own, number, SHARD_LEN, ALL, 2, MOST, 1))(routes_keys, routes_turns).reshape((NSEQ, SEQ, 2))
    segments = draw_segments(jax.random.fold_in(key_of[17], 71), 0)
    w_query = scatter_about(key_of[5], (D, HEADS * HD), (D // 2) ** -0.5, 0.3125, ((0, 4), (1, 2)), jnp.float32)
    w_key = scatter_about(key_of[6], (D, HEADS * HD), (D // 2) ** -0.5, 0.3125, ((0, 4), (1, 2)), jnp.float32)
    w_value = scatter_about(key_of[7], (D, HEADS * HD), D ** -0.5, 0.21875, ((0, 4), (1, 2)), jnp.float32)
    w_out = scatter_about(key_of[8], (D, HEADS * HD), (D // 16) ** -0.5, 0.875, ((0, 4), (1, 2)), jnp.float32)
    w_gate = scatter_about(key_of[9], (EXPERTS, D, FF), D ** -0.5, 0.21875, ((1, 4), (2, 2)), jnp.float32)
    w_up = scatter_about(key_of[10], (EXPERTS, D, FF), D ** -0.5, 0.21875, ((1, 4), (2, 2)), jnp.float32)
    w_down = scatter_about(key_of[11], (EXPERTS, D, FF), FF ** -0.5, 0.125, ((1, 4), (2, 2)), jnp.float32)
    router = scatter_about(key_of[12], (D, ALL), (3 * D) ** -0.5, 0.125, ((0, 4),), jnp.float32)
    const_proj = scatter_about(key_of[13], (D, 4), D ** -0.5, 0.21875, ((0, 4),), jnp.float32)
    const_vec = scatter_about(key_of[14], (D, 2), 1.0, 5.0, ((0, 4),), jnp.float32)
    norm_attn = jnp.clip(1.0 + 0.1 * jax.random.normal(key_of[15], (D,), jnp.float32), 0.5, 1.5)
    norm_moe = jnp.clip(1.0 + 0.1 * jax.random.normal(key_of[16], (D,), jnp.float32), 0.5, 1.5)
    return {"block_in": block_in, "cotangent": cotangent, "prev_logits": prev_logits, "routes": routes, "segments": segments, "w_query": w_query, "w_key": w_key, "w_value": w_value, "w_out": w_out, "w_gate": w_gate, "w_up": w_up, "w_down": w_down, "router": router, "const_proj": const_proj, "const_vec": const_vec, "norm_attn": norm_attn, "norm_moe": norm_moe}


EPSILON = 1e-06
MASKED = -1e+30

@jax.custom_vjp
def low(v):
    return lax.optimization_barrier(v.astype(jnp.bfloat16)).astype(jnp.float32)

@jax.custom_vjp
def low_back(v):
    return v

def low_keep(v):
    return (low(v), None)

def low_pass(kept, grad):
    return (grad,)

def back_keep(v):
    return (v, None)

def back_low(kept, grad):
    return (low(grad),)
low.defvjp(low_keep, low_pass)
low_back.defvjp(back_keep, back_low)

def matmul_high(operand, partner):
    return jnp.dot(operand, partner, precision=lax.Precision.HIGHEST, preferred_element_type=jnp.float32)

def einsum_high(pattern, operand, partner):
    return jnp.einsum(pattern, operand.astype(jnp.float32), partner.astype(jnp.float32), precision=lax.Precision.HIGHEST, preferred_element_type=jnp.float32)

def angles(positions):
    frequency = 10000.0 ** (-2.0 * jnp.arange(HD // 2, dtype=jnp.float32) / HD)
    turned = positions.astype(jnp.float32)[:, None] * frequency[None, :]
    return (jnp.cos(turned)[:, None, :], jnp.sin(turned)[:, None, :])

def rotate(tensor, cosine, sine_part):
    middle = tensor.shape[-1] // 2
    leading = tensor[..., :middle]
    trailing = tensor[..., middle:]
    return jnp.concatenate([leading * cosine - trailing * sine_part, trailing * cosine + leading * sine_part], axis=-1)

def allowed_mask(query_place, query_ids, key_place, key_ids):
    same_document = query_ids[:, None] == key_ids[None, :]
    distance = query_place[:, None] - key_place[None, :]
    return same_document & (distance >= 0) & (distance < WINDOW) & (key_place[None, :] >= 0)

def place_slots(route_rows):
    flat_routes = route_rows.reshape(-1).astype(jnp.int32)
    slot_count = EXPERTS * MOST
    matches = (flat_routes[:, None] == jnp.arange(EXPERTS, dtype=jnp.int32)[None, :]).astype(jnp.int32)
    earlier = jnp.cumsum(matches, axis=0, dtype=jnp.int32) - matches
    ranking = lax.optimization_barrier(jnp.sum(earlier * matches, axis=1, dtype=jnp.int32))
    is_expert = flat_routes < EXPERTS
    target = jnp.where(is_expert, flat_routes * MOST + ranking, slot_count).astype(jnp.int32)
    pair_numbers = jnp.arange(flat_routes.shape[0], dtype=jnp.int32)
    slot_pair = jnp.zeros((slot_count + 1,), jnp.int32).at[target].set(pair_numbers)[:slot_count]
    filled = jnp.zeros((slot_count + 1,), jnp.float32).at[target].set(1.0)[:slot_count]
    pair_slot = jnp.where(is_expert, target, 0).astype(jnp.int32)
    return (slot_pair, filled, pair_slot, is_expert.astype(jnp.float32))

def pick_rows(source, indices):
    return source[indices]

def expert_outputs(routed, route_ids, w_gate, w_up, w_down):
    shard_rows = routed.reshape(N_CTX, SHARD_LEN, D)
    shard_routes = route_ids.reshape(N_CTX, SHARD_LEN, 2)
    slot_pair, filled, pair_slot, is_expert = jax.vmap(place_slots)(shard_routes)
    gathered = jax.vmap(pick_rows)(shard_rows, slot_pair // 2).reshape(N_CTX, EXPERTS, MOST, D)
    gate_pre = low_back(einsum_high('cemd,edf->cemf', gathered, w_gate))
    up_pre = low_back(einsum_high('cemd,edf->cemf', gathered, w_up))
    activated = low(jax.nn.silu(gate_pre) * up_pre)
    results = low_back(einsum_high('cemf,edf->cemd', activated, w_down))
    results = (results * filled.reshape(N_CTX, EXPERTS, MOST)[..., None]).reshape(N_CTX, EXPERTS * MOST, D)
    picked = jax.vmap(pick_rows)(results, pair_slot) * is_expert[..., None]
    return picked.reshape(SEQ, 2, D)

def attention(queries, key_rows, values, positions, segment_ids):
    block_rows = min(512, SEQ)
    block_count = SEQ // block_rows

    def one_block(pieces):
        query_block, query_place, query_ids = pieces
        scores = einsum_high('qhd,khd->hqk', query_block, key_rows) * HD ** (-0.5)
        allowed = allowed_mask(query_place, query_ids, positions, segment_ids)
        scores = low_back(jnp.where(allowed[None], scores, MASKED))
        highest = lax.optimization_barrier(jnp.max(scores, axis=-1, keepdims=True))
        raised = jnp.exp(scores - highest)
        chances = low(raised / lax.optimization_barrier(jnp.sum(raised, axis=-1, keepdims=True)))
        return einsum_high('hqk,khd->qhd', chances, values).reshape(block_rows, HEADS * HD)
    mixed = lax.map(jax.checkpoint(one_block), (queries.reshape(block_count, block_rows, HEADS, HD), positions.reshape(block_count, block_rows), segment_ids.reshape(block_count, block_rows)))
    return mixed.reshape(SEQ, HEADS * HD)

def forward(layer_in, prev_logit, route_ids, segment_ids, w_query, w_key, w_value, w_out, w_gate, w_up, w_down, router, const_proj, const_vec, norm_attn, norm_moe):
    w_query, w_key, w_value, w_out = (low(w_query), low(w_key), low(w_value), low(w_out))
    w_gate, w_up, w_down, router = (low(w_gate), low(w_up), low(w_down), low(router))
    const_proj, const_vec, norm_attn, norm_moe = (low(const_proj), low(const_vec), low(norm_attn), low(norm_moe))
    spread_one = lax.rsqrt(lax.optimization_barrier(jnp.mean(layer_in * layer_in, axis=-1, keepdims=True)) + EPSILON)
    normed = low(layer_in * spread_one * norm_attn)
    positions = jnp.arange(SEQ, dtype=jnp.int32)
    cosine, sine_part = angles(positions)
    queries = low(rotate(low_back(matmul_high(normed, w_query)).reshape(SEQ, HEADS, HD), cosine, sine_part))
    key_rows = low(rotate(low_back(matmul_high(normed, w_key)).reshape(SEQ, HEADS, HD), cosine, sine_part))
    values = low(low_back(matmul_high(normed, w_value))).reshape(SEQ, HEADS, HD)
    mixed_heads = low(low_back(attention(queries, key_rows, values, positions, segment_ids)))
    attended = low_back(matmul_high(mixed_heads, w_out.T))
    residual = layer_in + attended
    spread_two = lax.rsqrt(lax.optimization_barrier(jnp.mean(residual * residual, axis=-1, keepdims=True)) + EPSILON)
    routed = low(residual * spread_two * norm_moe)
    logits = low_back(matmul_high(routed, router) + prev_logit)
    gate_weights = jax.nn.softmax(jnp.take_along_axis(logits, route_ids, axis=-1), axis=-1)
    expert_part = expert_outputs(routed, route_ids, w_gate, w_up, w_down)
    const_scores = low_back(matmul_high(routed, const_proj))
    first_mix = jax.nn.softmax(const_scores[:, 0:2], axis=-1)
    second_mix = jax.nn.softmax(const_scores[:, 2:4], axis=-1)
    const_first = first_mix[:, 0:1] * routed + first_mix[:, 1:2] * const_vec[None, :, 0]
    const_second = second_mix[:, 0:1] * routed + second_mix[:, 1:2] * const_vec[None, :, 1]
    special = jnp.where((route_ids == EXPERTS + 1)[..., None], routed[:, None, :], 0.0) + jnp.where((route_ids == EXPERTS + 2)[..., None], const_first[:, None, :], 0.0) + jnp.where((route_ids == EXPERTS + 3)[..., None], const_second[:, None, :], 0.0)
    return residual + lax.optimization_barrier(jnp.sum(gate_weights[..., None] * (expert_part + special), axis=1))

def reference(block_in, cotangent, prev_logits, routes, segments, w_query, w_key, w_value, w_out, w_gate, w_up, w_down, router, const_proj, const_vec, norm_attn, norm_moe):
    weights = (w_query, w_key, w_value, w_out, w_gate, w_up, w_down, router, const_proj, const_vec, norm_attn, norm_moe)

    def one_sequence(totals, pieces):
        sequence_in, sequence_upstream, sequence_prev, sequence_routes, sequence_ids = pieces

        def layer(layer_in, *params):
            return forward(layer_in, sequence_prev, sequence_routes, sequence_ids, *params)
        result, pullback = jax.vjp(layer, sequence_in.astype(jnp.float32), *weights)
        gradients = pullback(sequence_upstream.astype(jnp.float32))
        totals = tuple((summed + fresh for summed, fresh in zip(totals, gradients[1:])))
        return (totals, (result.astype(jnp.bfloat16), gradients[0]))
    initial = tuple((jnp.zeros(weight.shape, jnp.float32) for weight in weights))
    totals, (outputs, input_grad) = lax.scan(one_sequence, initial, (block_in, cotangent, prev_logits, routes, segments))
    return (outputs, input_grad, totals[0], totals[1], totals[2], totals[3], totals[4], totals[5], totals[6], totals[7], totals[8], totals[9], totals[10], totals[11])
```

```python
import functools

import jax
import jax.numpy as jnp
from jax import lax
from jax.experimental import pallas as pl
from jax.experimental.pallas import tpu as pltpu
from jax.sharding import Mesh
from jax.sharding import PartitionSpec as P

D = 768
HEADS = 12
HD = 64
EXPERTS = 4
ALL = 8
WINDOW = 1024
MOST = 192

EPSILON = 1e-06
MASKED = -1e30

CTX = ("hi", "lo")
HALF = jnp.bfloat16
WIDE = jnp.float32
TILE = 256
PAIR = 2 * HD
SMALL = 16
MIB = 1 << 20


def nn(a, b):
    return jnp.dot(a, b, preferred_element_type=WIDE)


def nt(a, b):
    return lax.dot_general(a, b, (((1,), (1,)), ((), ())), preferred_element_type=WIDE)


def call(body, grid, ins, outs, scratch=(), flops=0, moved=0, prefetch=0, aliases=None):
    grid_spec = pltpu.PrefetchScalarGridSpec(
        num_scalar_prefetch=prefetch,
        grid=grid,
        in_specs=ins,
        out_specs=[spec for spec, _ in outs],
        scratch_shapes=list(scratch),
    )
    return pl.pallas_call(
        body,
        grid_spec=grid_spec,
        out_shape=[shape for _, shape in outs],
        input_output_aliases=aliases or {},
        compiler_params=pltpu.CompilerParams(
            dimension_semantics=("arbitrary",) * len(grid), vmem_limit_bytes=44 * MIB
        ),
        cost_estimate=pl.CostEstimate(
            flops=int(flops), bytes_accessed=int(moved), transcendentals=0
        ),
    )


def whole(shape):
    zeros = (0,) * len(shape)
    return pl.BlockSpec(shape, lambda *_: zeros)


def fixed(block, place):
    return pl.BlockSpec(block, lambda *_: place)


def struct(shape, dtype):
    return jax.ShapeDtypeStruct(shape, dtype)


def spread_of(tensor):
    return lax.rsqrt(jnp.mean(tensor * tensor, axis=-1, keepdims=True) + EPSILON)


def partner(tensor):
    lane = lax.broadcasted_iota(jnp.int32, tensor.shape, 1)
    return jnp.where(
        (lane & (HD // 2)) == 0,
        pltpu.roll(tensor, PAIR - HD // 2, 1),
        pltpu.roll(tensor, HD // 2, 1),
    )


def rank_kernel(routes_t, routes, rank_rows, rank_columns):
    count = routes.shape[1]
    down = lax.broadcasted_iota(jnp.int32, (count, count), 0)
    across = lax.broadcasted_iota(jnp.int32, (count, count), 1)
    before = jnp.where(down < across, 1.0, 0.0).astype(HALF)
    after = jnp.where(across < down, 1.0, 0.0).astype(HALF)
    row_target = lax.broadcasted_iota(jnp.int32, (ALL, count), 0)
    names = (routes_t[0, 0:1, :] == row_target) | (routes_t[0, 1:2, :] == row_target)
    ranks = nn(jnp.where(names, 1.0, 0.0).astype(HALF), before)
    rank_rows[0] = jnp.where(names, ranks, -1.0)
    column_target = lax.broadcasted_iota(jnp.int32, (count, ALL), 1)
    named = (routes[0, :, 0:1] == column_target) | (routes[0, :, 1:2] == column_target)
    ranked = nn(after, jnp.where(named, 1.0, 0.0).astype(HALF))
    rank_columns[0] = jnp.where(named, ranked, -1.0)


def project_kernel(with_query, *refs):
    x_ref, rows_ref, cos_ref, sin_ref, weights = refs[:5]
    outs = refs[5:]
    tensor = x_ref[0].astype(WIDE)
    unit = tensor * spread_of(tensor)
    normed = (unit * rows_ref[14:15, :].astype(WIDE)).astype(HALF)
    outs[0][0] = normed
    cosine, sine = cos_ref[0], sin_ref[0]

    def turned(matrix, out, scale):
        flat = nn(normed, weights[matrix])
        for piece in range(flat.shape[1] // PAIR):
            lanes = slice(piece * PAIR, (piece + 1) * PAIR)
            part = flat[:, lanes]
            result = (part * cosine + partner(part) * sine).astype(HALF)
            out[0, :, lanes] = result if scale is None else result * scale

    turned(1, outs[1], None)
    outs[2][0] = nn(normed, weights[2]).astype(HALF)
    if with_query:
        turned(0, outs[3], jnp.asarray(HD ** (-0.5), HALF))


def fill_bias(query_ids, key_ids, bias):
    upper = upper_of()
    for tile in range(2):
        ids = query_ids[0, tile * TILE : (tile + 1) * TILE, :]
        first = key_ids[0, :, tile * TILE : (tile + 1) * TILE]
        last = key_ids[0, :, (tile + 4) * TILE : (tile + 5) * TILE]
        mixed = jnp.where(upper, first, last)
        bias[tile, :, :TILE] = jnp.where(mixed == ids, 0.0, MASKED)
        inner = key_ids[0, :, (tile + 1) * TILE : (tile + 4) * TILE]
        bias[tile, :, TILE:] = jnp.where(inner == ids, 0.0, MASKED)


def upper_of():
    down = lax.broadcasted_iota(jnp.int32, (TILE, TILE), 0)
    across = lax.broadcasted_iota(jnp.int32, (TILE, TILE), 1)
    return across > down


def head_lanes(head, rows):
    lane = lax.broadcasted_iota(jnp.int32, (rows, PAIR), 1)
    return (lane < HD) if head == 0 else (lane >= HD)


def folded(upper, spread):
    span = spread.shape[1]
    return (
        jnp.where(upper, spread[:, :TILE], spread[:, span - TILE :]),
        spread[:, TILE : span - TILE],
    )


def unfolded(upper, ends, middle):
    return jnp.concatenate(
        [jnp.where(upper, ends, 0.0), middle, jnp.where(upper, 0.0, ends)], axis=1
    ).astype(HALF)


def load_window(parts, window):
    rows = parts[0].shape[1]
    for place, part in enumerate(parts):
        window[place * rows : (place + 1) * rows, :] = part[0]


def attend_kernel(
    query, k2, k1, k0, v2, v1, v0, query_ids, key_ids, w_out, mixed, logs, attended, bias, keys, values, total
):
    step = pl.program_id(0)

    @pl.when(step == 0)
    def _():
        fill_bias(query_ids, key_ids, bias)

    load_window((k2, k1, k0), keys)
    load_window((v2, v1, v0), values)
    upper = upper_of()
    span = 5 * TILE
    for tile in range(2):
        rows = slice(tile * TILE, (tile + 1) * TILE)
        window = slice(tile * TILE, tile * TILE + span)
        results, totals = [], []
        for head in range(2):
            chosen = head_lanes(head, TILE)
            own = jnp.where(chosen, query[0, rows, :], jnp.zeros((), HALF))
            ends, middle = folded(upper, nt(own, keys[window, :]))
            ends = ends + bias[tile, :, :TILE]
            middle = middle + bias[tile, :, TILE:]
            highest = jnp.maximum(
                jnp.max(ends, axis=-1, keepdims=True), jnp.max(middle, axis=-1, keepdims=True)
            )
            ends = jnp.exp(ends - highest)
            middle = jnp.exp(middle - highest)
            summed = jnp.sum(ends, axis=-1, keepdims=True) + jnp.sum(middle, axis=-1, keepdims=True)
            out = nn(unfolded(upper, ends, middle), values[window, :]) / summed
            results.append(out)
            totals.append(jnp.broadcast_to(highest + jnp.log(summed), (TILE, PAIR)))
        chosen = head_lanes(0, TILE)
        mixed[rows, :] = jnp.where(chosen, results[0], results[1]).astype(HALF)
        logs[rows, :] = jnp.where(chosen, totals[0], totals[1])
    product = nt(mixed[...], w_out[0])

    @pl.when(step == 0)
    def _():
        total[...] = product

    @pl.when(step > 0)
    def _():
        total[...] += product

    @pl.when(step == pl.num_programs(0) - 1)
    def _():
        attended[...] = total[...].astype(HALF)


def residual_of(x_ref, own, other):
    return x_ref[0].astype(WIDE) + (own[...].astype(WIDE) + other[...].astype(WIDE))


def route_kernel(x_ref, own, other, rows_ref, routes, prev, routed_ref, targets_ref, scores_ref):
    residual = residual_of(x_ref, own, other)
    unit = residual * spread_of(residual)
    routed = (unit * rows_ref[15:16, :].astype(WIDE)).astype(HALF)
    routed_ref[...] = routed
    scores = nt(routed, rows_ref[...])
    scores_ref[...] = scores
    logits = scores[:, :ALL] + prev[0]
    target = lax.broadcasted_iota(jnp.int32, logits.shape, 1)
    first = routes[0, :, 0:1] == target
    second = routes[0, :, 1:2] == target
    zero = jnp.sum(jnp.where(first, logits, 0.0), axis=-1, keepdims=True)
    one = jnp.sum(jnp.where(second, logits, 0.0), axis=-1, keepdims=True)
    highest = jnp.maximum(zero, one)
    zero, one = jnp.exp(zero - highest), jnp.exp(one - highest)
    summed = zero + one
    targets_ref[...] = jnp.where(first, zero / summed, 0.0) + jnp.where(second, one / summed, 0.0)


def expert_kernel(
    expert, order, routed_a, routed_b, upstream, targets_a, targets_b, ranks, weights, theirs, mine, out_slots,
    grad_slots, rows, rows_t, cots, cots_t, out_total, grad_total
):
    step = pl.program_id(0)
    count = routed_a.shape[0]

    @pl.when(step == 0)
    def _():
        slot = lax.broadcasted_iota(jnp.int32, (MOST, count), 0).astype(WIDE)
        for seq, (routed, targets) in enumerate(((routed_a, targets_a), (routed_b, targets_b))):
            place = slice(seq * MOST, (seq + 1) * MOST)
            spread = jnp.where(slot == ranks[seq, expert : expert + 1, :], 1.0, 0.0).astype(HALF)
            rows[place, :] = nn(spread, routed[...]).astype(HALF)
            weighted = targets[:, expert : expert + 1] * upstream[seq].astype(WIDE)
            cots[place, :] = nn(spread, weighted.astype(HALF)).astype(HALF)
        rows_t[...] = rows[...].T
        cots_t[...] = cots[...].T

    here = [weights[0, :, 0, kind].reshape(D, weights.shape[-1]) for kind in range(3)]
    gate = nn(rows[...], here[0])
    up = nn(rows[...], here[1])
    sigmoid = 1.0 / (1.0 + jnp.exp(-gate))
    silu = gate * sigmoid
    activated = (silu * up).astype(HALF)
    activated_grad = nn(cots[...], here[2])
    up_grad = (activated_grad * silu).astype(HALF)
    gate_grad = (activated_grad * up * sigmoid * (1.0 + gate * (1.0 - sigmoid))).astype(HALF)
    out_part = nt(activated, here[2])
    grad_part = nt(gate_grad, here[0]) + nt(up_grad, here[1])

    @pl.when(step == 0)
    def _():
        out_total[...] = out_part
        grad_total[...] = grad_part

    @pl.when(step > 0)
    def _():
        out_total[...] += out_part
        grad_total[...] += grad_part

    grads = (nn(rows_t[...], gate_grad), nn(rows_t[...], up_grad), nn(cots_t[...], activated))

    @pl.when(step < 2)
    def _():
        for kind in range(3):
            theirs[0, kind] = grads[kind].astype(HALF)

    @pl.when(step >= 2)
    def _():
        for kind in range(3):
            mine[0, kind] = grads[kind].astype(HALF)

    @pl.when(step == pl.num_programs(0) - 1)
    def _():
        out_slots[...] = out_total[...].astype(HALF)
        grad_slots[...] = grad_total[...].astype(HALF)


def combine_kernel(*refs):
    outs, grads = refs[:EXPERTS], refs[EXPERTS : 2 * EXPERTS]
    ranks, targets, upstream, back_ref, sum_ref = refs[2 * EXPERTS :]
    count = upstream.shape[1]
    slot = lax.broadcasted_iota(jnp.int32, (count, MOST), 1).astype(WIDE)
    wide = upstream[0].astype(WIDE)
    back = total = None
    lane = lax.broadcasted_iota(jnp.int32, (count, PAIR), 1)
    dots = jnp.zeros((count, PAIR), WIDE)
    for expert in range(EXPERTS):
        spread = jnp.where(slot == ranks[0, :, expert : expert + 1], 1.0, 0.0).astype(HALF)
        part = nn(spread, grads[expert][...])
        back = part if back is None else back + part
        part = nn(spread, outs[expert][...])
        dots = dots + jnp.where(lane == expert, jnp.sum(part * wide, axis=-1, keepdims=True), 0.0)
        part = part * targets[:, expert : expert + 1]
        total = part if total is None else total + part
    back_ref[:, :D] = back.astype(HALF)
    main = dots.astype(HALF)
    rest = pltpu.roll(dots - main.astype(WIDE), ALL, 1)
    back_ref[:, D:] = jnp.where(lane < ALL, main.astype(WIDE), rest).astype(HALF)
    sum_ref[...] = total.astype(HALF)


def turn_kernel(
    x_ref, own, other, upstream, back_own, back_other, targets, scores, rows_ref, w_out, residual_grad_ref, cot_ref,
    mixed_grad_ref, small_ref, base_ref, tall_ref
):
    residual = residual_of(x_ref, own, other)
    spread = spread_of(residual)
    unit = residual * spread
    gain = rows_ref[15:16, :].astype(WIDE)
    routed = (unit * gain).astype(HALF)
    routed_wide = routed.astype(WIDE)
    up_half = upstream[0]
    up = up_half.astype(WIDE)
    vector = [rows_ref[12 + place : 13 + place, :].astype(WIDE) for place in range(2)]
    chosen = targets[...]
    mixing = scores[:, ALL : ALL + 4]

    def softmax_two(a, b):
        highest = jnp.maximum(a, b)
        a, b = jnp.exp(a - highest), jnp.exp(b - highest)
        return a / (a + b), b / (a + b)

    first = softmax_two(mixing[:, 0:1], mixing[:, 1:2])
    second = softmax_two(mixing[:, 2:3], mixing[:, 3:4])
    weight = [chosen[:, place : place + 1] for place in range(ALL)]
    base_ref[...] = (
        residual
        + routed_wide * (weight[5] + weight[6] * first[0] + weight[7] * second[0])
        + (weight[6] * first[1]) * vector[0]
        + (weight[7] * second[1]) * vector[1]
    )
    dot_routed = jnp.sum(up * routed_wide, axis=-1, keepdims=True)
    dot_small = nt(up_half, rows_ref[...])
    dot_vector = (dot_small[:, 12:13], dot_small[:, 13:14])
    halves = back_own[:, D:].astype(WIDE) + back_other[:, D:].astype(WIDE)
    halves = halves[:, :ALL] + halves[:, ALL : 2 * ALL]
    lane = lax.broadcasted_iota(jnp.int32, halves.shape, 1)
    dots = (
        jnp.where(lane < EXPERTS, halves, 0.0)
        + jnp.where(lane == EXPERTS + 1, dot_routed, 0.0)
        + jnp.where(lane == EXPERTS + 2, first[0] * dot_routed + first[1] * dot_vector[0], 0.0)
        + jnp.where(lane == EXPERTS + 3, second[0] * dot_routed + second[1] * dot_vector[1], 0.0)
    )
    logit_grad = chosen * (dots - jnp.sum(chosen * dots, axis=-1, keepdims=True))

    def mix_back(mix, scale, other_dot):
        one, two = scale * dot_routed, scale * other_dot
        inner = mix[0] * one + mix[1] * two
        return mix[0] * (one - inner), mix[1] * (two - inner)

    const_first = mix_back(first, weight[6], dot_vector[0])
    const_second = mix_back(second, weight[7], dot_vector[1])
    lane = lax.broadcasted_iota(jnp.int32, (up.shape[0], SMALL), 1)
    tall = jnp.concatenate([logit_grad, jnp.zeros_like(logit_grad)], axis=1)
    for place, column in enumerate(const_first + const_second):
        tall = tall + jnp.where(lane == ALL + place, column, 0.0)
    tall = tall.astype(HALF)
    tall_ref[...] = jnp.concatenate(
        [tall, jnp.zeros((up.shape[0], PAIR - SMALL), HALF)], axis=1
    )
    back = back_own[:, :D].astype(WIDE) + back_other[:, :D].astype(WIDE)
    routed_grad = (
        back + nn(tall, rows_ref[...]) + up * (weight[5] + first[0] * weight[6] + second[0] * weight[7])
    )
    zero = jnp.zeros((1, D), WIDE)
    small_ref[...] = jnp.concatenate(
        [
            jnp.sum((first[1] * weight[6]) * up, axis=0, keepdims=True),
            jnp.sum((second[1] * weight[7]) * up, axis=0, keepdims=True),
            zero,
            jnp.sum(routed_grad * unit, axis=0, keepdims=True),
            zero,
            zero,
            zero,
            zero,
        ],
        axis=0,
    )
    scaled = routed_grad * gain
    residual_grad = up + spread * (scaled - unit * jnp.mean(scaled * unit, axis=-1, keepdims=True))
    residual_grad_ref[...] = residual_grad
    cot = residual_grad.astype(HALF)
    cot_ref[...] = cot
    mixed_grad_ref[...] = nn(cot, w_out[0]).astype(HALF)


def attend_back_kernel(
    query, k2, k1, k0, v2, v1, v0, query_ids, key_ids, mixed_grad, logs, cos_ref, sin_ref, query_grad, grad2, grad1,
    grad0, bias, keys, values, key_total, value_total
):
    step = pl.program_id(0)

    @pl.when(step == 0)
    def _():
        fill_bias(query_ids, key_ids, bias)

    load_window((k2, k1, k0), keys)
    load_window((v2, v1, v0), values)
    upper = upper_of()
    span = 5 * TILE
    count = query.shape[1]

    def turned_back(gradient, place, rows):
        cosine, sine = cos_ref[place, rows, :], sin_ref[place, rows, :]
        return (gradient * cosine - partner(gradient) * sine).astype(HALF)

    key_total[...] = jnp.zeros_like(key_total)
    value_total[...] = jnp.zeros_like(value_total)
    for tile in range(2):
        rows = slice(tile * TILE, (tile + 1) * TILE)
        window = slice(tile * TILE, tile * TILE + span)
        results = []
        for head in range(2):
            chosen = head_lanes(head, TILE)
            nothing = jnp.zeros((), HALF)
            own = jnp.where(chosen, query[0, rows, :], nothing)
            out_grad = jnp.where(chosen, mixed_grad[rows, :], nothing)
            level = logs[rows, head * HD : head * HD + 1]
            ends, middle = folded(upper, nt(own, keys[window, :]))
            ends = jnp.exp(ends + bias[tile, :, :TILE] - level)
            middle = jnp.exp(middle + bias[tile, :, TILE:] - level)
            value_total[:, window] += nn(out_grad.T, unfolded(upper, ends, middle))
            ends_grad, middle_grad = folded(upper, nt(out_grad, values[window, :]))
            expected = jnp.sum(ends * ends_grad, axis=-1, keepdims=True) + jnp.sum(
                middle * middle_grad, axis=-1, keepdims=True
            )
            score_grad = unfolded(upper, ends * (ends_grad - expected), middle * (middle_grad - expected))
            key_total[:, window] += nn(own.T, score_grad)
            results.append(nn(score_grad, keys[window, :]))
        gradient = jnp.where(head_lanes(0, TILE), results[0], results[1]) * HD ** (-0.5)
        query_grad[rows, :] = turned_back(gradient, 2, rows)
    for place, grad in enumerate((grad2, grad1, grad0)):
        window = slice(place * count, (place + 1) * count)
        grad[0] = turned_back(key_total[:, window].T, place, slice(0, count))
        grad[1] = value_total[:, window].T.astype(HALF)


def weight_kernel(seqs, *refs):
    each = 3 + 1 + 3 + 3 + 1
    groups = [refs[seq * each : (seq + 1) * each] for seq in range(seqs)]
    weights, rows_ref, grads_ref, small_ref = refs[seqs * each :]

    def tn(a, b):
        return lax.dot_general(a, b, (((0,), (0,)), ((), ())), preferred_element_type=WIDE)

    query = key = value = out = small = extra = None

    def plus(a, b):
        return b if a is None else a + b

    for group in groups:
        normed = group[0:3]
        query_grad = group[3]
        pair_grads = group[4:7]
        cot, mixed, tall = group[7:10]
        extra = plus(extra, group[10][...])
        for place in range(3):
            flipped = normed[place][0].T
            key = plus(key, nn(flipped, pair_grads[place][0]))
            value = plus(value, nn(flipped, pair_grads[place][1]))
            if place == 2:
                query = plus(query, nn(flipped, query_grad[...]))
        out = plus(out, nn(cot[...].T, mixed[...]))
    norm = None
    for place, grad in enumerate((query, key, value)):
        grads_ref[place] = grad.astype(HALF)
        norm = plus(norm, jnp.sum(grad * weights[place].astype(WIDE), axis=-1, keepdims=True))
    grads_ref[3] = out.astype(HALF)
    gain = rows_ref[14:15, :].astype(WIDE)
    norm_row = jnp.broadcast_to(norm, (D, PAIR)).T[0:1, :] / gain
    lower = jnp.concatenate([extra[0:2], norm_row, extra[3:4]], axis=0)
    small_ref[0:8, :] = jnp.zeros((8, D), WIDE)
    small_ref[8:16, :] = jnp.concatenate([jnp.zeros((4, D), WIDE), lower], axis=0)


def input_kernel(query_grad, grad0, near, far, flag, weights, out_ref):
    keep = flag[0] == 0
    totals = []
    for kind in range(2):
        total = grad0[kind].astype(WIDE) + far[kind].astype(WIDE)
        total = total + jnp.where(keep, near[kind].astype(WIDE), 0.0)
        totals.append(total.astype(HALF))
    out_ref[...] = (
        nt(query_grad[...], weights[0]) + nt(totals[0], weights[1]) + nt(totals[1], weights[2])
    ).astype(HALF)


def final_kernel(seqs, *refs):
    x_ref, rows_ref = refs[:2]
    groups = [refs[2 + seq * 6 : 8 + seq * 6] for seq in range(seqs)]
    layer_ref, input_ref = refs[2 + seqs * 6 :]
    step = pl.program_id(0)
    for seq, (base, sum_own, sum_other, residual_grad, own, other) in enumerate(groups):

        @pl.when(step == seq)
        def _():
            summed = sum_own[...].astype(WIDE) + sum_other[...].astype(WIDE)
            layer_ref[0] = (base[...] + summed).astype(HALF)
            tensor = x_ref[0].astype(WIDE)
            spread = spread_of(tensor)
            unit = tensor * spread
            gradient = own[...].astype(WIDE) + other[...].astype(WIDE)
            scaled = gradient * rows_ref[14:15, :].astype(WIDE)
            input_ref[0] = residual_grad[...] + spread * (
                scaled - unit * jnp.mean(scaled * unit, axis=-1, keepdims=True)
            )


def place_kernel(order, own, near, far, *refs):
    outs = refs[-3:]
    step = pl.program_id(0)
    for place, block in enumerate((own, far, near, far)):

        @pl.when(step == place)
        def _():
            for kind in range(3):
                outs[kind][0] = block[0, kind].astype(WIDE)


def swap(block, axis):
    size = lax.axis_size(axis)
    return lax.ppermute(block, axis, [(i, i ^ 1) for i in range(size)])


def shift(block, axis, distance):
    size = lax.axis_size(axis)
    route = [(i, i + distance) for i in range(size) if 0 <= i + distance < size]
    return lax.ppermute(block, axis, route)


def pick(stack, index, axis=0):
    return lax.dynamic_index_in_dim(stack, index, axis, keepdims=False)


def scatter_rows(tensor, dimension):
    return lax.psum_scatter(tensor, "fsdp", scatter_dimension=dimension, tiled=True)


def sum_small(small):
    turned = swap(small, "tp")
    row = lax.broadcasted_iota(jnp.int32, small.shape, 0)
    small = small + jnp.where(row == 14, turned, 0.0)
    small = small + swap(small, "lo")
    hi_size = lax.axis_size("hi")
    small = small + swap(small, "hi") if hi_size == 2 else lax.psum(small, "hi")
    size = lax.axis_size("fsdp")
    if size > 4:
        return scatter_rows(small, 1)
    index = lax.axis_index("fsdp")
    blocks = small.reshape(SMALL, size, D // size).transpose(1, 0, 2)
    total = pick(blocks, index)
    for distance in range(1, size):
        sent = pick(blocks, lax.rem(index + distance, size))
        route = [(i, (i + distance) % size) for i in range(size)]
        total = total + lax.ppermute(sent, "fsdp", route)
    return total


def shards(
    block_in,
    cotangent,
    prev_logits,
    routes,
    segments,
    w_query,
    w_key,
    w_value,
    w_out,
    w_gate,
    w_up,
    w_down,
    router,
    const_proj,
    const_vec,
    norm_attn,
    norm_moe,
):
    seqs, count = block_in.shape[:2]
    width = w_query.shape[1]
    pairs = width // PAIR
    deep = w_gate.shape[1]
    hidden = w_gate.shape[2]
    hi, lo = lax.axis_index("hi"), lax.axis_index("lo")
    hi_size = lax.axis_size("hi")
    ctx = hi * 2 + lo
    ctx_size = hi_size * 2
    fsdp_size = lax.axis_size("fsdp")
    part = hidden // ctx_size
    order = jnp.stack([(1 - hi) * 2 + 1 - lo, hi * 2 + 1 - lo, (1 - hi) * 2 + lo, ctx]).astype(
        jnp.int32
    )

    small_rows = jnp.concatenate(
        [
            router.T,
            const_proj.T,
            const_vec.T,
            norm_attn[None, :],
            norm_moe[None, :],
        ],
        axis=0,
    ).astype(HALF)
    small_rows = lax.all_gather(small_rows, "fsdp", axis=1, tiled=True)
    attention_own = jnp.where(
        ctx == 0, w_query, jnp.where(ctx == 1, w_key, jnp.where(ctx == 2, w_value, w_out))
    ).astype(HALF)
    axes = CTX + ("fsdp",)
    attention_weights = lax.all_gather(attention_own, axes, axis=0).reshape(4, D, width)
    expert_own = jnp.stack(
        [
            lax.dynamic_slice_in_dim(w, ctx * part, part, axis=2).astype(HALF)
            for w in (w_gate, w_up, w_down)
        ],
        axis=1,
    )
    expert_own, attention_weights = lax.optimization_barrier((expert_own, attention_weights))
    expert_weights = lax.all_gather(expert_own, axes, axis=0).reshape(
        ctx_size, fsdp_size, EXPERTS, 3, deep, part
    )
    if deep % 16:
        expert_weights = expert_weights.transpose(0, 2, 3, 1, 4, 5).reshape(
            ctx_size, 1, EXPERTS, 3, D, part
        )

    far_rows = shift(block_in, "hi", 1)
    near_rows = swap(jnp.where(lo == 1, far_rows, block_in), "lo")
    far_ids = shift(segments, "hi", 1)
    near_ids = swap(jnp.where(lo == 1, far_ids, segments), "lo")
    far_ids = jnp.where(hi == 0, -1, far_ids)
    near_ids = jnp.where(ctx == 0, -1, near_ids)
    key_ids = jnp.concatenate([far_ids, near_ids, segments], axis=1)[:, None, :]
    query_ids = segments[:, :, None]
    positions = (ctx - 2) * count + jnp.arange(3 * count, dtype=jnp.int32)
    lane = jnp.arange(PAIR, dtype=jnp.int32)
    frequency = 10000.0 ** (-2.0 * (lane % (HD // 2)).astype(WIDE) / HD)
    turned = positions.astype(WIDE)[:, None] * frequency[None, :]
    cosine = jnp.cos(turned).reshape(3, count, PAIR)
    sine = (jnp.sin(turned) * jnp.where((lane & (HD // 2)) == 0, -1.0, 1.0)).reshape(3, count, PAIR)

    rank_rows, rank_columns = call(
        rank_kernel,
        (seqs,),
        [
            pl.BlockSpec((1, 2, count), lambda s: (s, 0, 0)),
            pl.BlockSpec((1, count, 2), lambda s: (s, 0, 0)),
        ],
        [
            (pl.BlockSpec((1, ALL, count), lambda s: (s, 0, 0)), struct((seqs, ALL, count), WIDE)),
            (pl.BlockSpec((1, count, ALL), lambda s: (s, 0, 0)), struct((seqs, count, ALL), WIDE)),
        ],
        flops=4e7,
        moved=1e6,
    )(routes.transpose(0, 2, 1), routes)

    def project(rows, place, with_query):
        spread = struct((seqs, count, width), HALF)
        by_seq = pl.BlockSpec((1, count, width), lambda s: (s, 0, 0))
        by_row = pl.BlockSpec((1, count, D), lambda s: (s, 0, 0))
        kinds = 3 if with_query else 2
        return call(
            functools.partial(project_kernel, with_query),
            (seqs,),
            [
                by_row,
                whole((SMALL, D)),
                fixed((1, count, PAIR), (place, 0, 0)),
                fixed((1, count, PAIR), (place, 0, 0)),
                whole((4, D, width)),
            ],
            [(by_row, struct((seqs, count, D), HALF))] + [(by_seq, spread)] * kinds,
            flops=2 * seqs * count * D * width * kinds,
            moved=4 * D * width * 2 + seqs * count * (4 * D + 2 * width * kinds),
        )(rows, small_rows, cosine, sine, attention_weights)

    normed0, key0, value0, query = project(block_in, 2, True)
    normed1, key1, value1 = project(near_rows, 1, False)
    normed2, key2, value2 = project(far_rows, 0, False)

    def pair_block(seq):
        return pl.BlockSpec((1, count, PAIR), lambda p, seq=seq: (seq, 0, p))

    flat_pair = pl.BlockSpec((count, PAIR), lambda p: (0, p))
    window_scratch = [
        pltpu.VMEM((2, TILE, 4 * TILE), WIDE),
        pltpu.VMEM((3 * count, PAIR), HALF),
        pltpu.VMEM((3 * count, PAIR), HALF),
    ]
    product = 2 * 2 * TILE * 5 * TILE * 256 * 2 * pairs

    def attend(seq):
        return call(
            attend_kernel,
            (pairs,),
            [pair_block(seq)] * 7
            + [
                fixed((1, count, 1), (seq, 0, 0)),
                fixed((1, 1, 3 * count), (seq, 0, 0)),
                pl.BlockSpec((1, D, PAIR), lambda p: (3, 0, p)),
            ],
            [
                (flat_pair, struct((count, width), HALF)),
                (flat_pair, struct((count, width), WIDE)),
                (whole((count, D)), struct((count, D), HALF)),
            ],
            window_scratch + [pltpu.VMEM((count, D), WIDE)],
            flops=4 * product,
            moved=1e7,
        )(query, key2, key1, key0, value2, value1, value0, query_ids, key_ids, attention_weights)

    mixed, logs, attended, attended_other = [], [], [], []
    for seq in range(seqs):
        one, two, three = attend(seq)
        mixed.append(one)
        logs.append(two)
        attended.append(three)
        attended_other.append(swap(three, "tp"))

    flat = whole((count, D))
    flat_small = whole((count, ALL))

    def one_seq(seq, columns):
        return fixed((1, count, columns), (seq, 0, 0))

    routed, targets, scores = [], [], []
    for seq in range(seqs):
        one, two, three = call(
            route_kernel,
            (1,),
            [one_seq(seq, D), flat, flat, whole((SMALL, D)), one_seq(seq, 2), one_seq(seq, ALL)],
            [
                (flat, struct((count, D), HALF)),
                (flat_small, struct((count, ALL), WIDE)),
                (whole((count, SMALL)), struct((count, SMALL), WIDE)),
            ],
            flops=2 * count * D * 256,
            moved=count * D * 8,
        )(block_in, attended[seq], attended_other[seq], small_rows, routes, prev_logits)
        routed.append(one)
        targets.append(two)
        scores.append(three)

    slots = seqs * MOST
    weight_block = (1,) + expert_weights.shape[1:2] + (1, 3) + expert_weights.shape[4:]
    out_slots, grad_slots, scattered = [], [], []
    for expert in range(EXPERTS):
        piece = (1, 3, D, part)
        theirs, mine, one, two = call(
            functools.partial(expert_kernel, expert),
            (ctx_size,),
            [
                flat,
                flat,
                whole((seqs, count, D)),
                flat_small,
                flat_small,
                whole((seqs, ALL, count)),
                pl.BlockSpec(
                    weight_block, lambda j, o, expert=expert: (o[j], 0, expert, 0, 0, 0)
                ),
            ],
            [
                (
                    pl.BlockSpec(piece, lambda j, o: (jnp.minimum(j, 1), 0, 0, 0)),
                    struct((2, 3, D, part), HALF),
                ),
                (
                    pl.BlockSpec(piece, lambda j, o: (jnp.maximum(j - 2, 0), 0, 0, 0)),
                    struct((2, 3, D, part), HALF),
                ),
                (whole((slots, D)), struct((slots, D), HALF)),
                (whole((slots, D)), struct((slots, D), HALF)),
            ],
            [
                pltpu.VMEM((slots, D), HALF),
                pltpu.VMEM((D, slots), HALF),
                pltpu.VMEM((slots, D), HALF),
                pltpu.VMEM((D, slots), HALF),
                pltpu.VMEM((slots, D), WIDE),
                pltpu.VMEM((slots, D), WIDE),
            ],
            flops=2 * 9 * slots * D * hidden,
            moved=12 * D * hidden + 8 * slots * D,
            prefetch=1,
        )(order, routed[0], routed[1], cotangent, targets[0], targets[1], rank_rows, expert_weights)
        out_slots.append(one)
        grad_slots.append(two)
        received = swap(theirs, "lo")
        crossing = swap(mine[0] + received[0], "hi")
        own = mine[1] + received[1] + crossing
        scattered.append(scatter_rows(own, 1))

    back, back_other, sums, sums_other = [], [], [], []
    for seq in range(seqs):
        slot_block = fixed((MOST, D), (seq, 0))
        one, two = call(
            combine_kernel,
            (1,),
            [slot_block] * (2 * EXPERTS) + [one_seq(seq, ALL), flat_small, one_seq(seq, D)],
            [
                (whole((count, D + PAIR)), struct((count, D + PAIR), HALF)),
                (flat, struct((count, D), HALF)),
            ],
            flops=4 * count * EXPERTS * MOST * D,
            moved=4 * slots * D + 6 * count * D,
        )(*out_slots, *grad_slots, rank_columns, targets[seq], cotangent)
        back.append(one)
        sums.append(two)
        back_other.append(swap(one, "tp"))
    for seq in range(seqs):
        sums_other.append(swap(sums[seq], "tp"))

    residual_grads, cots, mixed_grads, extras, bases, talls = [], [], [], [], [], []
    for seq in range(seqs):
        results = call(
            turn_kernel,
            (1,),
            [
                one_seq(seq, D),
                flat,
                flat,
                one_seq(seq, D),
                whole((count, D + PAIR)),
                whole((count, D + PAIR)),
                flat_small,
                whole((count, SMALL)),
                whole((SMALL, D)),
                fixed((1, D, width), (3, 0, 0)),
            ],
            [
                (flat, struct((count, D), WIDE)),
                (flat, struct((count, D), HALF)),
                (whole((count, width)), struct((count, width), HALF)),
                (whole((8, D)), struct((8, D), WIDE)),
                (flat, struct((count, D), WIDE)),
                (whole((count, PAIR)), struct((count, PAIR), HALF)),
            ],
            flops=2 * count * D * width,
            moved=count * D * 22,
        )(
            block_in,
            attended[seq],
            attended_other[seq],
            cotangent,
            back[seq],
            back_other[seq],
            targets[seq],
            scores[seq],
            small_rows,
            attention_weights,
        )
        for held, result in zip(
            (residual_grads, cots, mixed_grads, extras, bases, talls), results, strict=True
        ):
            held.append(result)

    query_grads, grads2, grads1, grads0 = [], [], [], []
    pair_out = (
        pl.BlockSpec((2, count, PAIR), lambda p: (0, 0, p)),
        struct((2, count, width), HALF),
    )
    table = whole((3, count, PAIR))
    near_grads, far_grads = [], []
    for seq in range(seqs):
        results = call(
            attend_back_kernel,
            (pairs,),
            [pair_block(seq)] * 7
            + [
                fixed((1, count, 1), (seq, 0, 0)),
                fixed((1, 1, 3 * count), (seq, 0, 0)),
                flat_pair,
                flat_pair,
                table,
                table,
            ],
            [(flat_pair, struct((count, width), HALF))] + [pair_out] * 3,
            window_scratch
            + [pltpu.VMEM((PAIR, 3 * count), WIDE), pltpu.VMEM((PAIR, 3 * count), WIDE)],
            flops=10 * product,
            moved=1e7,
        )(
            query,
            key2,
            key1,
            key0,
            value2,
            value1,
            value0,
            query_ids,
            key_ids,
            mixed_grads[seq],
            logs[seq],
            cosine,
            sine,
        )
        for held, result in zip((query_grads, grads2, grads1, grads0), results, strict=True):
            held.append(result)
        near = swap(results[2], "lo")
        sent = results[1] + jnp.where(lo == 1, near, jnp.zeros((), HALF))
        near_grads.append(near)
        far_grads.append(shift(sent, "hi", -1))

    operands, specs = [], []
    for seq in range(seqs):
        operands += [normed2, normed1, normed0, query_grads[seq], grads2[seq], grads1[seq], grads0[seq]]
        operands += [cots[seq], mixed[seq], talls[seq], extras[seq]]
        specs += [one_seq(seq, D)] * 3 + [whole((count, width))] + [whole((2, count, width))] * 3
        specs += [flat, whole((count, width)), whole((count, PAIR)), whole((8, D))]
    attention_grads, small = call(
        functools.partial(weight_kernel, seqs),
        (1,),
        specs + [whole((4, D, width)), whole((SMALL, D))],
        [
            (whole((4, D, width)), struct((4, D, width), HALF)),
            (whole((SMALL, D)), struct((SMALL, D), WIDE)),
        ],
        flops=2 * 8 * seqs * count * D * width,
        moved=2 * (4 * D * width * 2 + seqs * count * (4 * D + 8 * width)),
    )(*operands, attention_weights, small_rows)
    tall_rows = sum(
        lax.dot_general(
            talls[seq][:, :SMALL], routed[seq], (((0,), (0,)), ((), ())), preferred_element_type=WIDE
        )
        for seq in range(seqs)
    )
    small = sum_small(small + tall_rows)

    input_parts, input_others = [], []
    flag = lo.reshape(1).astype(jnp.int32)
    for seq in range(seqs):
        one = call(
            input_kernel,
            (1,),
            [
                whole((count, width)),
                whole((2, count, width)),
                whole((2, count, width)),
                whole((2, count, width)),
                pl.BlockSpec(memory_space=pltpu.SMEM),
                whole((4, D, width)),
            ],
            [(flat, struct((count, D), HALF))],
            flops=6 * count * D * width,
            moved=8 * D * width + count * (14 * width + 2 * D),
        )(query_grads[seq], grads0[seq], near_grads[seq], far_grads[seq], flag, attention_weights)[0]
        input_parts.append(one)
        input_others.append(swap(one, "tp"))

    operands, specs = [block_in, small_rows], [
        pl.BlockSpec((1, count, D), lambda s: (s, 0, 0)),
        whole((SMALL, D)),
    ]
    for seq in range(seqs):
        operands += [bases[seq], sums[seq], sums_other[seq], residual_grads[seq]]
        operands += [input_parts[seq], input_others[seq]]
        specs += [flat] * 6
    by_row = pl.BlockSpec((1, count, D), lambda s: (s, 0, 0))
    layer_out, grad_input = call(
        functools.partial(final_kernel, seqs),
        (seqs,),
        specs,
        [
            (by_row, struct((seqs, count, D), HALF)),
            (by_row, struct((seqs, count, D), WIDE)),
        ],
        flops=20 * seqs * count * D,
        moved=seqs * count * D * 24,
    )(*operands)

    paired = attention_grads.reshape(2, 2, D, width)
    received = swap(pick(paired, 1 - lo, 1), "lo")
    kept = pick(paired, lo, 1)
    crossing = swap(pick(kept, 1 - hi) + pick(received, 1 - hi), "hi")
    own = scatter_rows(pick(kept, hi) + pick(received, hi) + crossing, 0)
    near = swap(own, "lo")
    couple = jnp.stack([jnp.where(lo == 0, own, near), jnp.where(lo == 0, near, own)])
    across = swap(couple, "hi")
    wide_couple, wide_across = couple.astype(WIDE), across.astype(WIDE)
    lower = jnp.where(hi == 0, wide_couple, wide_across)
    higher = jnp.where(hi == 0, wide_across, wide_couple)

    grads = None
    for expert in range(EXPERTS):
        own = scattered[expert]
        near = swap(own, "lo")
        far = swap(jnp.stack([near, own]), "hi")
        block = (1, 3, deep, part)
        result = struct((EXPERTS, deep, hidden), WIDE)
        out_spec = pl.BlockSpec(
            (1, deep, part), lambda j, o, expert=expert: (expert, 0, o[3 - j])
        )
        previous = [] if grads is None else list(grads)
        grads = call(
            place_kernel,
            (ctx_size,),
            [
                whole(block),
                whole(block),
                pl.BlockSpec(block, lambda j, o: (jnp.where(j <= 2, 1, 0), 0, 0, 0)),
            ]
            + [pl.BlockSpec(memory_space=pl.ANY)] * len(previous),
            [(out_spec, result)] * 3,
            moved=3 * deep * hidden * 6,
            prefetch=1,
            aliases={4 + kind: kind for kind in range(3)} if previous else None,
        )(order, own[None], near[None], far, *previous)

    return (
        layer_out,
        grad_input,
        lower[0],
        lower[1],
        higher[0],
        higher[1],
        *grads,
        small[0:8].T,
        small[8:12].T,
        small[12:14].T,
        small[14],
        small[15],
    )


def solution(mesh):
    sizes = mesh.shape
    inner = Mesh(
        mesh.devices.reshape(sizes["fsdp"], sizes["ctx"] // 2, 2, sizes["tp"]),
        ("fsdp", "hi", "lo", "tp"),
    )
    rows = P("fsdp", CTX, None)
    matrix = P("fsdp", "tp")
    experts = P(None, "fsdp", "tp")
    narrow = P("fsdp", None)
    vector = P("fsdp")
    return jax.shard_map(
        shards,
        mesh=inner,
        in_specs=(rows,) * 4
        + (P("fsdp", CTX),)
        + (matrix,) * 4
        + (experts,) * 3
        + (narrow,) * 3
        + (vector,) * 2,
        out_specs=(rows,) * 2
        + (matrix,) * 4
        + (experts,) * 3
        + (narrow,) * 3
        + (vector,) * 2,
        check_vma=False,
    )
```

```python
import functools

import jax
import jax.numpy as jnp
from jax import lax
from jax.experimental import pallas as pl
from jax.experimental.pallas import tpu as pltpu
from jax.sharding import Mesh
from jax.sharding import PartitionSpec as P

D = 768
HEADS = 12
HD = 64
EXPERTS = 4
ALL = 8
WINDOW = 1024
MOST = 192

EPSILON = 1e-06
MASKED = -1e30

CTX = ("hi", "lo")
HALF = jnp.bfloat16
WIDE = jnp.float32
TILE = 256
PAIR = 2 * HD
SMALL = 16
MIB = 1 << 20


def nn(a, b):
    return jnp.dot(a, b, preferred_element_type=WIDE)


def nt(a, b):
    return lax.dot_general(a, b, (((1,), (1,)), ((), ())), preferred_element_type=WIDE)


def call(
    body,
    grid,
    ins,
    outs,
    scratch=(),
    flops=0,
    moved=0,
    prefetch=0,
    aliases=None,
    after=(),
    side=None,
):
    operands, specs, side_out = side or ((), (), None)
    own = prefetch + len(ins)
    first = own + len(operands) + len(after)

    def inner(*refs):
        results = first + len(outs)
        if side:
            total = refs[own][...].astype(WIDE)
            for ref in refs[own + 1 : own + len(operands)]:
                total = total + ref[...].astype(WIDE)
            refs[results][...] = total.astype(HALF)
        body(*refs[:own], *refs[first:results], *refs[results + (1 if side else 0) :])

    all_outs = list(outs) + ([side_out] if side else [])
    grid_spec = pltpu.PrefetchScalarGridSpec(
        num_scalar_prefetch=prefetch,
        grid=grid,
        in_specs=list(ins) + list(specs) + [pl.BlockSpec(memory_space=pl.ANY)] * len(after),
        out_specs=[spec for spec, _ in all_outs],
        scratch_shapes=list(scratch),
    )
    kernel = pl.pallas_call(
        inner,
        grid_spec=grid_spec,
        out_shape=[shape for _, shape in all_outs],
        input_output_aliases=aliases or {},
        compiler_params=pltpu.CompilerParams(
            dimension_semantics=("arbitrary",) * len(grid), vmem_limit_bytes=63 * MIB
        ),
        cost_estimate=pl.CostEstimate(
            flops=int(flops), bytes_accessed=int(moved), transcendentals=0
        ),
    )
    return lambda *arrays: kernel(*arrays, *operands, *after)


def side_sum(steps, stacks, index=None, plain=()):
    flat = [stack.reshape(-1, stack.shape[-1]) for stack in stacks]
    rows, columns = flat[0].shape
    rows = rows if index is None else rows // stacks[0].shape[0]
    start = 0 if index is None else index * steps
    block = (rows // steps, columns)
    out = pl.BlockSpec(block, lambda step, *_: (step, 0))
    specs = [pl.BlockSpec(block, lambda step, *_: (start + step, 0))] * len(flat)
    flat += [array.reshape(rows, columns) for array in plain]
    specs += [out] * len(plain)
    return flat, specs, (out, struct((rows, columns), HALF))


def whole(shape):
    zeros = (0,) * len(shape)
    return pl.BlockSpec(shape, lambda *_: zeros)


def fixed(block, place):
    return pl.BlockSpec(block, lambda *_: place)


def struct(shape, dtype):
    return jax.ShapeDtypeStruct(shape, dtype)


def spread_of(tensor):
    return lax.rsqrt(jnp.mean(tensor * tensor, axis=-1, keepdims=True) + EPSILON)


def partner(tensor):
    lane = lax.broadcasted_iota(jnp.int32, tensor.shape, 1)
    return jnp.where(
        (lane & (HD // 2)) == 0,
        pltpu.roll(tensor, PAIR - HD // 2, 1),
        pltpu.roll(tensor, HD // 2, 1),
    )


def rank_kernel(routes_t, routes, rank_rows, rank_columns):
    count = routes.shape[1]
    down = lax.broadcasted_iota(jnp.int32, (count, count), 0)
    across = lax.broadcasted_iota(jnp.int32, (count, count), 1)
    before = jnp.where(down < across, 1.0, 0.0).astype(HALF)
    after = jnp.where(across < down, 1.0, 0.0).astype(HALF)
    row_target = lax.broadcasted_iota(jnp.int32, (ALL, count), 0)
    names = (routes_t[0, 0:1, :] == row_target) | (routes_t[0, 1:2, :] == row_target)
    ranks = nn(jnp.where(names, 1.0, 0.0).astype(HALF), before)
    rank_rows[0] = jnp.where(names, ranks, -1.0)
    column_target = lax.broadcasted_iota(jnp.int32, (count, ALL), 1)
    named = (routes[0, :, 0:1] == column_target) | (routes[0, :, 1:2] == column_target)
    ranked = nn(after, jnp.where(named, 1.0, 0.0).astype(HALF))
    rank_columns[0] = jnp.where(named, ranked, -1.0)


def project_kernel(with_query, *refs):
    x_ref, rows_ref, cos_ref, sin_ref, weights = refs[:5]
    outs = refs[5:]
    tensor = x_ref[0].astype(WIDE)
    unit = tensor * spread_of(tensor)
    normed = (unit * rows_ref[14:15, :].astype(WIDE)).astype(HALF)
    outs[0][0] = normed
    cosine, sine = cos_ref[0], sin_ref[0]

    def turned(matrix, out, scale):
        flat = nn(normed, weights[matrix])
        for piece in range(flat.shape[1] // PAIR):
            lanes = slice(piece * PAIR, (piece + 1) * PAIR)
            part = flat[:, lanes]
            result = (part * cosine + partner(part) * sine).astype(HALF)
            out[0, :, lanes] = result if scale is None else result * scale

    turned(1, outs[1], None)
    outs[2][0] = nn(normed, weights[2]).astype(HALF)
    if with_query:
        turned(0, outs[3], jnp.asarray(HD ** (-0.5), HALF))


def fill_bias(query_ids, key_ids, bias):
    upper = upper_of()
    for tile in range(2):
        ids = query_ids[0, tile * TILE : (tile + 1) * TILE, :]
        first = key_ids[0, :, tile * TILE : (tile + 1) * TILE]
        last = key_ids[0, :, (tile + 4) * TILE : (tile + 5) * TILE]
        mixed = jnp.where(upper, first, last)
        bias[tile, :, :TILE] = jnp.where(mixed == ids, 0.0, MASKED)
        inner = key_ids[0, :, (tile + 1) * TILE : (tile + 4) * TILE]
        bias[tile, :, TILE:] = jnp.where(inner == ids, 0.0, MASKED)


def upper_of():
    down = lax.broadcasted_iota(jnp.int32, (TILE, TILE), 0)
    across = lax.broadcasted_iota(jnp.int32, (TILE, TILE), 1)
    return across > down


def head_lanes(head, rows):
    lane = lax.broadcasted_iota(jnp.int32, (rows, PAIR), 1)
    return (lane < HD) if head == 0 else (lane >= HD)


def folded(upper, spread):
    span = spread.shape[1]
    return (
        jnp.where(upper, spread[:, :TILE], spread[:, span - TILE :]),
        spread[:, TILE : span - TILE],
    )


def unfolded(upper, ends, middle):
    return jnp.concatenate(
        [jnp.where(upper, ends, 0.0), middle, jnp.where(upper, 0.0, ends)], axis=1
    ).astype(HALF)


def load_window(parts, window):
    rows = parts[0].shape[1]
    for place, part in enumerate(parts):
        window[place * rows : (place + 1) * rows, :] = part[0]


def attend_kernel(
    query, k2, k1, k0, v2, v1, v0, query_ids, key_ids, w_out, mixed, logs, attended, bias, keys, values, total
):
    step = pl.program_id(0)

    @pl.when(step == 0)
    def _():
        fill_bias(query_ids, key_ids, bias)

    load_window((k2, k1, k0), keys)
    load_window((v2, v1, v0), values)
    upper = upper_of()
    span = 5 * TILE
    for tile in range(2):
        rows = slice(tile * TILE, (tile + 1) * TILE)
        window = slice(tile * TILE, tile * TILE + span)
        results, totals = [], []
        for head in range(2):
            chosen = head_lanes(head, TILE)
            own = jnp.where(chosen, query[0, rows, :], jnp.zeros((), HALF))
            ends, middle = folded(upper, nt(own, keys[window, :]))
            ends = ends + bias[tile, :, :TILE]
            middle = middle + bias[tile, :, TILE:]
            highest = jnp.maximum(
                jnp.max(ends, axis=-1, keepdims=True), jnp.max(middle, axis=-1, keepdims=True)
            )
            ends = jnp.exp(ends - highest)
            middle = jnp.exp(middle - highest)
            summed = jnp.sum(ends, axis=-1, keepdims=True) + jnp.sum(middle, axis=-1, keepdims=True)
            out = nn(unfolded(upper, ends, middle), values[window, :]) / summed
            results.append(out)
            totals.append(jnp.broadcast_to(highest + jnp.log(summed), (TILE, PAIR)))
        chosen = head_lanes(0, TILE)
        mixed[rows, :] = jnp.where(chosen, results[0], results[1]).astype(HALF)
        logs[rows, :] = jnp.where(chosen, totals[0], totals[1])
    product = nt(mixed[...], w_out[0])

    @pl.when(step == 0)
    def _():
        total[...] = product

    @pl.when(step > 0)
    def _():
        total[...] += product

    @pl.when(step == pl.num_programs(0) - 1)
    def _():
        attended[...] = total[...].astype(HALF)


def residual_of(x_ref, own, other):
    return x_ref[0].astype(WIDE) + (own[...].astype(WIDE) + other[...].astype(WIDE))


def route_kernel(x_ref, own, other, rows_ref, routes, prev, routed_ref, targets_ref, scores_ref):
    residual = residual_of(x_ref, own, other)
    unit = residual * spread_of(residual)
    routed = (unit * rows_ref[15:16, :].astype(WIDE)).astype(HALF)
    routed_ref[...] = routed
    scores = nt(routed, rows_ref[...])
    scores_ref[...] = scores
    logits = scores[:, :ALL] + prev[0]
    target = lax.broadcasted_iota(jnp.int32, logits.shape, 1)
    first = routes[0, :, 0:1] == target
    second = routes[0, :, 1:2] == target
    zero = jnp.sum(jnp.where(first, logits, 0.0), axis=-1, keepdims=True)
    one = jnp.sum(jnp.where(second, logits, 0.0), axis=-1, keepdims=True)
    highest = jnp.maximum(zero, one)
    zero, one = jnp.exp(zero - highest), jnp.exp(one - highest)
    summed = zero + one
    targets_ref[...] = jnp.where(first, zero / summed, 0.0) + jnp.where(second, one / summed, 0.0)


def expert_kernel(
    expert, order, routed_a, routed_b, upstream, targets_a, targets_b, ranks, weights, theirs, mine, out_slots,
    grad_slots, rows, rows_t, cots, cots_t, out_total, grad_total
):
    step = pl.program_id(0)
    count = routed_a.shape[0]

    @pl.when(step == 0)
    def _():
        slot = lax.broadcasted_iota(jnp.int32, (MOST, count), 0).astype(WIDE)
        for seq, (routed, targets) in enumerate(((routed_a, targets_a), (routed_b, targets_b))):
            place = slice(seq * MOST, (seq + 1) * MOST)
            spread = jnp.where(slot == ranks[seq, expert : expert + 1, :], 1.0, 0.0).astype(HALF)
            rows[place, :] = nn(spread, routed[...]).astype(HALF)
            weighted = targets[:, expert : expert + 1] * upstream[seq].astype(WIDE)
            cots[place, :] = nn(spread, weighted.astype(HALF)).astype(HALF)
        rows_t[...] = rows[...].T
        cots_t[...] = cots[...].T

    here = [weights[0, :, kind, 0].reshape(D, weights.shape[-1]) for kind in range(3)]
    gate = nn(rows[...], here[0])
    up = nn(rows[...], here[1])
    sigmoid = 1.0 / (1.0 + jnp.exp(-gate))
    silu = gate * sigmoid
    activated = (silu * up).astype(HALF)
    activated_grad = nn(cots[...], here[2])
    up_grad = (activated_grad * silu).astype(HALF)
    gate_grad = (activated_grad * up * sigmoid * (1.0 + gate * (1.0 - sigmoid))).astype(HALF)
    out_part = nt(activated, here[2])
    grad_part = nt(gate_grad, here[0]) + nt(up_grad, here[1])

    @pl.when(step == 0)
    def _():
        out_total[...] = out_part
        grad_total[...] = grad_part

    @pl.when(step > 0)
    def _():
        out_total[...] += out_part
        grad_total[...] += grad_part

    grads = (nn(rows_t[...], gate_grad), nn(rows_t[...], up_grad), nn(cots_t[...], activated))

    @pl.when(step < 2)
    def _():
        for kind in range(3):
            theirs[0, kind] = grads[kind].astype(HALF)

    @pl.when(step >= 2)
    def _():
        for kind in range(3):
            mine[0, kind] = grads[kind].astype(HALF)

    @pl.when(step == pl.num_programs(0) - 1)
    def _():
        out_slots[...] = out_total[...].astype(HALF)
        grad_slots[...] = grad_total[...].astype(HALF)


def combine_kernel(*refs):
    outs, grads = refs[:EXPERTS], refs[EXPERTS : 2 * EXPERTS]
    ranks, targets, upstream, back_ref, sum_ref = refs[2 * EXPERTS :]
    count = upstream.shape[1]
    slot = lax.broadcasted_iota(jnp.int32, (count, MOST), 1).astype(WIDE)
    wide = upstream[0].astype(WIDE)
    back = total = None
    lane = lax.broadcasted_iota(jnp.int32, (count, PAIR), 1)
    dots = jnp.zeros((count, PAIR), WIDE)
    for expert in range(EXPERTS):
        spread = jnp.where(slot == ranks[0, :, expert : expert + 1], 1.0, 0.0).astype(HALF)
        part = nn(spread, grads[expert][...])
        back = part if back is None else back + part
        part = nn(spread, outs[expert][...])
        dots = dots + jnp.where(lane == expert, jnp.sum(part * wide, axis=-1, keepdims=True), 0.0)
        part = part * targets[:, expert : expert + 1]
        total = part if total is None else total + part
    back_ref[:, :D] = back.astype(HALF)
    main = dots.astype(HALF)
    rest = pltpu.roll(dots - main.astype(WIDE), ALL, 1)
    back_ref[:, D:] = jnp.where(lane < ALL, main.astype(WIDE), rest).astype(HALF)
    sum_ref[...] = total.astype(HALF)


def turn_kernel(
    x_ref, own, other, upstream, back_own, back_other, targets, scores, rows_ref, w_out, residual_grad_ref, cot_ref,
    mixed_grad_ref, small_ref, base_ref, tall_ref
):
    residual = residual_of(x_ref, own, other)
    spread = spread_of(residual)
    unit = residual * spread
    gain = rows_ref[15:16, :].astype(WIDE)
    routed = (unit * gain).astype(HALF)
    routed_wide = routed.astype(WIDE)
    up_half = upstream[0]
    up = up_half.astype(WIDE)
    vector = [rows_ref[12 + place : 13 + place, :].astype(WIDE) for place in range(2)]
    chosen = targets[...]
    mixing = scores[:, ALL : ALL + 4]

    def softmax_two(a, b):
        highest = jnp.maximum(a, b)
        a, b = jnp.exp(a - highest), jnp.exp(b - highest)
        return a / (a + b), b / (a + b)

    first = softmax_two(mixing[:, 0:1], mixing[:, 1:2])
    second = softmax_two(mixing[:, 2:3], mixing[:, 3:4])
    weight = [chosen[:, place : place + 1] for place in range(ALL)]
    base_ref[...] = (
        residual
        + routed_wide * (weight[5] + weight[6] * first[0] + weight[7] * second[0])
        + (weight[6] * first[1]) * vector[0]
        + (weight[7] * second[1]) * vector[1]
    )
    dot_routed = jnp.sum(up * routed_wide, axis=-1, keepdims=True)
    dot_small = nt(up_half, rows_ref[...])
    dot_vector = (dot_small[:, 12:13], dot_small[:, 13:14])
    halves = back_own[:, D:].astype(WIDE) + back_other[:, D:].astype(WIDE)
    halves = halves[:, :ALL] + halves[:, ALL : 2 * ALL]
    lane = lax.broadcasted_iota(jnp.int32, halves.shape, 1)
    dots = (
        jnp.where(lane < EXPERTS, halves, 0.0)
        + jnp.where(lane == EXPERTS + 1, dot_routed, 0.0)
        + jnp.where(lane == EXPERTS + 2, first[0] * dot_routed + first[1] * dot_vector[0], 0.0)
        + jnp.where(lane == EXPERTS + 3, second[0] * dot_routed + second[1] * dot_vector[1], 0.0)
    )
    logit_grad = chosen * (dots - jnp.sum(chosen * dots, axis=-1, keepdims=True))

    def mix_back(mix, scale, other_dot):
        one, two = scale * dot_routed, scale * other_dot
        inner = mix[0] * one + mix[1] * two
        return mix[0] * (one - inner), mix[1] * (two - inner)

    const_first = mix_back(first, weight[6], dot_vector[0])
    const_second = mix_back(second, weight[7], dot_vector[1])
    lane = lax.broadcasted_iota(jnp.int32, (up.shape[0], SMALL), 1)
    tall = jnp.concatenate([logit_grad, jnp.zeros_like(logit_grad)], axis=1)
    for place, column in enumerate(const_first + const_second):
        tall = tall + jnp.where(lane == ALL + place, column, 0.0)
    tall = tall.astype(HALF)
    tall_ref[...] = jnp.concatenate(
        [tall, jnp.zeros((up.shape[0], PAIR - SMALL), HALF)], axis=1
    )
    back = back_own[:, :D].astype(WIDE) + back_other[:, :D].astype(WIDE)
    routed_grad = (
        back + nn(tall, rows_ref[...]) + up * (weight[5] + first[0] * weight[6] + second[0] * weight[7])
    )
    zero = jnp.zeros((1, D), WIDE)
    sums = jnp.concatenate(
        [
            jnp.sum((first[1] * weight[6]) * up, axis=0, keepdims=True),
            jnp.sum((second[1] * weight[7]) * up, axis=0, keepdims=True),
            zero,
            jnp.sum(routed_grad * unit, axis=0, keepdims=True),
            zero,
            zero,
            zero,
            zero,
        ],
        axis=0,
    )
    step = pl.program_id(0)

    @pl.when(step == 0)
    def _():
        small_ref[...] = sums

    @pl.when(step > 0)
    def _():
        small_ref[...] += sums

    scaled = routed_grad * gain
    residual_grad = up + spread * (scaled - unit * jnp.mean(scaled * unit, axis=-1, keepdims=True))
    residual_grad_ref[...] = residual_grad
    cot = residual_grad.astype(HALF)
    cot_ref[...] = cot
    mixed_grad_ref[...] = nn(cot, w_out[0]).astype(HALF)


def attend_back_kernel(
    query, k2, k1, k0, v2, v1, v0, query_ids, key_ids, mixed_grad, logs, cos_ref, sin_ref, query_grad, grad2, grad1,
    grad0, bias, keys, values, key_total, value_total
):
    step = pl.program_id(0)

    @pl.when(step == 0)
    def _():
        fill_bias(query_ids, key_ids, bias)

    load_window((k2, k1, k0), keys)
    load_window((v2, v1, v0), values)
    upper = upper_of()
    span = 5 * TILE
    count = query.shape[1]

    def turned_back(gradient, place, rows):
        cosine, sine = cos_ref[place, rows, :], sin_ref[place, rows, :]
        return (gradient * cosine - partner(gradient) * sine).astype(HALF)

    key_total[...] = jnp.zeros_like(key_total)
    value_total[...] = jnp.zeros_like(value_total)
    for tile in range(2):
        rows = slice(tile * TILE, (tile + 1) * TILE)
        window = slice(tile * TILE, tile * TILE + span)
        results = []
        for head in range(2):
            chosen = head_lanes(head, TILE)
            nothing = jnp.zeros((), HALF)
            own = jnp.where(chosen, query[0, rows, :], nothing)
            out_grad = jnp.where(chosen, mixed_grad[rows, :], nothing)
            level = logs[rows, head * HD : head * HD + 1]
            ends, middle = folded(upper, nt(own, keys[window, :]))
            ends = jnp.exp(ends + bias[tile, :, :TILE] - level)
            middle = jnp.exp(middle + bias[tile, :, TILE:] - level)
            value_total[:, window] += nn(out_grad.T, unfolded(upper, ends, middle))
            ends_grad, middle_grad = folded(upper, nt(out_grad, values[window, :]))
            expected = jnp.sum(ends * ends_grad, axis=-1, keepdims=True) + jnp.sum(
                middle * middle_grad, axis=-1, keepdims=True
            )
            score_grad = unfolded(upper, ends * (ends_grad - expected), middle * (middle_grad - expected))
            key_total[:, window] += nn(own.T, score_grad)
            results.append(nn(score_grad, keys[window, :]))
        gradient = jnp.where(head_lanes(0, TILE), results[0], results[1]) * HD ** (-0.5)
        query_grad[rows, :] = turned_back(gradient, 2, rows)
    for place, grad in enumerate((grad2, grad1, grad0)):
        window = slice(place * count, (place + 1) * count)
        grad[0] = turned_back(key_total[:, window].T, place, slice(0, count))
        grad[1] = value_total[:, window].T.astype(HALF)


def weight_kernel(seqs, *refs):
    each = 3 + 1 + 3 + 3 + 1
    groups = [refs[seq * each : (seq + 1) * each] for seq in range(seqs)]
    weights, rows_ref, grads_ref, small_ref = refs[seqs * each :]

    def tn(a, b):
        return lax.dot_general(a, b, (((0,), (0,)), ((), ())), preferred_element_type=WIDE)

    query = key = value = out = small = extra = None

    def plus(a, b):
        return b if a is None else a + b

    for group in groups:
        normed = group[0:3]
        query_grad = group[3]
        pair_grads = group[4:7]
        cot, mixed, tall = group[7:10]
        extra = plus(extra, group[10][...])
        for place in range(3):
            flipped = normed[place][0].T
            key = plus(key, nn(flipped, pair_grads[place][0]))
            value = plus(value, nn(flipped, pair_grads[place][1]))
            if place == 2:
                query = plus(query, nn(flipped, query_grad[...]))
        out = plus(out, nn(cot[...].T, mixed[...]))
    norm = None
    for place, grad in enumerate((query, key, value)):
        grads_ref[place] = grad.astype(HALF)
        norm = plus(norm, jnp.sum(grad * weights[place].astype(WIDE), axis=-1, keepdims=True))
    grads_ref[3] = out.astype(HALF)
    gain = rows_ref[14:15, :].astype(WIDE)
    deep = norm.shape[0]
    norm_row = jnp.broadcast_to(norm, (deep, PAIR)).T[0:1, :] / gain
    lower = jnp.concatenate([extra[0:2], norm_row, extra[3:4]], axis=0)
    small_ref[0:8, :] = jnp.zeros((8, deep), WIDE)
    small_ref[8:16, :] = jnp.concatenate([jnp.zeros((4, deep), WIDE), lower], axis=0)


def relay_kernel(flag, far, near, out):
    out[...] = (
        far[...].astype(WIDE) + jnp.where(flag[0] == 1, near[...].astype(WIDE), 0.0)
    ).astype(HALF)


def input_kernel(query_grad, grad0, near, far, flag, weights, out_ref):
    keep = flag[0] == 0
    totals = []
    for kind in range(2):
        total = grad0[kind].astype(WIDE) + far[kind].astype(WIDE)
        total = total + jnp.where(keep, near[kind].astype(WIDE), 0.0)
        totals.append(total.astype(HALF))
    out_ref[...] = (
        nt(query_grad[...], weights[0]) + nt(totals[0], weights[1]) + nt(totals[1], weights[2])
    ).astype(HALF)


def layer_kernel(seqs, *refs):
    step = pl.program_id(0)
    for seq in range(seqs):
        base, own, other = refs[seq * 3 : seq * 3 + 3]

        @pl.when(step == seq)
        def _():
            summed = own[...].astype(WIDE) + other[...].astype(WIDE)
            refs[-1][0] = (base[...] + summed).astype(HALF)


def final_kernel(seqs, *refs):
    x_ref, rows_ref = refs[:2]
    step = pl.program_id(0)
    for seq in range(seqs):
        residual_grad, own, other = refs[2 + seq * 3 : 5 + seq * 3]

        @pl.when(step == seq)
        def _():
            tensor = x_ref[0].astype(WIDE)
            spread = spread_of(tensor)
            unit = tensor * spread
            gradient = own[...].astype(WIDE) + other[...].astype(WIDE)
            scaled = gradient * rows_ref[14:15, :].astype(WIDE)
            refs[-1][0] = residual_grad[...] + spread * (
                scaled - unit * jnp.mean(scaled * unit, axis=-1, keepdims=True)
            )


def order_kernel(index, *refs):
    parts, out = refs[:-1], refs[-1]
    size = len(parts)
    for distance, part in enumerate(parts):
        out[lax.rem(index[0] + size - distance, size)] = part[...]


def join_kernel(flag, own, other, out):
    half = own.shape[2]
    for place in range(own.shape[0]):
        first = own[place, 0]
        second = other[place, 0]
        start = place * 2 * half
        out[0, start : start + half, :] = jnp.where(flag[0] == 0, first, second)
        out[0, start + half : start + 2 * half, :] = jnp.where(flag[0] == 0, second, first)


def place_kernel(order, own, near, *refs):
    outs = refs[-3:]
    part = own.shape[-1]
    for place, block in ((3, own.at[1]), (2, own.at[0]), (1, near.at[1]), (0, near.at[0])):
        lanes = pl.ds(pl.multiple_of(order[place] * part, part), part)
        for kind in range(3):
            outs[kind][0, :, lanes] = block[kind].astype(WIDE)


def swap(block, axis):
    size = lax.axis_size(axis)
    return lax.ppermute(block, axis, [(i, i ^ 1) for i in range(size)])


def shift(block, axis, distance):
    size = lax.axis_size(axis)
    route = [(i, i + distance) for i in range(size) if 0 <= i + distance < size]
    return lax.ppermute(block, axis, route)


def pick(stack, index, axis=0):
    return lax.dynamic_index_in_dim(stack, index, axis, keepdims=False)


def scatter_rows(tensor, dimension):
    return lax.psum_scatter(tensor, "fsdp", scatter_dimension=dimension, tiled=True)


def ring(block, distance):
    size = lax.axis_size("fsdp")
    return lax.ppermute(block, "fsdp", [(i, (i + distance) % size) for i in range(size)])


def gather_blocks(block):
    size = lax.axis_size("fsdp")
    if size > 4:
        return lax.all_gather(block, "fsdp", axis=0)
    blocks = [block] + [ring(block, distance) for distance in range(1, size)]
    if block.ndim == 3:
        parts = whole(block.shape)
        out = (size,) + block.shape
        index = lax.axis_index("fsdp").reshape(1).astype(jnp.int32)
        return call(
            order_kernel,
            (1,),
            [parts] * size,
            [(whole(out), struct(out, HALF))],
            moved=4 * block.size * size,
            prefetch=1,
        )(index, *blocks)[0]
    stacked = jnp.stack(blocks[::-1] * 2)
    return lax.dynamic_slice_in_dim(stacked, size - 1 - lax.axis_index("fsdp"), size, axis=0)


def scatter_blocks(blocks):
    size = lax.axis_size("fsdp")
    if size > 4:
        return lax.psum_scatter(blocks, "fsdp", scatter_dimension=0)
    index = lax.axis_index("fsdp")
    total = pick(blocks, index).astype(WIDE)
    for distance in range(1, size):
        sent = pick(blocks, lax.rem(index + distance, size))
        total = total + ring(sent, distance).astype(WIDE)
    return total.astype(blocks.dtype)


def sum_small(small):
    turned = swap(small, "tp")
    row = lax.broadcasted_iota(jnp.int32, small.shape, 0)
    small = small + jnp.where(row == 14, turned, 0.0)
    small = small + swap(small, "lo")
    small = small + swap(small, "hi")
    size = lax.axis_size("fsdp")
    return scatter_blocks(small.reshape(SMALL, size, D // size).transpose(1, 0, 2))


def shards(
    block_in,
    cotangent,
    prev_logits,
    routes,
    segments,
    w_query,
    w_key,
    w_value,
    w_out,
    w_gate,
    w_up,
    w_down,
    router,
    const_proj,
    const_vec,
    norm_attn,
    norm_moe,
):
    seqs, count = block_in.shape[:2]
    width = w_query.shape[1]
    pairs = width // PAIR
    deep = w_gate.shape[1]
    hidden = w_gate.shape[2]
    hi, lo = lax.axis_index("hi"), lax.axis_index("lo")
    hi_size = lax.axis_size("hi")
    ctx = hi * 2 + lo
    ctx_size = hi_size * 2
    fsdp_size = lax.axis_size("fsdp")
    part = hidden // ctx_size
    order = jnp.stack([(1 - hi) * 2 + 1 - lo, hi * 2 + 1 - lo, (1 - hi) * 2 + lo, ctx]).astype(
        jnp.int32
    )

    flag = lo.reshape(1).astype(jnp.int32)

    def gather_matrices(matrices):
        half = deep // 2
        own = jnp.stack(
            [lax.dynamic_slice_in_dim(w, lo * half, half, axis=0).astype(HALF) for w in matrices]
        )
        return gather_blocks(own)

    def join_matrices(own):
        other = swap(own, "lo")
        size, kinds, half = own.shape[:3]
        if half % 16 == 0:
            block = pl.BlockSpec((size, 1, half, width), lambda kind: (0, kind, 0, 0))
            return call(
                join_kernel,
                (kinds,),
                [pl.BlockSpec(memory_space=pltpu.SMEM), block, block],
                [
                    (
                        pl.BlockSpec((1, D, width), lambda kind: (kind, 0, 0)),
                        struct((kinds, D, width), HALF),
                    )
                ],
                moved=8 * kinds * D * width,
            )(flag, own, other)[0]
        halves = jnp.stack([jnp.where(lo == 0, own, other), jnp.where(lo == 0, other, own)], axis=2)
        return halves.transpose(1, 0, 2, 3, 4).reshape(own.shape[1], D, width)

    def expert_block(first, last):
        return jnp.stack(
            [
                lax.dynamic_slice_in_dim(w[first:last], ctx * part, part, axis=2).astype(HALF)
                for w in (w_gate, w_up, w_down)
            ]
        )

    def gather_experts(block):
        gathered = lax.all_gather(block, CTX + ("fsdp",), axis=0).reshape(
            (ctx_size, fsdp_size) + block.shape
        )
        if deep % 16 == 0:
            return gathered
        return gathered.transpose(0, 2, 3, 1, 4, 5).reshape(
            (ctx_size, 1) + block.shape[:2] + (D, part)
        )

    groups = ((0, 3), (3, 4))
    expert_own = [expert_block(*group) for group in groups]

    tp = lax.axis_index("tp")
    parts = []
    for place in range(2):
        rows = slice(place * (count // 2), (place + 1) * (count // 2))
        parts.append(shift(pick(block_in, tp)[rows], "hi", 1))
    input_halves = gather_matrices((w_query, w_key, w_value))
    input_halves, expert_own, parts = lax.optimization_barrier((input_halves, expert_own, parts))
    expert_weights = [gather_experts(block) for block in expert_own]
    input_weights = join_matrices(input_halves)
    own_rows = jnp.concatenate(parts, axis=0)
    others = [swap(rows, "tp") for rows in parts]
    far_ids = shift(segments, "hi", 1)
    near_ids = swap(jnp.where(lo == 1, far_ids, segments), "lo")
    far_ids = jnp.where(hi == 0, -1, far_ids)
    near_ids = jnp.where(ctx == 0, -1, near_ids)
    key_ids = jnp.concatenate([far_ids, near_ids, segments], axis=1)[:, None, :]
    query_ids = segments[:, :, None]

    small_rows = jnp.concatenate(
        [router.T, const_proj.T, const_vec.T, norm_attn[None, :], norm_moe[None, :]], axis=0
    ).astype(HALF)
    small_rows = gather_blocks(small_rows).transpose(1, 0, 2).reshape(SMALL, D)

    out_weights = join_matrices(gather_matrices((w_out,)))

    positions = (ctx - 2) * count + jnp.arange(3 * count, dtype=jnp.int32)
    lane = jnp.arange(PAIR, dtype=jnp.int32)
    frequency = 10000.0 ** (-2.0 * (lane % (HD // 2)).astype(WIDE) / HD)
    turned = positions.astype(WIDE)[:, None] * frequency[None, :]
    cosine = jnp.cos(turned).reshape(3, count, PAIR)
    sine = (jnp.sin(turned) * jnp.where((lane & (HD // 2)) == 0, -1.0, 1.0)).reshape(3, count, PAIR)

    rank_rows, rank_columns = call(
        rank_kernel,
        (seqs,),
        [
            pl.BlockSpec((1, 2, count), lambda s: (s, 0, 0)),
            pl.BlockSpec((1, count, 2), lambda s: (s, 0, 0)),
        ],
        [
            (pl.BlockSpec((1, ALL, count), lambda s: (s, 0, 0)), struct((seqs, ALL, count), WIDE)),
            (pl.BlockSpec((1, count, ALL), lambda s: (s, 0, 0)), struct((seqs, count, ALL), WIDE)),
        ],
        flops=4e7,
        moved=1e6,
    )(routes.transpose(0, 2, 1), routes)

    def project(rows, place, with_query):
        spread = struct((seqs, count, width), HALF)
        by_seq = pl.BlockSpec((1, count, width), lambda s: (s, 0, 0))
        by_row = pl.BlockSpec((1, count, D), lambda s: (s, 0, 0))
        kinds = 3 if with_query else 2
        return call(
            functools.partial(project_kernel, with_query),
            (seqs,),
            [
                by_row,
                whole((SMALL, D)),
                fixed((1, count, PAIR), (place, 0, 0)),
                fixed((1, count, PAIR), (place, 0, 0)),
                whole((3, D, width)),
            ],
            [(by_row, struct((seqs, count, D), HALF))] + [(by_seq, spread)] * kinds,
            flops=2 * seqs * count * D * width * kinds,
            moved=4 * D * width * 2 + seqs * count * (4 * D + 2 * width * kinds),
        )(rows, small_rows, cosine, sine, input_weights)

    normed0, key0, value0, query = project(block_in, 2, True)
    query, others = lax.optimization_barrier((query, others))
    other_rows = jnp.concatenate(others, axis=0)
    far_rows = jnp.stack(
        [jnp.where(tp == 0, own_rows, other_rows), jnp.where(tp == 0, other_rows, own_rows)]
    )
    near_rows = swap(jnp.where(lo == 1, far_rows, block_in), "lo")
    normed1, key1, value1 = project(near_rows, 1, False)
    normed2, key2, value2 = project(far_rows, 0, False)

    def pair_block(seq):
        return pl.BlockSpec((1, count, PAIR), lambda p, seq=seq: (seq, 0, p))

    flat_pair = pl.BlockSpec((count, PAIR), lambda p: (0, p))
    window_scratch = [
        pltpu.VMEM((2, TILE, 4 * TILE), WIDE),
        pltpu.VMEM((3 * count, PAIR), HALF),
        pltpu.VMEM((3 * count, PAIR), HALF),
    ]
    product = 2 * 2 * TILE * 5 * TILE * 256 * 2 * pairs

    def attend(seq):
        return call(
            attend_kernel,
            (pairs,),
            [pair_block(seq)] * 7
            + [
                fixed((1, count, 1), (seq, 0, 0)),
                fixed((1, 1, 3 * count), (seq, 0, 0)),
                pl.BlockSpec((1, D, PAIR), lambda p: (0, 0, p)),
            ],
            [
                (flat_pair, struct((count, width), HALF)),
                (flat_pair, struct((count, width), WIDE)),
                (whole((count, D)), struct((count, D), HALF)),
            ],
            window_scratch + [pltpu.VMEM((count, D), WIDE)],
            flops=4 * product,
            moved=1e7,
        )(query, key2, key1, key0, value2, value1, value0, query_ids, key_ids, out_weights)

    mixed, logs, attended, attended_other = [], [], [], []
    for seq in range(seqs):
        one, two, three = attend(seq)
        mixed.append(one)
        logs.append(two)
        attended.append(three)
        attended_other.append(swap(three, "tp"))

    flat = whole((count, D))
    flat_small = whole((count, ALL))

    def one_seq(seq, columns):
        return fixed((1, count, columns), (seq, 0, 0))

    routed, targets, scores = [], [], []
    for seq in range(seqs):
        one, two, three = call(
            route_kernel,
            (1,),
            [one_seq(seq, D), flat, flat, whole((SMALL, D)), one_seq(seq, 2), one_seq(seq, ALL)],
            [
                (flat, struct((count, D), HALF)),
                (flat_small, struct((count, ALL), WIDE)),
                (whole((count, SMALL)), struct((count, SMALL), WIDE)),
            ],
            flops=2 * count * D * 256,
            moved=count * D * 8,
        )(block_in, attended[seq], attended_other[seq], small_rows, routes, prev_logits)
        routed.append(one)
        targets.append(two)
        scores.append(three)

    slots = seqs * MOST
    weight_shape = expert_weights[0].shape
    weight_block = (1,) + weight_shape[1:2] + (3, 1) + weight_shape[4:]
    out_slots, grad_slots, held, crossing, scattered = [], [], [], [], []
    for expert in range(EXPERTS):
        piece = (1, 3, D, part)
        group = 0 if expert < groups[1][0] else 1
        place = expert - groups[group][0]
        theirs, mine, one, two, *extra = call(
            functools.partial(expert_kernel, expert),
            (ctx_size,),
            [
                flat,
                flat,
                whole((seqs, count, D)),
                flat_small,
                flat_small,
                whole((seqs, ALL, count)),
                pl.BlockSpec(
                    weight_block, lambda j, o, place=place: (o[j], 0, 0, place, 0, 0)
                ),
            ],
            [
                (
                    pl.BlockSpec(piece, lambda j, o: (jnp.minimum(j, 1), 0, 0, 0)),
                    struct((2, 3, D, part), HALF),
                ),
                (
                    pl.BlockSpec(piece, lambda j, o: (jnp.maximum(j - 2, 0), 0, 0, 0)),
                    struct((2, 3, D, part), HALF),
                ),
                (whole((slots, D)), struct((slots, D), HALF)),
                (whole((slots, D)), struct((slots, D), HALF)),
            ],
            [
                pltpu.VMEM((slots, D), HALF),
                pltpu.VMEM((D, slots), HALF),
                pltpu.VMEM((slots, D), HALF),
                pltpu.VMEM((D, slots), HALF),
                pltpu.VMEM((slots, D), WIDE),
                pltpu.VMEM((slots, D), WIDE),
            ],
            flops=2 * 9 * slots * D * hidden,
            moved=12 * D * hidden + 8 * slots * D,
            prefetch=1,
            side=side_sum(ctx_size, held[expert - 2]) if expert >= 2 else None,
            after=out_slots[-1:],
        )(order, routed[0], routed[1], cotangent, targets[0], targets[1], rank_rows, expert_weights[group])
        out_slots.append(one)
        grad_slots.append(two)
        held.append((mine, swap(theirs, "lo")))
        if extra:
            scattered.append(scatter_rows(extra[0].reshape(2, 3, D, part), 2))

    def finish(total):
        scattered.append(scatter_rows(total.reshape(3, D, part), 1))

    def couple_of(expert):
        own = scattered[expert]
        across = swap(own, "hi")
        return own + across[::-1] if expert < 2 else jnp.stack([across, own])

    back, back_other, sums, sums_other = [], [], [], []
    tiles = 4
    tile = count // tiles

    def tile_rows(columns):
        return pl.BlockSpec((tile, columns), lambda t: (t, 0))

    def tile_seq(seq, columns):
        return pl.BlockSpec((1, tile, columns), lambda t: (seq, t, 0))

    for seq in range(seqs):
        slot_block = fixed((MOST, D), (seq, 0))
        one, two, sent = call(
            combine_kernel,
            (tiles,),
            [slot_block] * (2 * EXPERTS)
            + [tile_seq(seq, ALL), tile_rows(ALL), tile_seq(seq, D)],
            [
                (tile_rows(D + PAIR), struct((count, D + PAIR), HALF)),
                (tile_rows(D), struct((count, D), HALF)),
            ],
            flops=4 * count * EXPERTS * MOST * D,
            moved=4 * slots * D + 6 * count * D,
            side=side_sum(tiles, held[2 + seq], 0),
        )(*out_slots, *grad_slots, rank_columns, targets[seq], cotangent)
        back.append(one)
        sums.append(two)
        back_other.append(swap(one, "tp"))
        crossing.append(swap(sent, "hi"))
    for seq in range(seqs):
        sums_other.append(swap(sums[seq], "tp"))

    residual_grads, cots, mixed_grads, extras, bases, talls = [], [], [], [], [], []
    def turn(seq):
        results = call(
            turn_kernel,
            (tiles,),
            [
                tile_seq(seq, D),
                tile_rows(D),
                tile_rows(D),
                tile_seq(seq, D),
                tile_rows(D + PAIR),
                tile_rows(D + PAIR),
                tile_rows(ALL),
                tile_rows(SMALL),
                whole((SMALL, D)),
                whole((1, D, width)),
            ],
            [
                (tile_rows(D), struct((count, D), WIDE)),
                (tile_rows(D), struct((count, D), HALF)),
                (tile_rows(width), struct((count, width), HALF)),
                (whole((8, D)), struct((8, D), WIDE)),
                (tile_rows(D), struct((count, D), WIDE)),
                (tile_rows(PAIR), struct((count, PAIR), HALF)),
            ],
            flops=2 * count * D * width,
            moved=count * D * 22,
            after=(scattered[1],) if seq else (),
        )(
            block_in,
            attended[seq],
            attended_other[seq],
            cotangent,
            back[seq],
            back_other[seq],
            targets[seq],
            scores[seq],
            small_rows,
            out_weights,
        )
        for kept, result in zip(
            (residual_grads, cots, mixed_grads, extras, bases, talls), results, strict=True
        ):
            kept.append(result)

    query_grads, grads2, grads1, grads0 = [], [], [], []
    pair_out = (
        pl.BlockSpec((2, count, PAIR), lambda p: (0, 0, p)),
        struct((2, count, width), HALF),
    )
    table = whole((3, count, PAIR))
    near_grads, far_grads, sents = [], [], []

    def attend_back(seq):
        results = call(
            attend_back_kernel,
            (pairs,),
            [pair_block(seq)] * 7
            + [
                fixed((1, count, 1), (seq, 0, 0)),
                fixed((1, 1, 3 * count), (seq, 0, 0)),
                flat_pair,
                flat_pair,
                table,
                table,
            ],
            [(flat_pair, struct((count, width), HALF))] + [pair_out] * 3,
            window_scratch
            + [pltpu.VMEM((PAIR, 3 * count), WIDE), pltpu.VMEM((PAIR, 3 * count), WIDE)],
            flops=10 * product,
            moved=1e7,
            after=(sums_other[seq],) + ((sents[0], couples[0]) if seq else ()),
            side=side_sum(pairs, held[2 + seq], 1, (crossing[seq],)),
        )(
            query,
            key2,
            key1,
            key0,
            value2,
            value1,
            value0,
            query_ids,
            key_ids,
            mixed_grads[seq],
            logs[seq],
            cosine,
            sine,
        )
        for kept, result in zip((query_grads, grads2, grads1, grads0), results[:4], strict=True):
            kept.append(result)
        finish(results[4])
        near_grads.append(swap(results[2], "lo"))

    def send_back(seq, after):
        sents.append(
            call(
                relay_kernel,
                (2,),
                [pl.BlockSpec(memory_space=pltpu.SMEM)]
                + [pl.BlockSpec((1, count, width), lambda kind: (kind, 0, 0))] * 2,
                [
                    (
                        pl.BlockSpec((1, count, width), lambda kind: (kind, 0, 0)),
                        struct((2, count, width), HALF),
                    )
                ],
                moved=12 * count * width,
                after=after,
            )(flag, grads2[seq], near_grads[seq])[0]
        )
        far_grads.append(shift(sents[seq], "hi", -1))

    def enter(seq, after):
        one = call(
            input_kernel,
            (tiles // 2,),
            [
                pl.BlockSpec((2 * tile, width), lambda t: (t, 0)),
            ]
            + [pl.BlockSpec((2, 2 * tile, width), lambda t: (0, t, 0))] * 3
            + [
                pl.BlockSpec(memory_space=pltpu.SMEM),
                whole((3, D, width)),
            ],
            [
                (
                    pl.BlockSpec((2 * tile, D), lambda t: (t, 0)),
                    struct((count, D), HALF),
                )
            ],
            flops=6 * count * D * width,
            moved=8 * D * width + count * (14 * width + 2 * D),
            after=after,
        )(query_grads[seq], grads0[seq], near_grads[seq], far_grads[seq], flag, input_weights)[0]
        input_parts.append(one)
        input_others.append(swap(one, "tp"))

    input_parts, input_others = [], []
    turn(0)
    attend_back(0)
    couples = [couple_of(0)]
    turn(1)
    send_back(0, ())
    attend_back(1)
    enter(0, (query_grads[1], scattered[2]))
    send_back(1, (input_parts[0],))
    couples.append(couple_of(1))
    couples.append(couple_of(2))

    def half_map(seq):
        last = 1 if seq == 0 else 0
        return lambda s, t: (jnp.where(s == seq, t, last), 0)

    operands, specs = [], []
    columns = D // 3

    def by_column(rows, lead=()):
        zeros = (0,) * len(lead)
        return pl.BlockSpec(lead + (rows, columns), lambda t: zeros + (0, t))

    for seq in range(seqs):
        operands += [normed2, normed1, normed0, query_grads[seq], grads2[seq], grads1[seq], grads0[seq]]
        operands += [cots[seq], mixed[seq], talls[seq], extras[seq]]
        specs += [pl.BlockSpec((1, count, columns), lambda t, seq=seq: (seq, 0, t))] * 3
        specs += [whole((count, width))] + [whole((2, count, width))] * 3
        specs += [by_column(count), whole((count, width)), whole((count, PAIR)), by_column(8)]
    by_depth = pl.BlockSpec((3, columns, width), lambda t: (0, t, 0))
    attention_grads, small = call(
        functools.partial(weight_kernel, seqs),
        (3,),
        specs + [by_depth, by_column(SMALL)],
        [
            (
                pl.BlockSpec((4, columns, width), lambda t: (0, t, 0)),
                struct((4, D, width), HALF),
            ),
            (by_column(SMALL), struct((SMALL, D), WIDE)),
        ],
        flops=2 * 8 * seqs * count * D * width,
        moved=2 * (4 * D * width * 2 + seqs * count * (4 * D + 8 * width)),
        after=(sents[1], couples[1]),
    )(*operands, input_weights, small_rows)
    tall_rows = sum(
        lax.dot_general(
            talls[seq][:, :SMALL], routed[seq], (((0,), (0,)), ((), ())), preferred_element_type=WIDE
        )
        for seq in range(seqs)
    )
    small = sum_small(small + tall_rows)

    paired = attention_grads.reshape(2, 2, D, width)
    theirs = pick(paired, 1 - lo, 1)
    layer_out = call(
        functools.partial(layer_kernel, seqs),
        (seqs, 2),
        [
            pl.BlockSpec((2 * tile, D), half_map(seq))
            for seq in range(seqs)
            for _ in range(3)
        ],
        [
            (
                pl.BlockSpec((1, 2 * tile, D), lambda s, t: (s, t, 0)),
                struct((seqs, count, D), HALF),
            )
        ],
        moved=seqs * count * D * 10,
        after=(theirs,),
    )(*[array for seq in range(seqs) for array in (bases[seq], sums[seq], sums_other[seq])])[0]
    enter(1, (layer_out, couples[2]))
    received = swap(theirs, "lo")
    received, input_parts[1] = lax.optimization_barrier((received, input_parts[1]))
    input_others[1] = swap(input_parts[1], "tp")

    by_tile = pl.BlockSpec((1, tile, D), lambda s, t: (s, t, 0))
    operands, specs = [block_in, small_rows], [by_tile, whole((SMALL, D))]
    for seq in range(seqs):
        operands += [residual_grads[seq], input_parts[seq], input_others[seq]]
        last = tiles - 1 if seq == 0 else 0
        specs += [
            pl.BlockSpec(
                (tile, D), lambda s, t, seq=seq, last=last: (jnp.where(s == seq, t, last), 0)
            )
        ] * 3
    grad_input = call(
        functools.partial(final_kernel, seqs),
        (seqs, tiles),
        specs,
        [
            (by_tile, struct((seqs, count, D), WIDE)),
        ],
        flops=20 * seqs * count * D,
        moved=seqs * count * D * 14,
    )(*operands)[0]

    kept = pick(paired, lo, 1)
    crossing = swap(pick(kept, 1 - hi) + pick(received, 1 - hi), "hi")
    own = (pick(kept, hi) + pick(received, hi) + crossing).reshape(fsdp_size, deep, width)
    own = scatter_blocks(own)
    across = swap(own, "hi")
    couple = jnp.stack([jnp.where(hi == 0, own, across), jnp.where(hi == 0, across, own)])
    other = swap(couple, "lo")
    wide_couple, wide_other = couple.astype(WIDE), other.astype(WIDE)
    lower = jnp.where(lo == 0, wide_couple, wide_other)
    higher = jnp.where(lo == 0, wide_other, wide_couple)

    couples.append(couple_of(3))
    grads = None
    for expert in range(EXPERTS):
        couple = couples[expert]
        other = swap(couple, "lo")
        result = struct((EXPERTS, deep, hidden), WIDE)
        out_spec = fixed((1, deep, hidden), (expert, 0, 0))
        previous = [] if grads is None else list(grads)
        grads = call(
            place_kernel,
            (1,),
            [whole((2, 3, deep, part))] * 2
            + [pl.BlockSpec(memory_space=pl.ANY)] * len(previous),
            [(out_spec, result)] * 3,
            moved=3 * deep * hidden * 6,
            prefetch=1,
            aliases={3 + kind: kind for kind in range(3)} if previous else None,
        )(order, couple, other, *previous)

    return (
        layer_out,
        grad_input,
        lower[0],
        higher[0],
        lower[1],
        higher[1],
        *grads,
        small[0:8].T,
        small[8:12].T,
        small[12:14].T,
        small[14],
        small[15],
    )


def solution(mesh):
    sizes = mesh.shape
    inner = Mesh(
        mesh.devices.reshape(sizes["fsdp"], sizes["ctx"] // 2, 2, sizes["tp"]),
        ("fsdp", "hi", "lo", "tp"),
    )
    rows = P("fsdp", CTX, None)
    matrix = P("fsdp", "tp")
    experts = P(None, "fsdp", "tp")
    narrow = P("fsdp", None)
    vector = P("fsdp")
    return jax.shard_map(
        shards,
        mesh=inner,
        in_specs=(rows,) * 4
        + (P("fsdp", CTX),)
        + (matrix,) * 4
        + (experts,) * 3
        + (narrow,) * 3
        + (vector,) * 2,
        out_specs=(rows,) * 2
        + (matrix,) * 4
        + (experts,) * 3
        + (narrow,) * 3
        + (vector,) * 2,
        check_vma=False,
    )
```

```python
import functools

import jax
import jax.numpy as jnp
from jax import lax
from jax.experimental import pallas as pl
from jax.experimental.pallas import tpu as pltpu
from jax.sharding import Mesh
from jax.sharding import PartitionSpec as P

D = 768
HEADS = 12
HD = 64
EXPERTS = 4
ALL = 8
WINDOW = 1024
MOST = 192

EPSILON = 1e-06
MASKED = -1e30

CTX = ("hi", "lo")
HALF = jnp.bfloat16
WIDE = jnp.float32
TILE = 256
PAIR = 2 * HD
SMALL = 16
MIB = 1 << 20
SCALE = 2.0
MICROS = {
    "project_kernel": 6,
    "attend_kernel": 12,
    "route_kernel": 3,
    "expert_kernel": 17,
    "combine_kernel": 7,
    "turn_kernel": 11,
    "attend_back_kernel": 19,
    "weight_kernel": 12,
    "input_kernel": 4,
    "layer_kernel": 5,
    "final_kernel": 8,
    "place_kernel": 5,
    "join_kernel": 4,
    "cast_kernel": 4,
}


def nn(a, b):
    return jnp.dot(a, b, preferred_element_type=WIDE)


def nt(a, b):
    return lax.dot_general(a, b, (((1,), (1,)), ((), ())), preferred_element_type=WIDE)


def call(
    body,
    grid,
    ins,
    outs,
    scratch=(),
    prefetch=0,
    aliases=None,
    after=(),
    side=(),
):
    operands = [array for job in side for array in job[0]]
    specs = [spec for job in side for spec in job[1]]
    name = getattr(body, "func", body).__name__
    own = prefetch + len(ins)
    first = own + len(operands) + len(after)

    def inner(*refs):
        start, results = own, first + len(outs)
        for place, job in enumerate(side):
            total = refs[start][...].astype(WIDE)
            for ref in refs[start + 1 : start + len(job[0])]:
                total = total + ref[...].astype(WIDE)
            refs[results + place][...] = total.astype(HALF)
            start += len(job[0])
        body(*refs[:own], *refs[first:results], *refs[results + len(side) :])

    all_outs = list(outs) + [job[2] for job in side]
    grid_spec = pltpu.PrefetchScalarGridSpec(
        num_scalar_prefetch=prefetch,
        grid=grid,
        in_specs=list(ins) + specs + [pl.BlockSpec(memory_space=pl.ANY)] * len(after),
        out_specs=[spec for spec, _ in all_outs],
        scratch_shapes=list(scratch),
    )
    kernel = pl.pallas_call(
        inner,
        grid_spec=grid_spec,
        out_shape=[shape for _, shape in all_outs],
        input_output_aliases=aliases or {},
        compiler_params=pltpu.CompilerParams(
            dimension_semantics=("arbitrary",) * len(grid), vmem_limit_bytes=64 * MIB
        ),
        cost_estimate=pl.CostEstimate(
            flops=int(MICROS.get(name, 2) * SCALE * 1e9), bytes_accessed=0, transcendentals=0
        ),
    )
    return lambda *arrays: kernel(*arrays, *operands, *after)


def side_sum(steps, stacks, index=None, plain=()):
    flat = [stack.reshape(-1, stack.shape[-1]) for stack in stacks]
    rows, columns = flat[0].shape
    rows = rows if index is None else rows // stacks[0].shape[0]
    start = 0 if index is None else index * steps
    block = (rows // steps, columns)
    out = pl.BlockSpec(block, lambda step, *_: (step, 0))
    specs = [pl.BlockSpec(block, lambda step, *_: (start + step, 0))] * len(flat)
    flat += [array.reshape(rows, columns) for array in plain]
    specs += [out] * len(plain)
    return flat, specs, (out, struct((rows, columns), HALF))


def whole(shape):
    zeros = (0,) * len(shape)
    return pl.BlockSpec(shape, lambda *_: zeros)


def fixed(block, place):
    return pl.BlockSpec(block, lambda *_: place)


def struct(shape, dtype):
    return jax.ShapeDtypeStruct(shape, dtype)


def spread_of(tensor):
    return lax.rsqrt(jnp.mean(tensor * tensor, axis=-1, keepdims=True) + EPSILON)


def partner(tensor):
    lane = lax.broadcasted_iota(jnp.int32, tensor.shape, 1)
    return jnp.where(
        (lane & (HD // 2)) == 0,
        pltpu.roll(tensor, PAIR - HD // 2, 1),
        pltpu.roll(tensor, HD // 2, 1),
    )


def rank_kernel(routes_t, routes, rank_rows, rank_columns):
    count = routes.shape[1]
    down = lax.broadcasted_iota(jnp.int32, (count, count), 0)
    across = lax.broadcasted_iota(jnp.int32, (count, count), 1)
    before = jnp.where(down < across, 1.0, 0.0).astype(HALF)
    after = jnp.where(across < down, 1.0, 0.0).astype(HALF)
    row_target = lax.broadcasted_iota(jnp.int32, (ALL, count), 0)
    names = (routes_t[0, 0:1, :] == row_target) | (routes_t[0, 1:2, :] == row_target)
    ranks = nn(jnp.where(names, 1.0, 0.0).astype(HALF), before)
    rank_rows[0] = jnp.where(names, ranks, -1.0)
    column_target = lax.broadcasted_iota(jnp.int32, (count, ALL), 1)
    named = (routes[0, :, 0:1] == column_target) | (routes[0, :, 1:2] == column_target)
    ranked = nn(after, jnp.where(named, 1.0, 0.0).astype(HALF))
    rank_columns[0] = jnp.where(named, ranked, -1.0)


def project_kernel(with_query, *refs):
    x_ref, rows_ref, cos_ref, sin_ref, weights = refs[:5]
    outs = refs[5:]
    tensor = x_ref[0].astype(WIDE)
    unit = tensor * spread_of(tensor)
    normed = (unit * rows_ref[14:15, :].astype(WIDE)).astype(HALF)
    outs[0][0] = normed
    cosine, sine = cos_ref[0], sin_ref[0]

    def turned(matrix, out, scale):
        flat = nn(normed, weights[matrix])
        for piece in range(flat.shape[1] // PAIR):
            lanes = slice(piece * PAIR, (piece + 1) * PAIR)
            part = flat[:, lanes]
            result = (part * cosine + partner(part) * sine).astype(HALF)
            out[0, :, lanes] = result if scale is None else result * scale

    turned(1, outs[1], None)
    outs[2][0] = nn(normed, weights[2]).astype(HALF)
    if with_query:
        turned(0, outs[3], jnp.asarray(HD ** (-0.5), HALF))


def fill_bias(query_ids, key_ids, bias):
    upper = upper_of()
    for tile in range(2):
        ids = query_ids[0, tile * TILE : (tile + 1) * TILE, :]
        first = key_ids[0, :, tile * TILE : (tile + 1) * TILE]
        last = key_ids[0, :, (tile + 4) * TILE : (tile + 5) * TILE]
        mixed = jnp.where(upper, first, last)
        bias[tile, :, :TILE] = jnp.where(mixed == ids, 0.0, MASKED)
        inner = key_ids[0, :, (tile + 1) * TILE : (tile + 4) * TILE]
        bias[tile, :, TILE:] = jnp.where(inner == ids, 0.0, MASKED)


def upper_of():
    down = lax.broadcasted_iota(jnp.int32, (TILE, TILE), 0)
    across = lax.broadcasted_iota(jnp.int32, (TILE, TILE), 1)
    return across > down


def head_lanes(head, rows):
    lane = lax.broadcasted_iota(jnp.int32, (rows, PAIR), 1)
    return (lane < HD) if head == 0 else (lane >= HD)


def folded(upper, spread):
    span = spread.shape[1]
    return (
        jnp.where(upper, spread[:, :TILE], spread[:, span - TILE :]),
        spread[:, TILE : span - TILE],
    )


def unfolded(upper, ends, middle):
    return jnp.concatenate(
        [jnp.where(upper, ends, 0.0), middle, jnp.where(upper, 0.0, ends)], axis=1
    ).astype(HALF)


def load_window(parts, window):
    rows = parts[0].shape[1]
    for place, part in enumerate(parts):
        window[place * rows : (place + 1) * rows, :] = part[0]


def attend_kernel(
    query, k2, k1, k0, v2, v1, v0, query_ids, key_ids, w_out, mixed, logs, attended, bias, keys, values, total
):
    step = pl.program_id(0)

    @pl.when(step == 0)
    def _():
        fill_bias(query_ids, key_ids, bias)

    load_window((k2, k1, k0), keys)
    load_window((v2, v1, v0), values)
    upper = upper_of()
    span = 5 * TILE
    for tile in range(2):
        rows = slice(tile * TILE, (tile + 1) * TILE)
        window = slice(tile * TILE, tile * TILE + span)
        results, totals = [], []
        for head in range(2):
            chosen = head_lanes(head, TILE)
            own = jnp.where(chosen, query[0, rows, :], jnp.zeros((), HALF))
            ends, middle = folded(upper, nt(own, keys[window, :]))
            ends = ends + bias[tile, :, :TILE]
            middle = middle + bias[tile, :, TILE:]
            highest = jnp.maximum(
                jnp.max(ends, axis=-1, keepdims=True), jnp.max(middle, axis=-1, keepdims=True)
            )
            ends = jnp.exp(ends - highest)
            middle = jnp.exp(middle - highest)
            summed = jnp.sum(ends, axis=-1, keepdims=True) + jnp.sum(middle, axis=-1, keepdims=True)
            out = nn(unfolded(upper, ends, middle), values[window, :]) / summed
            results.append(out)
            totals.append(jnp.broadcast_to(highest + jnp.log(summed), (TILE, PAIR)))
        chosen = head_lanes(0, TILE)
        mixed[rows, :] = jnp.where(chosen, results[0], results[1]).astype(HALF)
        logs[rows, :] = jnp.where(chosen, totals[0], totals[1])
    product = nt(mixed[...], w_out[0])

    @pl.when(step == 0)
    def _():
        total[...] = product

    @pl.when(step > 0)
    def _():
        total[...] += product

    @pl.when(step == pl.num_programs(0) - 1)
    def _():
        attended[...] = total[...].astype(HALF)


def residual_of(x_ref, own, other):
    return x_ref[0].astype(WIDE) + (own[...].astype(WIDE) + other[...].astype(WIDE))


def route_kernel(x_ref, own, other, rows_ref, routes, prev, routed_ref, targets_ref, scores_ref):
    residual = residual_of(x_ref, own, other)
    unit = residual * spread_of(residual)
    routed = (unit * rows_ref[15:16, :].astype(WIDE)).astype(HALF)
    routed_ref[...] = routed
    scores = nt(routed, rows_ref[...])
    scores_ref[...] = scores
    logits = scores[:, :ALL] + prev[0]
    target = lax.broadcasted_iota(jnp.int32, logits.shape, 1)
    first = routes[0, :, 0:1] == target
    second = routes[0, :, 1:2] == target
    zero = jnp.sum(jnp.where(first, logits, 0.0), axis=-1, keepdims=True)
    one = jnp.sum(jnp.where(second, logits, 0.0), axis=-1, keepdims=True)
    highest = jnp.maximum(zero, one)
    zero, one = jnp.exp(zero - highest), jnp.exp(one - highest)
    summed = zero + one
    targets_ref[...] = jnp.where(first, zero / summed, 0.0) + jnp.where(second, one / summed, 0.0)


def expert_kernel(
    expert, order, routed_a, routed_b, upstream, targets_a, targets_b, ranks, weights, theirs, mine, out_slots,
    grad_slots, rows, rows_t, cots, cots_t, out_total, grad_total
):
    step = pl.program_id(0)
    count = routed_a.shape[0]

    @pl.when(step == 0)
    def _():
        slot = lax.broadcasted_iota(jnp.int32, (MOST, count), 0).astype(WIDE)
        for seq, (routed, targets) in enumerate(((routed_a, targets_a), (routed_b, targets_b))):
            place = slice(seq * MOST, (seq + 1) * MOST)
            spread = jnp.where(slot == ranks[seq, expert : expert + 1, :], 1.0, 0.0).astype(HALF)
            rows[place, :] = nn(spread, routed[...]).astype(HALF)
            weighted = targets[:, expert : expert + 1] * upstream[seq].astype(WIDE)
            cots[place, :] = nn(spread, weighted.astype(HALF)).astype(HALF)
        rows_t[...] = rows[...].T
        cots_t[...] = cots[...].T

    here = [weights[0, :, kind, 0].reshape(D, weights.shape[-1]) for kind in range(3)]
    gate = nn(rows[...], here[0])
    up = nn(rows[...], here[1])
    sigmoid = 1.0 / (1.0 + jnp.exp(-gate))
    silu = gate * sigmoid
    activated = (silu * up).astype(HALF)
    activated_grad = nn(cots[...], here[2])
    up_grad = (activated_grad * silu).astype(HALF)
    gate_grad = (activated_grad * up * sigmoid * (1.0 + gate * (1.0 - sigmoid))).astype(HALF)
    out_part = nt(activated, here[2])
    grad_part = nt(gate_grad, here[0]) + nt(up_grad, here[1])

    @pl.when(step == 0)
    def _():
        out_total[...] = out_part
        grad_total[...] = grad_part

    @pl.when(step > 0)
    def _():
        out_total[...] += out_part
        grad_total[...] += grad_part

    grads = (nn(rows_t[...], gate_grad), nn(rows_t[...], up_grad), nn(cots_t[...], activated))

    @pl.when(step < 2)
    def _():
        for kind in range(3):
            theirs[0, kind] = grads[kind].astype(HALF)

    @pl.when(step >= 2)
    def _():
        for kind in range(3):
            mine[0, kind] = grads[kind].astype(HALF)

    @pl.when(step == pl.num_programs(0) - 1)
    def _():
        out_slots[...] = out_total[...].astype(HALF)
        grad_slots[...] = grad_total[...].astype(HALF)


def combine_kernel(*refs):
    outs, grads = refs[:EXPERTS], refs[EXPERTS : 2 * EXPERTS]
    ranks, targets, upstream, back_ref, sum_ref = refs[2 * EXPERTS :]
    count = upstream.shape[1]
    slot = lax.broadcasted_iota(jnp.int32, (count, MOST), 1).astype(WIDE)
    wide = upstream[0].astype(WIDE)
    back = total = None
    lane = lax.broadcasted_iota(jnp.int32, (count, PAIR), 1)
    dots = jnp.zeros((count, PAIR), WIDE)
    for expert in range(EXPERTS):
        spread = jnp.where(slot == ranks[0, :, expert : expert + 1], 1.0, 0.0).astype(HALF)
        part = nn(spread, grads[expert][...])
        back = part if back is None else back + part
        part = nn(spread, outs[expert][...])
        dots = dots + jnp.where(lane == expert, jnp.sum(part * wide, axis=-1, keepdims=True), 0.0)
        part = part * targets[:, expert : expert + 1]
        total = part if total is None else total + part
    back_ref[:, :D] = back.astype(HALF)
    main = dots.astype(HALF)
    rest = pltpu.roll(dots - main.astype(WIDE), ALL, 1)
    back_ref[:, D:] = jnp.where(lane < ALL, main.astype(WIDE), rest).astype(HALF)
    sum_ref[...] = total.astype(HALF)


def turn_kernel(
    x_ref, own, other, upstream, back_own, back_other, targets, scores, rows_ref, w_out, residual_grad_ref, cot_ref,
    mixed_grad_ref, small_ref, base_ref, tall_ref
):
    residual = residual_of(x_ref, own, other)
    spread = spread_of(residual)
    unit = residual * spread
    gain = rows_ref[15:16, :].astype(WIDE)
    routed = (unit * gain).astype(HALF)
    routed_wide = routed.astype(WIDE)
    up_half = upstream[0]
    up = up_half.astype(WIDE)
    vector = [rows_ref[12 + place : 13 + place, :].astype(WIDE) for place in range(2)]
    chosen = targets[...]
    mixing = scores[:, ALL : ALL + 4]

    def softmax_two(a, b):
        highest = jnp.maximum(a, b)
        a, b = jnp.exp(a - highest), jnp.exp(b - highest)
        return a / (a + b), b / (a + b)

    first = softmax_two(mixing[:, 0:1], mixing[:, 1:2])
    second = softmax_two(mixing[:, 2:3], mixing[:, 3:4])
    weight = [chosen[:, place : place + 1] for place in range(ALL)]
    base_ref[...] = (
        residual
        + routed_wide * (weight[5] + weight[6] * first[0] + weight[7] * second[0])
        + (weight[6] * first[1]) * vector[0]
        + (weight[7] * second[1]) * vector[1]
    )
    dot_routed = jnp.sum(up * routed_wide, axis=-1, keepdims=True)
    dot_small = nt(up_half, rows_ref[...])
    dot_vector = (dot_small[:, 12:13], dot_small[:, 13:14])
    halves = back_own[:, D:].astype(WIDE) + back_other[:, D:].astype(WIDE)
    halves = halves[:, :ALL] + halves[:, ALL : 2 * ALL]
    lane = lax.broadcasted_iota(jnp.int32, halves.shape, 1)
    dots = (
        jnp.where(lane < EXPERTS, halves, 0.0)
        + jnp.where(lane == EXPERTS + 1, dot_routed, 0.0)
        + jnp.where(lane == EXPERTS + 2, first[0] * dot_routed + first[1] * dot_vector[0], 0.0)
        + jnp.where(lane == EXPERTS + 3, second[0] * dot_routed + second[1] * dot_vector[1], 0.0)
    )
    logit_grad = chosen * (dots - jnp.sum(chosen * dots, axis=-1, keepdims=True))

    def mix_back(mix, scale, other_dot):
        one, two = scale * dot_routed, scale * other_dot
        inner = mix[0] * one + mix[1] * two
        return mix[0] * (one - inner), mix[1] * (two - inner)

    const_first = mix_back(first, weight[6], dot_vector[0])
    const_second = mix_back(second, weight[7], dot_vector[1])
    lane = lax.broadcasted_iota(jnp.int32, (up.shape[0], SMALL), 1)
    tall = jnp.concatenate([logit_grad, jnp.zeros_like(logit_grad)], axis=1)
    for place, column in enumerate(const_first + const_second):
        tall = tall + jnp.where(lane == ALL + place, column, 0.0)
    tall = tall.astype(HALF)
    tall_ref[...] = jnp.concatenate(
        [tall, jnp.zeros((up.shape[0], PAIR - SMALL), HALF)], axis=1
    )
    back = back_own[:, :D].astype(WIDE) + back_other[:, :D].astype(WIDE)
    routed_grad = (
        back + nn(tall, rows_ref[...]) + up * (weight[5] + first[0] * weight[6] + second[0] * weight[7])
    )
    zero = jnp.zeros((1, D), WIDE)
    sums = jnp.concatenate(
        [
            jnp.sum((first[1] * weight[6]) * up, axis=0, keepdims=True),
            jnp.sum((second[1] * weight[7]) * up, axis=0, keepdims=True),
            zero,
            jnp.sum(routed_grad * unit, axis=0, keepdims=True),
            zero,
            zero,
            zero,
            zero,
        ],
        axis=0,
    )
    step = pl.program_id(0)

    @pl.when(step == 0)
    def _():
        small_ref[...] = sums

    @pl.when(step > 0)
    def _():
        small_ref[...] += sums

    scaled = routed_grad * gain
    residual_grad = up + spread * (scaled - unit * jnp.mean(scaled * unit, axis=-1, keepdims=True))
    residual_grad_ref[...] = residual_grad
    cot = residual_grad.astype(HALF)
    cot_ref[...] = cot
    mixed_grad_ref[...] = nn(cot, w_out[0]).astype(HALF)


def attend_back_kernel(
    query, k2, k1, k0, v2, v1, v0, query_ids, key_ids, mixed_grad, logs, cos_ref, sin_ref, query_grad, grad2, grad1,
    grad0, bias, keys, values, key_total, value_total
):
    step = pl.program_id(0)

    @pl.when(step == 0)
    def _():
        fill_bias(query_ids, key_ids, bias)

    load_window((k2, k1, k0), keys)
    load_window((v2, v1, v0), values)
    upper = upper_of()
    span = 5 * TILE
    count = query.shape[1]

    def turned_back(gradient, place, rows):
        cosine, sine = cos_ref[place, rows, :], sin_ref[place, rows, :]
        return (gradient * cosine - partner(gradient) * sine).astype(HALF)

    key_total[...] = jnp.zeros_like(key_total)
    value_total[...] = jnp.zeros_like(value_total)
    for tile in range(2):
        rows = slice(tile * TILE, (tile + 1) * TILE)
        window = slice(tile * TILE, tile * TILE + span)
        results = []
        for head in range(2):
            chosen = head_lanes(head, TILE)
            nothing = jnp.zeros((), HALF)
            own = jnp.where(chosen, query[0, rows, :], nothing)
            out_grad = jnp.where(chosen, mixed_grad[rows, :], nothing)
            level = logs[rows, head * HD : head * HD + 1]
            ends, middle = folded(upper, nt(own, keys[window, :]))
            ends = jnp.exp(ends + bias[tile, :, :TILE] - level)
            middle = jnp.exp(middle + bias[tile, :, TILE:] - level)
            value_total[:, window] += nn(out_grad.T, unfolded(upper, ends, middle))
            ends_grad, middle_grad = folded(upper, nt(out_grad, values[window, :]))
            expected = jnp.sum(ends * ends_grad, axis=-1, keepdims=True) + jnp.sum(
                middle * middle_grad, axis=-1, keepdims=True
            )
            score_grad = unfolded(upper, ends * (ends_grad - expected), middle * (middle_grad - expected))
            key_total[:, window] += nn(own.T, score_grad)
            results.append(nn(score_grad, keys[window, :]))
        gradient = jnp.where(head_lanes(0, TILE), results[0], results[1]) * HD ** (-0.5)
        query_grad[rows, :] = turned_back(gradient, 2, rows)
    for place, grad in enumerate((grad2, grad1, grad0)):
        window = slice(place * count, (place + 1) * count)
        grad[0] = turned_back(key_total[:, window].T, place, slice(0, count))
        grad[1] = value_total[:, window].T.astype(HALF)


def weight_kernel(seqs, *refs):
    each = 3 + 1 + 3 + 3 + 1
    groups = [refs[seq * each : (seq + 1) * each] for seq in range(seqs)]
    weights, rows_ref, grads_ref, small_ref = refs[seqs * each :]

    def tn(a, b):
        return lax.dot_general(a, b, (((0,), (0,)), ((), ())), preferred_element_type=WIDE)

    query = key = value = out = small = extra = None

    def plus(a, b):
        return b if a is None else a + b

    for group in groups:
        normed = group[0:3]
        query_grad = group[3]
        pair_grads = group[4:7]
        cot, mixed, tall = group[7:10]
        extra = plus(extra, group[10][...])
        for place in range(3):
            flipped = normed[place][0].T
            key = plus(key, nn(flipped, pair_grads[place][0]))
            value = plus(value, nn(flipped, pair_grads[place][1]))
            if place == 2:
                query = plus(query, nn(flipped, query_grad[...]))
        out = plus(out, nn(cot[...].T, mixed[...]))
    norm = None
    for place, grad in enumerate((query, key, value)):
        grads_ref[place] = grad.astype(HALF)
        norm = plus(norm, jnp.sum(grad * weights[place].astype(WIDE), axis=-1, keepdims=True))
    grads_ref[3] = out.astype(HALF)
    gain = rows_ref[14:15, :].astype(WIDE)
    deep = norm.shape[0]
    norm_row = jnp.broadcast_to(norm, (deep, PAIR)).T[0:1, :] / gain
    lower = jnp.concatenate([extra[0:2], norm_row, extra[3:4]], axis=0)
    small_ref[0:8, :] = jnp.zeros((8, deep), WIDE)
    small_ref[8:16, :] = jnp.concatenate([jnp.zeros((4, deep), WIDE), lower], axis=0)


def relay_kernel(flag, far, near, out):
    out[...] = (
        far[...].astype(WIDE) + jnp.where(flag[0] == 1, near[...].astype(WIDE), 0.0)
    ).astype(HALF)


def input_kernel(query_grad, grad0, near, far, flag, weights, out_ref):
    keep = flag[0] == 0
    totals = []
    for kind in range(2):
        total = grad0[kind].astype(WIDE) + far[kind].astype(WIDE)
        total = total + jnp.where(keep, near[kind].astype(WIDE), 0.0)
        totals.append(total.astype(HALF))
    out_ref[...] = (
        nt(query_grad[...], weights[0]) + nt(totals[0], weights[1]) + nt(totals[1], weights[2])
    ).astype(HALF)


def layer_kernel(seqs, *refs):
    step = pl.program_id(0)
    for seq in range(seqs):
        base, own, other = refs[seq * 3 : seq * 3 + 3]

        @pl.when(step == seq)
        def _():
            summed = own[...].astype(WIDE) + other[...].astype(WIDE)
            refs[-1][0] = (base[...] + summed).astype(HALF)


def final_kernel(seqs, *refs):
    x_ref, rows_ref = refs[:2]
    step = pl.program_id(0)
    for seq in range(seqs):
        residual_grad, own, other = refs[2 + seq * 3 : 5 + seq * 3]

        @pl.when(step == seq)
        def _():
            tensor = x_ref[0].astype(WIDE)
            spread = spread_of(tensor)
            unit = tensor * spread
            gradient = own[...].astype(WIDE) + other[...].astype(WIDE)
            scaled = gradient * rows_ref[14:15, :].astype(WIDE)
            refs[-1][0] = residual_grad[...] + spread * (
                scaled - unit * jnp.mean(scaled * unit, axis=-1, keepdims=True)
            )


def cast_kernel(order, *refs):
    for kind in range(3):
        refs[-1][kind] = refs[kind][...].astype(HALF)


def order_kernel(index, *refs):
    parts, out = refs[:-1], refs[-1]
    size = len(parts)
    for distance, part in enumerate(parts):
        out[lax.rem(index[0] + size - distance, size)] = part[...]


def join_kernel(flag, own, other, out):
    half = own.shape[2]
    for place in range(own.shape[0]):
        first, second = own[place, 0], other[place, 0]
        start = place * 2 * half
        out[0, start : start + half, :] = jnp.where(flag[0] == 0, first, second)
        out[0, start + half : start + 2 * half, :] = jnp.where(flag[0] == 0, second, first)


def place_kernel(order, *refs):
    outs = refs[-3:]
    part = refs[0].shape[-1]
    for expert in range(2):
        own, near = refs[2 * expert : 2 * expert + 2]
        for place, block in ((3, own.at[1]), (2, own.at[0]), (1, near.at[1]), (0, near.at[0])):
            lanes = pl.ds(pl.multiple_of(order[place] * part, part), part)
            for kind in range(3):
                outs[kind][expert, :, lanes] = block[kind].astype(WIDE)


def swap(block, axis):
    size = lax.axis_size(axis)
    return lax.ppermute(block, axis, [(i, i ^ 1) for i in range(size)])


def shift(block, axis, distance):
    size = lax.axis_size(axis)
    route = [(i, i + distance) for i in range(size) if 0 <= i + distance < size]
    return lax.ppermute(block, axis, route)


def pick(stack, index, axis=0):
    return lax.dynamic_index_in_dim(stack, index, axis, keepdims=False)


def scatter_rows(tensor, dimension):
    return lax.psum_scatter(tensor, "fsdp", scatter_dimension=dimension, tiled=True)


def ring(block, distance):
    size = lax.axis_size("fsdp")
    return lax.ppermute(block, "fsdp", [(i, (i + distance) % size) for i in range(size)])


def gather_blocks(block):
    size = lax.axis_size("fsdp")
    if size > 4:
        return lax.all_gather(block, "fsdp", axis=0)
    blocks = [block] + [ring(block, distance) for distance in range(1, size)]
    if block.ndim == 3:
        parts = whole(block.shape)
        out = (size,) + block.shape
        index = lax.axis_index("fsdp").reshape(1).astype(jnp.int32)
        return call(
            order_kernel,
            (1,),
            [parts] * size,
            [(whole(out), struct(out, HALF))],
            prefetch=1,
        )(index, *blocks)[0]
    stacked = jnp.stack(blocks[::-1] * 2)
    return lax.dynamic_slice_in_dim(stacked, size - 1 - lax.axis_index("fsdp"), size, axis=0)


def scatter_blocks(blocks):
    size = lax.axis_size("fsdp")
    if size > 4:
        return lax.psum_scatter(blocks, "fsdp", scatter_dimension=0)
    index = lax.axis_index("fsdp")
    total = pick(blocks, index).astype(WIDE)
    for distance in range(1, size):
        sent = pick(blocks, lax.rem(index + distance, size))
        total = total + ring(sent, distance).astype(WIDE)
    return total.astype(blocks.dtype)


def shards(
    block_in,
    cotangent,
    prev_logits,
    routes,
    segments,
    w_query,
    w_key,
    w_value,
    w_out,
    w_gate,
    w_up,
    w_down,
    router,
    const_proj,
    const_vec,
    norm_attn,
    norm_moe,
):
    seqs, count = block_in.shape[:2]
    width = w_query.shape[1]
    pairs = width // PAIR
    deep = w_gate.shape[1]
    hidden = w_gate.shape[2]
    hi, lo = lax.axis_index("hi"), lax.axis_index("lo")
    hi_size = lax.axis_size("hi")
    ctx = hi * 2 + lo
    ctx_size = hi_size * 2
    fsdp_size = lax.axis_size("fsdp")
    part = hidden // ctx_size
    order = jnp.stack([(1 - hi) * 2 + 1 - lo, hi * 2 + 1 - lo, (1 - hi) * 2 + lo, ctx]).astype(
        jnp.int32
    )

    flag = lo.reshape(1).astype(jnp.int32)

    def join_matrices(own):
        other = swap(own, "lo")
        size, kinds, half = own.shape[:3]
        if half % 16 == 0:
            block = pl.BlockSpec((size, 1, half, width), lambda kind: (0, kind, 0, 0))
            return call(
                join_kernel,
                (kinds,),
                [pl.BlockSpec(memory_space=pltpu.SMEM), block, block],
                [
                    (
                        pl.BlockSpec((1, D, width), lambda kind: (kind, 0, 0)),
                        struct((kinds, D, width), HALF),
                    )
                ],
            )(flag, own, other)[0]
        halves = jnp.stack([jnp.where(lo == 0, own, other), jnp.where(lo == 0, other, own)], axis=2)
        return halves.transpose(1, 0, 2, 3, 4).reshape(kinds, D, width)

    half = deep // 2
    matrix_own = jnp.stack(
        [
            lax.dynamic_slice_in_dim(w, lo * half, half, axis=0).astype(HALF)
            for w in (w_query, w_key, w_value, w_out)
        ]
    )

    expert_own = call(
        cast_kernel,
        (EXPERTS,),
        [pl.BlockSpec((1, deep, part), lambda e, o: (e, 0, o[3]))] * 3,
        [
            (
                pl.BlockSpec((3, 1, deep, part), lambda e, o: (0, e, 0, 0)),
                struct((3, EXPERTS, deep, part), HALF),
            )
        ],
        prefetch=1,
    )(order, w_gate, w_up, w_down)[0]

    tp = lax.axis_index("tp")
    parts = []
    for place in range(2):
        rows = slice(place * (count // 2), (place + 1) * (count // 2))
        parts.append(shift(pick(block_in, tp)[rows], "hi", 1))
    matrix_own = gather_blocks(matrix_own)
    matrix_own, expert_own, parts = lax.optimization_barrier((matrix_own, expert_own, parts))
    expert_weights = lax.all_gather(expert_own, CTX + ("fsdp",), axis=0).reshape(
        ctx_size, fsdp_size, 3, EXPERTS, deep, part
    )
    if deep % 16:
        expert_weights = expert_weights.transpose(0, 2, 3, 1, 4, 5).reshape(
            ctx_size, 1, 3, EXPERTS, D, part
        )
    matrices = join_matrices(matrix_own)
    own_rows = jnp.concatenate(parts, axis=0)
    other_rows = jnp.concatenate([swap(rows, "tp") for rows in parts], axis=0)
    far_rows = jnp.stack(
        [jnp.where(tp == 0, own_rows, other_rows), jnp.where(tp == 0, other_rows, own_rows)]
    )
    near_rows = swap(jnp.where(lo == 1, far_rows, block_in), "lo")
    far_ids = shift(segments, "hi", 1)
    near_ids = swap(jnp.where(lo == 1, far_ids, segments), "lo")
    far_ids = jnp.where(hi == 0, -1, far_ids)
    near_ids = jnp.where(ctx == 0, -1, near_ids)
    key_ids = jnp.concatenate([far_ids, near_ids, segments], axis=1)[:, None, :]
    query_ids = segments[:, :, None]

    small_rows = jnp.concatenate(
        [router.T, const_proj.T, const_vec.T, norm_attn[None, :], norm_moe[None, :]], axis=0
    ).astype(HALF)
    small_rows = gather_blocks(small_rows).transpose(1, 0, 2).reshape(SMALL, D)

    positions = (ctx - 2) * count + jnp.arange(3 * count, dtype=jnp.int32)
    lane = jnp.arange(PAIR, dtype=jnp.int32)
    frequency = 10000.0 ** (-2.0 * (lane % (HD // 2)).astype(WIDE) / HD)
    turned = positions.astype(WIDE)[:, None] * frequency[None, :]
    cosine = jnp.cos(turned).reshape(3, count, PAIR)
    sine = (jnp.sin(turned) * jnp.where((lane & (HD // 2)) == 0, -1.0, 1.0)).reshape(3, count, PAIR)

    rank_rows, rank_columns = call(
        rank_kernel,
        (seqs,),
        [
            pl.BlockSpec((1, 2, count), lambda s: (s, 0, 0)),
            pl.BlockSpec((1, count, 2), lambda s: (s, 0, 0)),
        ],
        [
            (pl.BlockSpec((1, ALL, count), lambda s: (s, 0, 0)), struct((seqs, ALL, count), WIDE)),
            (pl.BlockSpec((1, count, ALL), lambda s: (s, 0, 0)), struct((seqs, count, ALL), WIDE)),
        ],
    )(routes.transpose(0, 2, 1), routes)

    def project(rows, place, with_query, after=()):
        spread = struct((seqs, count, width), HALF)
        by_seq = pl.BlockSpec((1, count, width), lambda s: (s, 0, 0))
        by_row = pl.BlockSpec((1, count, D), lambda s: (s, 0, 0))
        kinds = 3 if with_query else 2
        return call(
            functools.partial(project_kernel, with_query),
            (seqs,),
            [
                by_row,
                whole((SMALL, D)),
                fixed((1, count, PAIR), (place, 0, 0)),
                fixed((1, count, PAIR), (place, 0, 0)),
                whole((3, D, width)),
            ],
            [(by_row, struct((seqs, count, D), HALF))] + [(by_seq, spread)] * kinds,
            after=after,
        )(rows, small_rows, cosine, sine, matrices)

    normed0, key0, value0, query = project(block_in, 2, True, (near_rows,))
    normed1, key1, value1 = project(near_rows, 1, False)
    normed2, key2, value2 = project(far_rows, 0, False)

    def pair_block(seq):
        return pl.BlockSpec((1, count, PAIR), lambda p, seq=seq: (seq, 0, p))

    flat_pair = pl.BlockSpec((count, PAIR), lambda p: (0, p))
    window_scratch = [
        pltpu.VMEM((2, TILE, 4 * TILE), WIDE),
        pltpu.VMEM((3 * count, PAIR), HALF),
        pltpu.VMEM((3 * count, PAIR), HALF),
    ]
    product = 2 * 2 * TILE * 5 * TILE * 256 * 2 * pairs

    def attend(seq):
        return call(
            attend_kernel,
            (pairs,),
            [pair_block(seq)] * 7
            + [
                fixed((1, count, 1), (seq, 0, 0)),
                fixed((1, 1, 3 * count), (seq, 0, 0)),
                pl.BlockSpec((1, D, PAIR), lambda p: (3, 0, p)),
            ],
            [
                (flat_pair, struct((count, width), HALF)),
                (flat_pair, struct((count, width), WIDE)),
                (whole((count, D)), struct((count, D), HALF)),
            ],
            window_scratch + [pltpu.VMEM((count, D), WIDE)],
        )(query, key2, key1, key0, value2, value1, value0, query_ids, key_ids, matrices)

    mixed, logs, attended, attended_other = [], [], [], []
    for seq in range(seqs):
        one, two, three = attend(seq)
        mixed.append(one)
        logs.append(two)
        attended.append(three)
        attended_other.append(swap(three, "tp"))

    flat = whole((count, D))
    flat_small = whole((count, ALL))

    def one_seq(seq, columns):
        return fixed((1, count, columns), (seq, 0, 0))

    routed, targets, scores = [], [], []
    for seq in range(seqs):
        one, two, three = call(
            route_kernel,
            (1,),
            [one_seq(seq, D), flat, flat, whole((SMALL, D)), one_seq(seq, 2), one_seq(seq, ALL)],
            [
                (flat, struct((count, D), HALF)),
                (flat_small, struct((count, ALL), WIDE)),
                (whole((count, SMALL)), struct((count, SMALL), WIDE)),
            ],
        )(block_in, attended[seq], attended_other[seq], small_rows, routes, prev_logits)
        routed.append(one)
        targets.append(two)
        scores.append(three)

    slots = seqs * MOST
    weight_shape = expert_weights.shape
    weight_block = (1,) + weight_shape[1:2] + (3, 1) + weight_shape[4:]
    piece = (1, 3, D, part)
    out_slots, grad_slots, held, crossing = [], [], [], []
    scattered = [None] * EXPERTS

    def finish(expert, total):
        scattered[expert] = scatter_rows(total, total.ndim - 2)

    for expert in range(EXPERTS):
        theirs, mine, one, two, *totals = call(
            functools.partial(expert_kernel, expert),
            (ctx_size,),
            [
                flat,
                flat,
                whole((seqs, count, D)),
                flat_small,
                flat_small,
                whole((seqs, ALL, count)),
                pl.BlockSpec(
                    weight_block, lambda j, o, expert=expert: (o[j], 0, 0, expert, 0, 0)
                ),
            ],
            [
                (
                    pl.BlockSpec(piece, lambda j, o: (jnp.minimum(j, 1), 0, 0, 0)),
                    struct((2, 3, D, part), HALF),
                ),
                (
                    pl.BlockSpec(piece, lambda j, o: (jnp.maximum(j - 2, 0), 0, 0, 0)),
                    struct((2, 3, D, part), HALF),
                ),
                (whole((slots, D)), struct((slots, D), HALF)),
                (whole((slots, D)), struct((slots, D), HALF)),
            ],
            [
                pltpu.VMEM((slots, D), HALF),
                pltpu.VMEM((D, slots), HALF),
                pltpu.VMEM((slots, D), HALF),
                pltpu.VMEM((D, slots), HALF),
                pltpu.VMEM((slots, D), WIDE),
                pltpu.VMEM((slots, D), WIDE),
            ],
            prefetch=1,
            side=[side_sum(ctx_size, held[expert - 2])] if expert >= 2 else (),
            after=out_slots[-1:],
        )(order, routed[0], routed[1], cotangent, targets[0], targets[1], rank_rows, expert_weights)
        out_slots.append(one)
        grad_slots.append(two)
        held.append((mine, swap(theirs, "lo")))
        if totals:
            finish(expert - 2, totals[0].reshape(2, 3, D, part))

    def couple_of(place):
        own = scattered[place]
        across = swap(own, "hi")
        return jnp.stack([across, own]) if place >= 2 else own + across[::-1]

    back, back_other, sums, sums_other = [], [], [], []
    tiles = 4
    tile = count // tiles

    def tile_rows(columns):
        return pl.BlockSpec((tile, columns), lambda t: (t, 0))

    def tile_seq(seq, columns):
        return pl.BlockSpec((1, tile, columns), lambda t: (seq, t, 0))

    for seq in range(seqs):
        slot_block = fixed((MOST, D), (seq, 0))
        one, two, sent = call(
            combine_kernel,
            (tiles,),
            [slot_block] * (2 * EXPERTS)
            + [tile_seq(seq, ALL), tile_rows(ALL), tile_seq(seq, D)],
            [
                (tile_rows(D + PAIR), struct((count, D + PAIR), HALF)),
                (tile_rows(D), struct((count, D), HALF)),
            ],
            side=[side_sum(tiles, held[2 + seq], 0)],
        )(*out_slots, *grad_slots, rank_columns, targets[seq], cotangent)
        back.append(one)
        sums.append(two)
        back_other.append(swap(one, "tp"))
        crossing.append(swap(sent, "hi"))

    residual_grads, cots, mixed_grads, extras, bases, talls = [], [], [], [], [], []
    def turn(seq):
        results = call(
            turn_kernel,
            (tiles,),
            [
                tile_seq(seq, D),
                tile_rows(D),
                tile_rows(D),
                tile_seq(seq, D),
                tile_rows(D + PAIR),
                tile_rows(D + PAIR),
                tile_rows(ALL),
                tile_rows(SMALL),
                whole((SMALL, D)),
                fixed((1, D, width), (3, 0, 0)),
            ],
            [
                (tile_rows(D), struct((count, D), WIDE)),
                (tile_rows(D), struct((count, D), HALF)),
                (tile_rows(width), struct((count, width), HALF)),
                (whole((8, D)), struct((8, D), WIDE)),
                (tile_rows(D), struct((count, D), WIDE)),
                (tile_rows(PAIR), struct((count, PAIR), HALF)),
            ],
            side=[side_sum(tiles, held[3], 1, (crossing[1],))] if seq else (),
            after=(sums_other[0],) if seq else (),
        )(
            block_in,
            attended[seq],
            attended_other[seq],
            cotangent,
            back[seq],
            back_other[seq],
            targets[seq],
            scores[seq],
            small_rows,
            matrices,
        )
        for kept, result in zip(
            (residual_grads, cots, mixed_grads, extras, bases, talls), results[:6], strict=True
        ):
            kept.append(result)
        if seq:
            finish(3, results[6].reshape(3, D, part))

    query_grads, grads2, grads1, grads0 = [], [], [], []
    pair_out = (
        pl.BlockSpec((2, count, PAIR), lambda p: (0, 0, p)),
        struct((2, count, width), HALF),
    )
    table = whole((3, count, PAIR))
    near_grads, far_grads, sents = [], [], []

    def attend_back(seq):
        results = call(
            attend_back_kernel,
            (pairs,),
            [pair_block(seq)] * 7
            + [
                fixed((1, count, 1), (seq, 0, 0)),
                fixed((1, 1, 3 * count), (seq, 0, 0)),
                flat_pair,
                flat_pair,
                table,
                table,
            ],
            [(flat_pair, struct((count, width), HALF))] + [pair_out] * 3,
            window_scratch
            + [pltpu.VMEM((PAIR, 3 * count), WIDE), pltpu.VMEM((PAIR, 3 * count), WIDE)],
            after=(sents[0], couples[0]) if seq else (),
            side=() if seq else [side_sum(pairs, held[2], 1, (crossing[0],))],
        )(
            query,
            key2,
            key1,
            key0,
            value2,
            value1,
            value0,
            query_ids,
            key_ids,
            mixed_grads[seq],
            logs[seq],
            cosine,
            sine,
        )
        for kept, result in zip((query_grads, grads2, grads1, grads0), results[:4], strict=True):
            kept.append(result)
        if not seq:
            finish(2, results[4].reshape(3, D, part))
        near_grads.append(swap(results[2], "lo"))

    def send_back(seq, after):
        sents.append(
            call(
                relay_kernel,
                (2,),
                [pl.BlockSpec(memory_space=pltpu.SMEM)]
                + [pl.BlockSpec((1, count, width), lambda kind: (kind, 0, 0))] * 2,
                [
                    (
                        pl.BlockSpec((1, count, width), lambda kind: (kind, 0, 0)),
                        struct((2, count, width), HALF),
                    )
                ],
                after=after,
            )(flag, grads2[seq], near_grads[seq])[0]
        )
        far_grads.append(shift(sents[seq], "hi", -1))

    def enter(seq, after):
        one = call(
            input_kernel,
            (tiles // 2,),
            [
                pl.BlockSpec((2 * tile, width), lambda t: (t, 0)),
            ]
            + [pl.BlockSpec((2, 2 * tile, width), lambda t: (0, t, 0))] * 3
            + [
                pl.BlockSpec(memory_space=pltpu.SMEM),
                whole((3, D, width)),
            ],
            [
                (
                    pl.BlockSpec((2 * tile, D), lambda t: (t, 0)),
                    struct((count, D), HALF),
                )
            ],
            after=after,
        )(query_grads[seq], grads0[seq], near_grads[seq], far_grads[seq], flag, matrices)[0]
        input_parts.append(one)
        input_others.append(swap(one, "tp"))

    input_parts, input_others = [], []
    def send_sums(seq):
        sums[seq], mixed_grads[seq] = lax.optimization_barrier((sums[seq], mixed_grads[seq]))
        sums_other.append(swap(sums[seq], "tp"))

    turn(0)
    send_sums(0)
    attend_back(0)
    couples = [couple_of(0)]
    turn(1)
    send_sums(1)
    send_back(0, ())
    attend_back(1)
    enter(0, (query_grads[1], sums_other[1]))
    couples.append(couple_of(1))
    send_back(1, (input_parts[0], couples[1]))
    couples.append(couple_of(2))

    def half_map(seq):
        last = 1 if seq == 0 else 0
        return lambda s, t: (jnp.where(s == seq, t, last), 0)

    operands, specs = [], []
    columns = D // 3

    def by_column(rows, lead=()):
        zeros = (0,) * len(lead)
        return pl.BlockSpec(lead + (rows, columns), lambda t: zeros + (0, t))

    for seq in range(seqs):
        operands += [normed2, normed1, normed0, query_grads[seq], grads2[seq], grads1[seq], grads0[seq]]
        operands += [cots[seq], mixed[seq], talls[seq], extras[seq]]
        specs += [pl.BlockSpec((1, count, columns), lambda t, seq=seq: (seq, 0, t))] * 3
        specs += [whole((count, width))] + [whole((2, count, width))] * 3
        specs += [by_column(count), whole((count, width)), whole((count, PAIR)), by_column(8)]
    by_depth = pl.BlockSpec((3, columns, width), lambda t: (0, t, 0))
    attention_grads, small = call(
        functools.partial(weight_kernel, seqs),
        (3,),
        specs + [by_depth, by_column(SMALL)],
        [
            (
                pl.BlockSpec((4, columns, width), lambda t: (0, t, 0)),
                struct((4, D, width), HALF),
            ),
            (by_column(SMALL), struct((SMALL, D), WIDE)),
        ],
        after=(sents[1],),
    )(*operands, matrices, small_rows)
    tall_rows = sum(
        lax.dot_general(
            talls[seq][:, :SMALL], routed[seq], (((0,), (0,)), ((), ())), preferred_element_type=WIDE
        )
        for seq in range(seqs)
    )
    small = (small + tall_rows).astype(HALF)

    layer_out = call(
        functools.partial(layer_kernel, seqs),
        (seqs, 2),
        [
            pl.BlockSpec((2 * tile, D), half_map(seq))
            for seq in range(seqs)
            for _ in range(3)
        ],
        [
            (
                pl.BlockSpec((1, 2 * tile, D), lambda s, t: (s, t, 0)),
                struct((seqs, count, D), HALF),
            )
        ],
        after=(attention_grads,),
    )(*[array for seq in range(seqs) for array in (bases[seq], sums[seq], sums_other[seq])])[0]
    enter(1, (layer_out, couples[2], input_others[0], scattered[3]))
    attention_grads, small, input_parts[1] = lax.optimization_barrier(
        (attention_grads, small, input_parts[1])
    )
    input_others[1] = swap(input_parts[1], "tp")

    paired = attention_grads.reshape(2, 2, D, width)
    rest = small.reshape(-1, width)
    received = swap(
        jnp.concatenate([pick(paired, 1 - lo, 1).reshape(2 * D, width), rest], axis=0), "lo"
    )
    kept = pick(paired, lo, 1) + received[: 2 * D].reshape(2, D, width)
    rest = rest + received[2 * D :]
    crossed = swap(jnp.concatenate([pick(kept, 1 - hi), rest], axis=0), "hi")
    crossed, input_others[1], scattered[3] = lax.optimization_barrier(
        (crossed, input_others[1], scattered[3])
    )
    couples.append(couple_of(3))
    own = pick(kept, hi) + crossed[:D]
    rest = (rest + crossed[D:]).reshape(SMALL, fsdp_size, deep).transpose(1, 0, 2)
    own = jnp.concatenate(
        [own.reshape(fsdp_size, deep, width), rest.reshape(fsdp_size, -1, width)], axis=1
    )

    by_tile = pl.BlockSpec((1, tile, D), lambda s, t: (s, t, 0))
    operands, specs = [block_in, small_rows], [by_tile, whole((SMALL, D))]
    for seq in range(seqs):
        operands += [residual_grads[seq], input_parts[seq], input_others[seq]]
        last = tiles - 1 if seq == 0 else 0
        specs += [
            pl.BlockSpec(
                (tile, D), lambda s, t, seq=seq, last=last: (jnp.where(s == seq, t, last), 0)
            )
        ] * 3
    grad_input = call(
        functools.partial(final_kernel, seqs),
        (seqs, tiles),
        specs,
        [
            (by_tile, struct((seqs, count, D), WIDE)),
        ],
    )(*operands)[0]

    own, grad_input = lax.optimization_barrier((scatter_blocks(own), grad_input))
    small = own[deep:].reshape(SMALL, deep).astype(WIDE)
    norm_grad = small[14] + swap(small[14], "tp")
    own = own[:deep]
    across = swap(own, "hi")
    couple = jnp.stack([jnp.where(hi == 0, own, across), jnp.where(hi == 0, across, own)])
    other = swap(couple, "lo")
    wide_couple, wide_other = couple.astype(WIDE), other.astype(WIDE)
    lower = jnp.where(lo == 0, wide_couple, wide_other)
    higher = jnp.where(lo == 0, wide_other, wide_couple)

    result = struct((EXPERTS, deep, hidden), WIDE)
    grads = None
    for group in (couples[:2], couples[2:]):
        operands = [array for couple in group for array in (couple, swap(couple, "lo"))]
        previous = [] if grads is None else list(grads)
        grads = call(
            place_kernel,
            (1,),
            [whole(array.shape) for array in operands]
            + [pl.BlockSpec(memory_space=pl.ANY)] * len(previous),
            [(fixed((2, deep, hidden), (1 if previous else 0, 0, 0)), result)] * 3,
            prefetch=1,
            aliases={1 + len(operands) + kind: kind for kind in range(3)} if previous else None,
        )(order, *operands, *previous)

    return (
        layer_out,
        grad_input,
        lower[0],
        higher[0],
        lower[1],
        higher[1],
        *grads,
        small[0:8].T,
        small[8:12].T,
        small[12:14].T,
        norm_grad,
        small[15],
    )


def solution(mesh):
    sizes = mesh.shape
    inner = Mesh(
        mesh.devices.reshape(sizes["fsdp"], sizes["ctx"] // 2, 2, sizes["tp"]),
        ("fsdp", "hi", "lo", "tp"),
    )
    rows = P("fsdp", CTX, None)
    matrix = P("fsdp", "tp")
    experts = P(None, "fsdp", "tp")
    narrow = P("fsdp", None)
    vector = P("fsdp")
    return jax.shard_map(
        shards,
        mesh=inner,
        in_specs=(rows,) * 4
        + (P("fsdp", CTX),)
        + (matrix,) * 4
        + (experts,) * 3
        + (narrow,) * 3
        + (vector,) * 2,
        out_specs=(rows,) * 2
        + (matrix,) * 4
        + (experts,) * 3
        + (narrow,) * 3
        + (vector,) * 2,
        check_vma=False,
    )
```

```python
import functools

import jax
import jax.numpy as jnp
from jax import lax
from jax.experimental import pallas as pl
from jax.experimental.pallas import tpu as pltpu
from jax.sharding import Mesh
from jax.sharding import PartitionSpec as P

D = 768
HEADS = 12
HD = 64
EXPERTS = 4
ALL = 8
WINDOW = 1024
MOST = 192

EPSILON = 1e-06
MASKED = -1e30

CTX = ("hi", "lo")
HALF = jnp.bfloat16
WIDE = jnp.float32
TILE = 256
PAIR = 2 * HD
SMALL = 16
SIDE = 32
MIB = 1 << 20
COSTS = {
    "project": 10,
    "attend": 2,
    "route": 40,
    "expert0": 0,
    "expert1": 10,
    "expert2": 1,
    "expert3": 1,
    "combine0": 10,
    "combine1": 20,
    "turn0": 2,
    "turn1": 40,
    "back0": 10,
    "back1": 1,
    "relay0": 80,
    "relay1": 0,
    "input0": 5,
    "input1": 80,
    "weight": 20,
    "layer": 0,
    "fold": 40,
    "split": 5,
    "final": 20,
    "place0": 0,
    "place3": 5,
    "unpack": 2,
}


def nn(a, b):
    return jnp.dot(a, b, preferred_element_type=WIDE)


def nt(a, b):
    return lax.dot_general(a, b, (((1,), (1,)), ((), ())), preferred_element_type=WIDE)


def call(
    tag,
    body,
    grid,
    ins,
    outs,
    scratch=(),
    prefetch=0,
    aliases=None,
    after=(),
    side=(),
):
    operands = [array for job in side for array in job[0]]
    specs = [spec for job in side for spec in job[1]]
    kind = tag.rstrip("0123456789")
    own = prefetch + len(ins)
    first = own + len(operands) + len(after)

    def inner(*refs):
        start, results = own, first + len(outs)
        for place, job in enumerate(side):
            total = refs[start][...].astype(WIDE)
            for ref in refs[start + 1 : start + len(job[0])]:
                total = total + ref[...].astype(WIDE)
            refs[results + place][...] = total.astype(HALF)
            start += len(job[0])
        body(*refs[:own], *refs[first:results], *refs[results + len(side) :])

    all_outs = list(outs) + [job[2] for job in side]
    grid_spec = pltpu.PrefetchScalarGridSpec(
        num_scalar_prefetch=prefetch,
        grid=grid,
        in_specs=list(ins) + specs + [pl.BlockSpec(memory_space=pl.ANY)] * len(after),
        out_specs=[spec for spec, _ in all_outs],
        scratch_shapes=list(scratch),
    )
    kernel = pl.pallas_call(
        inner,
        grid_spec=grid_spec,
        name=tag,
        out_shape=[shape for _, shape in all_outs],
        input_output_aliases=aliases or {},
        compiler_params=pltpu.CompilerParams(
            dimension_semantics=("arbitrary",) * len(grid), vmem_limit_bytes=64 * MIB
        ),
        cost_estimate=pl.CostEstimate(
            flops=int(COSTS.get(tag, COSTS.get(kind, 2)) * 1e9), bytes_accessed=0, transcendentals=0
        ),
    )
    return lambda *arrays: kernel(*arrays, *operands, *after)


def side_sum(steps, stacks, index=None, plain=()):
    flat = [stack.reshape(-1, stack.shape[-1]) for stack in stacks]
    rows, columns = flat[0].shape
    rows = rows if index is None else rows // stacks[0].shape[0]
    start = 0 if index is None else index * steps
    block = (rows // steps, columns)
    out = pl.BlockSpec(block, lambda step, *_: (step, 0))
    specs = [pl.BlockSpec(block, lambda step, *_: (start + step, 0))] * len(flat)
    flat += [array.reshape(rows, columns) for array in plain]
    specs += [out] * len(plain)
    return flat, specs, (out, struct((rows, columns), HALF))


def whole(shape):
    zeros = (0,) * len(shape)
    return pl.BlockSpec(shape, lambda *_: zeros)


def fixed(block, place):
    return pl.BlockSpec(block, lambda *_: place)


def struct(shape, dtype):
    return jax.ShapeDtypeStruct(shape, dtype)


def spread_of(tensor):
    return lax.rsqrt(jnp.mean(tensor * tensor, axis=-1, keepdims=True) + EPSILON)


def partner(tensor):
    lane = lax.broadcasted_iota(jnp.int32, tensor.shape, 1)
    return jnp.where(
        (lane & (HD // 2)) == 0,
        pltpu.roll(tensor, PAIR - HD // 2, 1),
        pltpu.roll(tensor, HD // 2, 1),
    )


def rank_kernel(routes_t, routes, rank_rows, rank_columns):
    count = routes.shape[1]
    down = lax.broadcasted_iota(jnp.int32, (count, count), 0)
    across = lax.broadcasted_iota(jnp.int32, (count, count), 1)
    before = jnp.where(down < across, 1.0, 0.0).astype(HALF)
    after = jnp.where(across < down, 1.0, 0.0).astype(HALF)
    row_target = lax.broadcasted_iota(jnp.int32, (ALL, count), 0)
    names = (routes_t[0, 0:1, :] == row_target) | (routes_t[0, 1:2, :] == row_target)
    ranks = nn(jnp.where(names, 1.0, 0.0).astype(HALF), before)
    rank_rows[0] = jnp.where(names, ranks, -1.0)
    column_target = lax.broadcasted_iota(jnp.int32, (count, ALL), 1)
    named = (routes[0, :, 0:1] == column_target) | (routes[0, :, 1:2] == column_target)
    ranked = nn(after, jnp.where(named, 1.0, 0.0).astype(HALF))
    rank_columns[0] = jnp.where(named, ranked, -1.0)


def project_kernel(with_query, *refs):
    x_ref, rows_ref, cos_ref, sin_ref, weights = refs[:5]
    outs = refs[5:]
    tensor = x_ref[0].astype(WIDE)
    unit = tensor * spread_of(tensor)
    normed = (unit * rows_ref[14:15, :].astype(WIDE)).astype(HALF)
    outs[0][0] = normed
    cosine, sine = cos_ref[0], sin_ref[0]

    def turned(matrix, out, scale):
        flat = nn(normed, weights[matrix])
        for piece in range(flat.shape[1] // PAIR):
            lanes = slice(piece * PAIR, (piece + 1) * PAIR)
            part = flat[:, lanes]
            result = (part * cosine + partner(part) * sine).astype(HALF)
            out[0, :, lanes] = result if scale is None else result * scale

    turned(1, outs[1], None)
    outs[2][0] = nn(normed, weights[2]).astype(HALF)
    if with_query:
        turned(0, outs[3], jnp.asarray(HD ** (-0.5), HALF))


def fill_bias(query_ids, key_ids, bias):
    upper = upper_of()
    for tile in range(2):
        ids = query_ids[0, tile * TILE : (tile + 1) * TILE, :]
        first = key_ids[0, :, tile * TILE : (tile + 1) * TILE]
        last = key_ids[0, :, (tile + 4) * TILE : (tile + 5) * TILE]
        mixed = jnp.where(upper, first, last)
        bias[tile, :, :TILE] = jnp.where(mixed == ids, 0.0, MASKED)
        inner = key_ids[0, :, (tile + 1) * TILE : (tile + 4) * TILE]
        bias[tile, :, TILE:] = jnp.where(inner == ids, 0.0, MASKED)


def upper_of():
    down = lax.broadcasted_iota(jnp.int32, (TILE, TILE), 0)
    across = lax.broadcasted_iota(jnp.int32, (TILE, TILE), 1)
    return across > down


def head_lanes(head, rows):
    lane = lax.broadcasted_iota(jnp.int32, (rows, PAIR), 1)
    return (lane < HD) if head == 0 else (lane >= HD)


def folded(upper, spread):
    span = spread.shape[1]
    return (
        jnp.where(upper, spread[:, :TILE], spread[:, span - TILE :]),
        spread[:, TILE : span - TILE],
    )


def unfolded(upper, ends, middle):
    return jnp.concatenate(
        [jnp.where(upper, ends, 0.0), middle, jnp.where(upper, 0.0, ends)], axis=1
    ).astype(HALF)


def load_window(parts, window):
    rows = parts[0].shape[1]
    for place, part in enumerate(parts):
        window[place * rows : (place + 1) * rows, :] = part[0]


def attend_kernel(
    query, k2, k1, k0, v2, v1, v0, query_ids, key_ids, w_out, mixed, logs, attended, bias, keys, values, total
):
    step = pl.program_id(0)

    @pl.when(step == 0)
    def _():
        fill_bias(query_ids, key_ids, bias)

    load_window((k2, k1, k0), keys)
    load_window((v2, v1, v0), values)
    upper = upper_of()
    span = 5 * TILE
    for tile in range(2):
        rows = slice(tile * TILE, (tile + 1) * TILE)
        window = slice(tile * TILE, tile * TILE + span)
        results, totals = [], []
        for head in range(2):
            chosen = head_lanes(head, TILE)
            own = jnp.where(chosen, query[0, rows, :], jnp.zeros((), HALF))
            ends, middle = folded(upper, nt(own, keys[window, :]))
            ends = ends + bias[tile, :, :TILE]
            middle = middle + bias[tile, :, TILE:]
            highest = jnp.maximum(
                jnp.max(ends, axis=-1, keepdims=True), jnp.max(middle, axis=-1, keepdims=True)
            )
            ends = jnp.exp(ends - highest)
            middle = jnp.exp(middle - highest)
            summed = jnp.sum(ends, axis=-1, keepdims=True) + jnp.sum(middle, axis=-1, keepdims=True)
            out = nn(unfolded(upper, ends, middle), values[window, :]) / summed
            results.append(out)
            totals.append(jnp.broadcast_to(highest + jnp.log(summed), (TILE, PAIR)))
        chosen = head_lanes(0, TILE)
        mixed[rows, :] = jnp.where(chosen, results[0], results[1]).astype(HALF)
        logs[rows, :] = jnp.where(chosen, totals[0], totals[1])
    product = nt(mixed[...], w_out[0])

    @pl.when(step == 0)
    def _():
        total[...] = product

    @pl.when(step > 0)
    def _():
        total[...] += product

    @pl.when(step == pl.num_programs(0) - 1)
    def _():
        attended[...] = total[...].astype(HALF)


def residual_of(x_ref, own, other):
    return x_ref[0].astype(WIDE) + (own[...].astype(WIDE) + other[...].astype(WIDE))


def softmax_two(a, b):
    highest = jnp.maximum(a, b)
    a, b = jnp.exp(a - highest), jnp.exp(b - highest)
    return a / (a + b), b / (a + b)


def mix_back(mix, one, two):
    inner = mix[0] * one + mix[1] * two
    return mix[0] * (one - inner), mix[1] * (two - inner)


def put(total, columns, first):
    lane = lax.broadcasted_iota(jnp.int32, total.shape, 1)
    for place, column in enumerate(columns):
        total = total + jnp.where(lane == first + place, column, 0.0)
    return total


def route_kernel(
    x_ref, own, other, upstream, rows_ref, routes, prev, routed_ref, side_ref, base_ref, small_ref
):
    residual = residual_of(x_ref, own, other)
    unit = residual * spread_of(residual)
    routed = (unit * rows_ref[15:16, :].astype(WIDE)).astype(HALF)
    routed_ref[...] = routed
    routed_wide = routed.astype(WIDE)
    scores = nt(routed, rows_ref[...])
    logits = scores[:, :ALL] + prev[0]
    target = lax.broadcasted_iota(jnp.int32, logits.shape, 1)
    picked = [routes[0, :, place : place + 1] == target for place in range(2)]
    chosen = [jnp.sum(jnp.where(one, logits, 0.0), axis=-1, keepdims=True) for one in picked]
    chosen = softmax_two(*chosen)
    weights = jnp.where(picked[0], chosen[0], 0.0) + jnp.where(picked[1], chosen[1], 0.0)
    copy, one, two = (weights[:, place : place + 1] for place in (5, 6, 7))
    first = softmax_two(scores[:, 8:9], scores[:, 9:10])
    second = softmax_two(scores[:, 10:11], scores[:, 11:12])
    vector = [rows_ref[12 + place : 13 + place, :].astype(WIDE) for place in range(2)]
    direct = copy + one * first[0] + two * second[0]
    base_ref[...] = (
        residual + routed_wide * direct + (one * first[1]) * vector[0] + (two * second[1]) * vector[1]
    )
    up_half = upstream[0]
    up = up_half.astype(WIDE)
    dot = jnp.sum(up * routed_wide, axis=-1, keepdims=True)
    dots = nt(up_half, rows_ref[...])
    dot_one, dot_two = dots[:, 12:13], dots[:, 13:14]
    side = put(
        jnp.zeros(side_ref.shape, WIDE),
        (dot, first[0] * dot + first[1] * dot_one, second[0] * dot + second[1] * dot_two),
        ALL + EXPERTS + 1,
    )
    side = put(side, mix_back(first, one * dot, one * dot_one), 16)
    side = put(side, mix_back(second, two * dot, two * dot_two), 18)
    side = put(side, (direct,), 20)
    side_ref[...] = side
    side_ref[:, :ALL] = weights
    step = pl.program_id(0)
    sums = jnp.concatenate(
        [
            jnp.sum((one * first[1]) * up, axis=0, keepdims=True),
            jnp.sum((two * second[1]) * up, axis=0, keepdims=True),
            jnp.zeros((6, D), WIDE),
        ],
        axis=0,
    )

    @pl.when(step == 0)
    def _():
        small_ref[...] = sums

    @pl.when(step > 0)
    def _():
        small_ref[...] += sums


def expert_kernel(
    expert, order, routed_a, routed_b, upstream, targets_a, targets_b, ranks, weights, theirs, mine, out_slots,
    grad_slots, rows, rows_t, cots, cots_t, out_total, grad_total
):
    step = pl.program_id(0)
    count = routed_a.shape[0]

    @pl.when(step == 0)
    def _():
        slot = lax.broadcasted_iota(jnp.int32, (MOST, count), 0).astype(WIDE)
        for seq, (routed, targets) in enumerate(((routed_a, targets_a), (routed_b, targets_b))):
            place = slice(seq * MOST, (seq + 1) * MOST)
            spread = jnp.where(slot == ranks[seq, expert : expert + 1, :], 1.0, 0.0).astype(HALF)
            rows[place, :] = nn(spread, routed[...]).astype(HALF)
            weighted = targets[:, expert : expert + 1] * upstream[seq].astype(WIDE)
            cots[place, :] = nn(spread, weighted.astype(HALF)).astype(HALF)
        rows_t[...] = rows[...].T
        cots_t[...] = cots[...].T

    here = [weights[0, :, kind, 0].reshape(D, weights.shape[-1]) for kind in range(3)]
    gate = nn(rows[...], here[0])
    up = nn(rows[...], here[1])
    sigmoid = 1.0 / (1.0 + jnp.exp(-gate))
    silu = gate * sigmoid
    activated = (silu * up).astype(HALF)
    activated_grad = nn(cots[...], here[2])
    up_grad = (activated_grad * silu).astype(HALF)
    gate_grad = (activated_grad * up * sigmoid * (1.0 + gate * (1.0 - sigmoid))).astype(HALF)
    out_part = nt(activated, here[2])
    grad_part = nt(gate_grad, here[0]) + nt(up_grad, here[1])

    @pl.when(step == 0)
    def _():
        out_total[...] = out_part
        grad_total[...] = grad_part

    @pl.when(step > 0)
    def _():
        out_total[...] += out_part
        grad_total[...] += grad_part

    grads = (nn(rows_t[...], gate_grad), nn(rows_t[...], up_grad), nn(cots_t[...], activated))

    @pl.when(step < 2)
    def _():
        for kind in range(3):
            theirs[0, kind] = grads[kind].astype(HALF)

    @pl.when(step >= 2)
    def _():
        for kind in range(3):
            mine[0, kind] = grads[kind].astype(HALF)

    @pl.when(step == pl.num_programs(0) - 1)
    def _():
        out_slots[...] = out_total[...].astype(HALF)
        grad_slots[...] = grad_total[...].astype(HALF)


def combine_kernel(*refs):
    outs, grads = refs[:EXPERTS], refs[EXPERTS : 2 * EXPERTS]
    ranks, targets, upstream, back_ref, sum_ref = refs[2 * EXPERTS :]
    count = upstream.shape[1]
    slot = lax.broadcasted_iota(jnp.int32, (count, MOST), 1).astype(WIDE)
    wide = upstream[0].astype(WIDE)
    back = total = None
    lane = lax.broadcasted_iota(jnp.int32, (count, PAIR), 1)
    dots = jnp.zeros((count, PAIR), WIDE)
    for expert in range(EXPERTS):
        spread = jnp.where(slot == ranks[0, :, expert : expert + 1], 1.0, 0.0).astype(HALF)
        part = nn(spread, grads[expert][...])
        back = part if back is None else back + part
        part = nn(spread, outs[expert][...])
        dots = dots + jnp.where(lane == expert, jnp.sum(part * wide, axis=-1, keepdims=True), 0.0)
        part = part * targets[:, expert : expert + 1]
        total = part if total is None else total + part
    back_ref[:, :D] = back.astype(HALF)
    main = dots.astype(HALF)
    rest = pltpu.roll(dots - main.astype(WIDE), ALL, 1)
    back_ref[:, D:] = jnp.where(lane < ALL, main.astype(WIDE), rest).astype(HALF)
    sum_ref[...] = total.astype(HALF)


def turn_kernel(
    x_ref, own, other, upstream, back_own, back_other, side, rows_ref, w_out, residual_grad_ref, cot_ref,
    mixed_grad_ref, small_ref, tall_ref
):
    residual = residual_of(x_ref, own, other)
    spread = spread_of(residual)
    unit = residual * spread
    up = upstream[0].astype(WIDE)
    weights = side[:, :ALL]
    halves = back_own[:, D:].astype(WIDE) + back_other[:, D:].astype(WIDE)
    halves = halves[:, :ALL] + halves[:, ALL : 2 * ALL]
    lane = lax.broadcasted_iota(jnp.int32, halves.shape, 1)
    dots = jnp.where(lane < EXPERTS, halves, 0.0) + side[:, ALL : 2 * ALL]
    logit_grad = weights * (dots - jnp.sum(weights * dots, axis=-1, keepdims=True))
    rest = jnp.concatenate([side[:, 16:20], jnp.zeros((up.shape[0], 4), WIDE)], axis=1)
    tall = jnp.concatenate([logit_grad, rest], axis=1).astype(HALF)
    tall_ref[...] = jnp.concatenate(
        [tall, jnp.zeros((up.shape[0], PAIR - SMALL), HALF)], axis=1
    )
    back = back_own[:, :D].astype(WIDE) + back_other[:, :D].astype(WIDE)
    routed_grad = back + nn(tall, rows_ref[...]) + up * side[:, 20:21]
    step = pl.program_id(0)
    sums = jnp.sum(routed_grad * unit, axis=0, keepdims=True)
    sums = jnp.concatenate([jnp.zeros((3, D), WIDE), sums, jnp.zeros((4, D), WIDE)], axis=0)

    @pl.when(step == 0)
    def _():
        small_ref[...] = sums

    @pl.when(step > 0)
    def _():
        small_ref[...] += sums

    scaled = routed_grad * rows_ref[15:16, :].astype(WIDE)
    residual_grad = up + spread * (scaled - unit * jnp.mean(scaled * unit, axis=-1, keepdims=True))
    residual_grad_ref[...] = residual_grad
    cot = residual_grad.astype(HALF)
    cot_ref[...] = cot
    mixed_grad_ref[...] = nn(cot, w_out[0]).astype(HALF)


def attend_back_kernel(
    query, k2, k1, k0, v2, v1, v0, query_ids, key_ids, mixed_grad, logs, cos_ref, sin_ref, query_grad, grad2, grad1,
    grad0, bias, keys, values, key_total, value_total
):
    step = pl.program_id(0)

    @pl.when(step == 0)
    def _():
        fill_bias(query_ids, key_ids, bias)

    load_window((k2, k1, k0), keys)
    load_window((v2, v1, v0), values)
    upper = upper_of()
    span = 5 * TILE
    count = query.shape[1]

    def turned_back(gradient, place, rows):
        cosine, sine = cos_ref[place, rows, :], sin_ref[place, rows, :]
        return (gradient * cosine - partner(gradient) * sine).astype(HALF)

    key_total[...] = jnp.zeros_like(key_total)
    value_total[...] = jnp.zeros_like(value_total)
    for tile in range(2):
        rows = slice(tile * TILE, (tile + 1) * TILE)
        window = slice(tile * TILE, tile * TILE + span)
        results = []
        for head in range(2):
            chosen = head_lanes(head, TILE)
            nothing = jnp.zeros((), HALF)
            own = jnp.where(chosen, query[0, rows, :], nothing)
            out_grad = jnp.where(chosen, mixed_grad[rows, :], nothing)
            level = logs[rows, head * HD : head * HD + 1]
            ends, middle = folded(upper, nt(own, keys[window, :]))
            ends = jnp.exp(ends + bias[tile, :, :TILE] - level)
            middle = jnp.exp(middle + bias[tile, :, TILE:] - level)
            value_total[:, window] += nn(out_grad.T, unfolded(upper, ends, middle))
            ends_grad, middle_grad = folded(upper, nt(out_grad, values[window, :]))
            expected = jnp.sum(ends * ends_grad, axis=-1, keepdims=True) + jnp.sum(
                middle * middle_grad, axis=-1, keepdims=True
            )
            score_grad = unfolded(upper, ends * (ends_grad - expected), middle * (middle_grad - expected))
            key_total[:, window] += nn(own.T, score_grad)
            results.append(nn(score_grad, keys[window, :]))
        gradient = jnp.where(head_lanes(0, TILE), results[0], results[1]) * HD ** (-0.5)
        query_grad[rows, :] = turned_back(gradient, 2, rows)
    for place, grad in enumerate((grad2, grad1, grad0)):
        window = slice(place * count, (place + 1) * count)
        grad[0] = turned_back(key_total[:, window].T, place, slice(0, count))
        grad[1] = value_total[:, window].T.astype(HALF)


def weight_kernel(seqs, slots, *refs):
    each = 13
    groups = [refs[seq * each : (seq + 1) * each] for seq in range(seqs)]
    weights, rows_ref, theirs, mine = refs[seqs * each :]
    step = pl.program_id(0)
    query = key = value = out = small = None

    def plus(a, b):
        return b if a is None else a + b

    for group in groups:
        normed = group[0:3]
        query_grad = group[3]
        pair_grads = group[4:7]
        cot, mixed, tall, routed, extra, early = group[7:13]
        small = plus(small, nn(tall[...].T[:SMALL], routed[...]))
        lower = extra[0:4, :] + early[0:4, :]
        small = small + jnp.concatenate([jnp.zeros((SMALL - 4, lower.shape[1]), WIDE), lower], axis=0)
        for place in range(3):
            flipped = normed[place][0].T
            key = plus(key, nn(flipped, pair_grads[place][0]))
            value = plus(value, nn(flipped, pair_grads[place][1]))
            if place == 2:
                query = plus(query, nn(flipped, query_grad[...]))
        out = plus(out, nn(cot[...].T, mixed[...]))
    norm = None
    deep = out.shape[0]
    rows = pl.ds(pl.multiple_of(step * deep, deep), deep)
    for place, grad in enumerate((query, key, value, out)):
        if place < 3:
            norm = plus(norm, jnp.sum(grad * weights[place].astype(WIDE), axis=-1, keepdims=True))
        half = grad.astype(HALF)
        slot = slots[place]

        @pl.when(slot < 2)
        def _():
            theirs[jnp.minimum(slot, 1), rows, :] = half

        @pl.when(slot >= 2)
        def _():
            mine[jnp.maximum(slot - 2, 0), rows, :] = half

    gain = rows_ref[14:15, :].astype(WIDE)
    norm_row = jnp.broadcast_to(norm, (deep, PAIR)).T[0:1, :] / gain
    row = lax.broadcasted_iota(jnp.int32, small.shape, 0)
    small = jnp.where(row == 14, norm_row, small).astype(HALF)
    theirs[step, D : D + SMALL, :] = small
    mine[step, D : D + SMALL, :] = small


def fold_kernel(mine, received, sent, kept):
    for place, out in ((0, sent), (1, kept)):
        out[:D, :] = (mine[place, :D].astype(WIDE) + received[place, :D].astype(WIDE)).astype(HALF)
        for half in range(2):
            small = mine[half, D:].astype(WIDE) + received[half, D:].astype(WIDE)
            out[D + half * SMALL : D + (half + 1) * SMALL, :] = small.astype(HALF)


def split_kernel(index, kept, received, *outs):
    size = len(outs)
    deep = D // size
    width = kept.shape[1]

    def total(rows):
        return (kept[rows, :].astype(WIDE) + received[rows, :].astype(WIDE)).astype(HALF)

    small = jnp.concatenate(
        [total(slice(D + half * SMALL, D + (half + 1) * SMALL)) for half in range(2)], axis=1
    )
    for distance, out in enumerate(outs):
        place = lax.rem(index[0] + distance, size)
        out[:deep, :] = total(pl.ds(pl.multiple_of(place * deep, deep), deep))
        part = small[:, :deep]
        for other in range(1, size):
            part = jnp.where(place == other, small[:, other * deep : (other + 1) * deep], part)
        out[deep:, :] = jnp.concatenate([part, jnp.zeros((SMALL, width - deep), HALF)], axis=1)


def relay_kernel(flag, far, near, out):
    out[...] = (
        far[...].astype(WIDE) + jnp.where(flag[0] == 1, near[...].astype(WIDE), 0.0)
    ).astype(HALF)


def input_kernel(query_grad, grad0, near, far, flag, weights, out_ref):
    keep = flag[0] == 0
    totals = []
    for kind in range(2):
        total = grad0[kind].astype(WIDE) + far[kind].astype(WIDE)
        total = total + jnp.where(keep, near[kind].astype(WIDE), 0.0)
        totals.append(total.astype(HALF))
    out_ref[...] = (
        nt(query_grad[...], weights[0]) + nt(totals[0], weights[1]) + nt(totals[1], weights[2])
    ).astype(HALF)


def layer_kernel(seqs, *refs):
    step = pl.program_id(0)
    for seq in range(seqs):
        base, own, other = refs[seq * 3 : seq * 3 + 3]

        @pl.when(step == seq)
        def _():
            summed = own[...].astype(WIDE) + other[...].astype(WIDE)
            refs[-1][0] = (base[...] + summed).astype(HALF)


def final_kernel(seqs, *refs):
    x_ref, rows_ref = refs[:2]
    step = pl.program_id(0)
    for seq in range(seqs):
        residual_grad, own, other = refs[2 + seq * 3 : 5 + seq * 3]

        @pl.when(step == seq)
        def _():
            tensor = x_ref[0].astype(WIDE)
            spread = spread_of(tensor)
            unit = tensor * spread
            gradient = own[...].astype(WIDE) + other[...].astype(WIDE)
            scaled = gradient * rows_ref[14:15, :].astype(WIDE)
            refs[-1][0] = residual_grad[...] + spread * (
                scaled - unit * jnp.mean(scaled * unit, axis=-1, keepdims=True)
            )


def pack_kernel(flag, query, key, value, out, *refs):
    packed = refs[-1]
    deep, width = query.shape
    half = deep // 2
    start = pl.multiple_of(flag[0] * half, half)
    for place, matrix in enumerate((query, key, value, out)):
        packed[place * half : (place + 1) * half, :] = matrix[pl.ds(start, half), :].astype(HALF)
    rows = jnp.concatenate([ref[...] for ref in refs[:-1]], axis=0)
    rows = jnp.concatenate([rows, jnp.zeros((SMALL, width - deep), WIDE)], axis=1)
    packed[4 * half :, :] = rows.astype(HALF)


def cast_kernel(order, *refs):
    for kind in range(3):
        refs[-1][kind] = refs[kind][...].astype(HALF)


def order_kernel(index, *refs):
    parts, out = refs[:-1], refs[-1]
    size = len(parts)
    for distance, part in enumerate(parts):
        out[lax.rem(index[0] + size - distance, size)] = part[...]


def join_kernel(flag, own, other, out):
    half = own.shape[1]
    for place in range(own.shape[0]):
        first, second = own[place], other[place]
        start = place * 2 * half
        out[0, start : start + half, :] = jnp.where(flag[0] == 0, first, second)
        out[0, start + half : start + 2 * half, :] = jnp.where(flag[0] == 0, second, first)


def place_kernel(order, *refs):
    outs = refs[-3:]
    part = refs[0].shape[-1]
    for expert in range(2):
        for core, (own, across) in enumerate(
            (refs[4 * expert : 4 * expert + 2], refs[4 * expert + 2 : 4 * expert + 4])
        ):
            for far in range(2):
                lanes = pl.ds(pl.multiple_of(order[3 - far - 2 * core] * part, part), part)
                for kind in range(3):
                    if len(own.shape) == 4:
                        block = own[1 - far, kind].astype(WIDE) + across[far, kind].astype(WIDE)
                    else:
                        block = (across if far else own)[kind].astype(WIDE)
                    outs[kind][expert, :, lanes] = block


def unpack_kernel(slots, own, across, near, far, *outs):
    for place, out in enumerate(outs):
        block = jnp.where(slots[place] == 3, own[...].astype(WIDE), across[...].astype(WIDE))
        block = jnp.where(slots[place] == 1, near[...].astype(WIDE), block)
        block = jnp.where(slots[place] == 0, far[...].astype(WIDE), block)
        out[...] = block[: out.shape[0]]


def swap(block, axis):
    size = lax.axis_size(axis)
    return lax.ppermute(block, axis, [(i, i ^ 1) for i in range(size)])


def shift(block, axis, distance):
    size = lax.axis_size(axis)
    route = [(i, i + distance) for i in range(size) if 0 <= i + distance < size]
    return lax.ppermute(block, axis, route)


def pick(stack, index, axis=0):
    return lax.dynamic_index_in_dim(stack, index, axis, keepdims=False)


def scatter_rows(tensor, dimension):
    return lax.psum_scatter(tensor, "fsdp", scatter_dimension=dimension, tiled=True)


def ring(block, distance):
    size = lax.axis_size("fsdp")
    return lax.ppermute(block, "fsdp", [(i, (i + distance) % size) for i in range(size)])


def gather_blocks(block):
    size = lax.axis_size("fsdp")
    if size > 4:
        return lax.all_gather(block, "fsdp", axis=0)
    blocks = [block] + [ring(block, distance) for distance in range(1, size)]
    if block.shape[0] % 16 == 0:
        parts = whole(block.shape)
        out = (size,) + block.shape
        index = lax.axis_index("fsdp").reshape(1).astype(jnp.int32)
        return call(
            "order",
            order_kernel,
            (1,),
            [parts] * size,
            [(whole(out), struct(out, HALF))],
            prefetch=1,
        )(index, *blocks)[0]
    stacked = jnp.stack(blocks[::-1] * 2)
    start = size - 1 - lax.axis_index("fsdp")
    return lax.dynamic_slice_in_dim(stacked, start, size, axis=0)


def scatter_blocks(blocks):
    size = lax.axis_size("fsdp")
    if size > 4:
        return lax.psum_scatter(blocks, "fsdp", scatter_dimension=0)
    index = lax.axis_index("fsdp")
    total = pick(blocks, index).astype(WIDE)
    for distance in range(1, size):
        sent = pick(blocks, lax.rem(index + distance, size))
        total = total + ring(sent, distance).astype(WIDE)
    return total.astype(blocks.dtype)


def shards(
    block_in,
    cotangent,
    prev_logits,
    routes,
    segments,
    w_query,
    w_key,
    w_value,
    w_out,
    w_gate,
    w_up,
    w_down,
    router,
    const_proj,
    const_vec,
    norm_attn,
    norm_moe,
):
    seqs, count = block_in.shape[:2]
    width = w_query.shape[1]
    pairs = width // PAIR
    deep = w_gate.shape[1]
    hidden = w_gate.shape[2]
    hi, lo = lax.axis_index("hi"), lax.axis_index("lo")
    hi_size = lax.axis_size("hi")
    ctx = hi * 2 + lo
    ctx_size = hi_size * 2
    fsdp_size = lax.axis_size("fsdp")
    part = hidden // ctx_size
    order = jnp.stack([(1 - hi) * 2 + 1 - lo, hi * 2 + 1 - lo, (1 - hi) * 2 + lo, ctx]).astype(
        jnp.int32
    )

    flag = lo.reshape(1).astype(jnp.int32)

    positions = (ctx - 2) * count + jnp.arange(3 * count, dtype=jnp.int32)
    lane = jnp.arange(PAIR, dtype=jnp.int32)
    frequency = 10000.0 ** (-2.0 * (lane % (HD // 2)).astype(WIDE) / HD)
    turned = positions.astype(WIDE)[:, None] * frequency[None, :]
    cosine = jnp.cos(turned).reshape(3, count, PAIR)
    sine = (jnp.sin(turned) * jnp.where((lane & (HD // 2)) == 0, -1.0, 1.0)).reshape(3, count, PAIR)

    rank_rows, rank_columns = call(
        "rank",
        rank_kernel,
        (seqs,),
        [
            pl.BlockSpec((1, 2, count), lambda s: (s, 0, 0)),
            pl.BlockSpec((1, count, 2), lambda s: (s, 0, 0)),
        ],
        [
            (pl.BlockSpec((1, ALL, count), lambda s: (s, 0, 0)), struct((seqs, ALL, count), WIDE)),
            (pl.BlockSpec((1, count, ALL), lambda s: (s, 0, 0)), struct((seqs, count, ALL), WIDE)),
        ],
    )(routes.transpose(0, 2, 1), routes)

    half = deep // 2
    rows = 4 * half + SMALL
    rows = rows + -rows % 16
    narrow = (router.T, const_proj.T, const_vec.T, norm_attn[None, :], norm_moe[None, :])
    if half % 16 == 0:
        operands = (w_query, w_key, w_value, w_out) + narrow
        matrix_own = call(
            "pack",
            pack_kernel,
            (1,),
            [pl.BlockSpec(memory_space=pltpu.SMEM)] + [whole(array.shape) for array in operands],
            [(whole((rows, width)), struct((rows, width), HALF))],
        )(flag, *operands)[0]
    else:
        matrix_own = [
            lax.dynamic_slice_in_dim(w, lo * half, half, axis=0)
            for w in (w_query, w_key, w_value, w_out)
        ]
        small_rows = jnp.concatenate(narrow, axis=0)
        small_rows = jnp.pad(small_rows, ((0, rows - 4 * half - SMALL), (0, width - deep)))
        matrix_own = jnp.concatenate(matrix_own + [small_rows], axis=0).astype(HALF)

    def join_matrices(own):
        other = swap(own, "lo")
        if half % 16 == 0:
            block = pl.BlockSpec((fsdp_size, half, width), lambda kind: (0, kind, 0))
            return call(
                "join",
                join_kernel,
                (4,),
                [pl.BlockSpec(memory_space=pltpu.SMEM), block, block],
                [
                    (
                        pl.BlockSpec((1, D, width), lambda kind: (kind, 0, 0)),
                        struct((4, D, width), HALF),
                    )
                ],
            )(flag, own, other)[0]
        halves = [
            blocks[:, : 4 * half].reshape(fsdp_size, 4, half, width) for blocks in (own, other)
        ]
        halves = jnp.stack(
            [jnp.where(lo == 0, *halves), jnp.where(lo == 0, *halves[::-1])], axis=2
        )
        return halves.transpose(1, 0, 2, 3, 4).reshape(4, D, width)

    expert_own = call(
        "cast",
        cast_kernel,
        (EXPERTS,),
        [pl.BlockSpec((1, deep, part), lambda e, o: (e, 0, o[3]))] * 3,
        [
            (
                pl.BlockSpec((3, 1, deep, part), lambda e, o: (0, e, 0, 0)),
                struct((3, EXPERTS, deep, part), HALF),
            )
        ],
        prefetch=1,
    )(order, w_gate, w_up, w_down)[0]

    far_rows = shift(block_in, "hi", 1)
    matrix_own = gather_blocks(matrix_own)
    matrix_own, expert_own, far_rows, cosine, sine, rank_rows, rank_columns = lax.optimization_barrier(
        (matrix_own, expert_own, far_rows, cosine, sine, rank_rows, rank_columns)
    )
    expert_weights = lax.all_gather(expert_own, CTX + ("fsdp",), axis=0).reshape(
        ctx_size, fsdp_size, 3, EXPERTS, deep, part
    )
    if deep % 16:
        expert_weights = expert_weights.transpose(0, 2, 3, 1, 4, 5).reshape(
            ctx_size, 1, 3, EXPERTS, D, part
        )
    matrices = join_matrices(matrix_own)
    small_rows = matrix_own[:, 4 * half : 4 * half + SMALL, :deep]
    small_rows = small_rows.transpose(1, 0, 2).reshape(SMALL, D)
    near_rows = swap(jnp.where(lo == 1, far_rows, block_in), "lo")
    far_ids = shift(segments, "hi", 1)
    near_ids = swap(jnp.where(lo == 1, far_ids, segments), "lo")
    far_ids = jnp.where(hi == 0, -1, far_ids)
    near_ids = jnp.where(ctx == 0, -1, near_ids)
    key_ids = jnp.concatenate([far_ids, near_ids, segments], axis=1)[:, None, :]
    query_ids = segments[:, :, None]

    def project(rows, place, with_query, after=()):
        spread = struct((seqs, count, width), HALF)
        by_seq = pl.BlockSpec((1, count, width), lambda s: (s, 0, 0))
        by_row = pl.BlockSpec((1, count, D), lambda s: (s, 0, 0))
        kinds = 3 if with_query else 2
        return call(
            f"project{place}",
            functools.partial(project_kernel, with_query),
            (seqs,),
            [
                by_row,
                whole((SMALL, D)),
                fixed((1, count, PAIR), (place, 0, 0)),
                fixed((1, count, PAIR), (place, 0, 0)),
                whole((3, D, width)),
            ],
            [(by_row, struct((seqs, count, D), HALF))] + [(by_seq, spread)] * kinds,
            after=after,
        )(rows, small_rows, cosine, sine, matrices)

    normed0, key0, value0, query = project(block_in, 2, True, (near_rows,))
    normed1, key1, value1 = project(near_rows, 1, False)
    normed2, key2, value2 = project(far_rows, 0, False)

    def pair_block(seq):
        return pl.BlockSpec((1, count, PAIR), lambda p, seq=seq: (seq, 0, p))

    flat_pair = pl.BlockSpec((count, PAIR), lambda p: (0, p))
    window_scratch = [
        pltpu.VMEM((2, TILE, 4 * TILE), WIDE),
        pltpu.VMEM((3 * count, PAIR), HALF),
        pltpu.VMEM((3 * count, PAIR), HALF),
    ]
    product = 2 * 2 * TILE * 5 * TILE * 256 * 2 * pairs

    def attend(seq):
        return call(
            f"attend{seq}",
            attend_kernel,
            (pairs,),
            [pair_block(seq)] * 7
            + [
                fixed((1, count, 1), (seq, 0, 0)),
                fixed((1, 1, 3 * count), (seq, 0, 0)),
                pl.BlockSpec((1, D, PAIR), lambda p: (3, 0, p)),
            ],
            [
                (flat_pair, struct((count, width), HALF)),
                (flat_pair, struct((count, width), WIDE)),
                (whole((count, D)), struct((count, D), HALF)),
            ],
            window_scratch + [pltpu.VMEM((count, D), WIDE)],
        )(query, key2, key1, key0, value2, value1, value0, query_ids, key_ids, matrices)

    mixed, logs, attended, attended_other = [], [], [], []
    for seq in range(seqs):
        one, two, three = attend(seq)
        mixed.append(one)
        logs.append(two)
        attended.append(three)
        attended_other.append(swap(three, "tp"))

    flat = whole((count, D))
    flat_small = whole((count, SIDE))

    def one_seq(seq, columns):
        return fixed((1, count, columns), (seq, 0, 0))

    tiles = 4
    tile = count // tiles

    def tile_rows(columns):
        return pl.BlockSpec((tile, columns), lambda t: (t, 0))

    def tile_seq(seq, columns):
        return pl.BlockSpec((1, tile, columns), lambda t: (seq, t, 0))

    routed, targets, bases, earlies = [], [], [], []
    for seq in range(seqs):
        results = call(
            f"route{seq}",
            route_kernel,
            (tiles,),
            [
                tile_seq(seq, D),
                tile_rows(D),
                tile_rows(D),
                tile_seq(seq, D),
                whole((SMALL, D)),
                tile_seq(seq, 2),
                tile_seq(seq, ALL),
            ],
            [
                (tile_rows(D), struct((count, D), HALF)),
                (tile_rows(SIDE), struct((count, SIDE), WIDE)),
                (tile_rows(D), struct((count, D), WIDE)),
                (whole((8, D)), struct((8, D), WIDE)),
            ],
        )(
            block_in,
            attended[seq],
            attended_other[seq],
            cotangent,
            small_rows,
            routes,
            prev_logits,
        )
        for kept, result in zip((routed, targets, bases, earlies), results, strict=True):
            kept.append(result)

    slots = seqs * MOST
    weight_shape = expert_weights.shape
    weight_block = (1,) + weight_shape[1:2] + (3, 1) + weight_shape[4:]
    piece = (1, 3, D, part)
    out_slots, grad_slots, held, crossing = [], [], [], []
    scattered = [None] * EXPERTS

    def finish(expert, total):
        scattered[expert] = scatter_rows(total, total.ndim - 2)

    for expert in range(EXPERTS):
        theirs, mine, one, two, *totals = call(
            f"expert{expert}",
            functools.partial(expert_kernel, expert),
            (ctx_size,),
            [
                flat,
                flat,
                whole((seqs, count, D)),
                flat_small,
                flat_small,
                whole((seqs, ALL, count)),
                pl.BlockSpec(
                    weight_block, lambda j, o, expert=expert: (o[j], 0, 0, expert, 0, 0)
                ),
            ],
            [
                (
                    pl.BlockSpec(piece, lambda j, o: (jnp.minimum(j, 1), 0, 0, 0)),
                    struct((2, 3, D, part), HALF),
                ),
                (
                    pl.BlockSpec(piece, lambda j, o: (jnp.maximum(j - 2, 0), 0, 0, 0)),
                    struct((2, 3, D, part), HALF),
                ),
                (whole((slots, D)), struct((slots, D), HALF)),
                (whole((slots, D)), struct((slots, D), HALF)),
            ],
            [
                pltpu.VMEM((slots, D), HALF),
                pltpu.VMEM((D, slots), HALF),
                pltpu.VMEM((slots, D), HALF),
                pltpu.VMEM((D, slots), HALF),
                pltpu.VMEM((slots, D), WIDE),
                pltpu.VMEM((slots, D), WIDE),
            ],
            prefetch=1,
            side=[side_sum(ctx_size, held[expert - 2])] if expert >= 2 else (),
            after=out_slots[-1:],
        )(order, routed[0], routed[1], cotangent, targets[0], targets[1], rank_rows, expert_weights)
        out_slots.append(one)
        grad_slots.append(two)
        held.append((mine, swap(theirs, "lo")))
        if totals:
            finish(expert - 2, totals[0].reshape(2, 3, D, part))

    def couple_of(place):
        return scattered[place], swap(scattered[place], "hi")

    back, back_other, sums, sums_other = [], [], [], []
    for seq in range(seqs):
        slot_block = fixed((MOST, D), (seq, 0))
        one, two, sent = call(
            f"combine{seq}",
            combine_kernel,
            (tiles,),
            [slot_block] * (2 * EXPERTS)
            + [tile_seq(seq, ALL), tile_rows(SIDE), tile_seq(seq, D)],
            [
                (tile_rows(D + PAIR), struct((count, D + PAIR), HALF)),
                (tile_rows(D), struct((count, D), HALF)),
            ],
            side=[side_sum(tiles, held[2 + seq], 0)],
        )(*out_slots, *grad_slots, rank_columns, targets[seq], cotangent)
        back.append(one)
        sums.append(two)
        back_other.append(swap(one, "tp"))
        crossing.append(swap(sent, "hi"))

    residual_grads, cots, mixed_grads, extras, talls = [], [], [], [], []
    def turn(seq):
        results = call(
            f"turn{seq}",
            turn_kernel,
            (tiles,),
            [
                tile_seq(seq, D),
                tile_rows(D),
                tile_rows(D),
                tile_seq(seq, D),
                tile_rows(D + PAIR),
                tile_rows(D + PAIR),
                tile_rows(SIDE),
                whole((SMALL, D)),
                fixed((1, D, width), (3, 0, 0)),
            ],
            [
                (tile_rows(D), struct((count, D), WIDE)),
                (tile_rows(D), struct((count, D), HALF)),
                (tile_rows(width), struct((count, width), HALF)),
                (whole((8, D)), struct((8, D), WIDE)),
                (tile_rows(PAIR), struct((count, PAIR), HALF)),
            ],
            side=[side_sum(tiles, held[2 + place], 1, (crossing[place],)) for place in range(2)]
            if seq
            else (),
            after=(query_grads[0],) if seq else (),
        )(
            block_in,
            attended[seq],
            attended_other[seq],
            cotangent,
            back[seq],
            back_other[seq],
            targets[seq],
            small_rows,
            matrices,
        )
        for kept, result in zip(
            (residual_grads, cots, mixed_grads, extras, talls), results[:5], strict=True
        ):
            kept.append(result)
        if seq:
            finish(2, results[5].reshape(3, D, part))
            finish(3, results[6].reshape(3, D, part))

    query_grads, grads2, grads1, grads0 = [], [], [], []
    pair_out = (
        pl.BlockSpec((2, count, PAIR), lambda p: (0, 0, p)),
        struct((2, count, width), HALF),
    )
    table = whole((3, count, PAIR))
    near_grads, far_grads, sents = [], [], []

    def attend_back(seq):
        results = call(
            f"back{seq}",
            attend_back_kernel,
            (pairs,),
            [pair_block(seq)] * 7
            + [
                fixed((1, count, 1), (seq, 0, 0)),
                fixed((1, 1, 3 * count), (seq, 0, 0)),
                flat_pair,
                flat_pair,
                table,
                table,
            ],
            [(flat_pair, struct((count, width), HALF))] + [pair_out] * 3,
            window_scratch
            + [pltpu.VMEM((PAIR, 3 * count), WIDE), pltpu.VMEM((PAIR, 3 * count), WIDE)],
            after=(sents[0], sums_other[0]) if seq else (crossing[0],),
        )(
            query,
            key2,
            key1,
            key0,
            value2,
            value1,
            value0,
            query_ids,
            key_ids,
            mixed_grads[seq],
            logs[seq],
            cosine,
            sine,
        )
        for kept, result in zip((query_grads, grads2, grads1, grads0), results[:4], strict=True):
            kept.append(result)
        near_grads.append(swap(results[2], "lo"))

    def send_back(seq, after):
        sents.append(
            call(
                f"relay{seq}",
                relay_kernel,
                (2,),
                [pl.BlockSpec(memory_space=pltpu.SMEM)]
                + [pl.BlockSpec((1, count, width), lambda kind: (kind, 0, 0))] * 2,
                [
                    (
                        pl.BlockSpec((1, count, width), lambda kind: (kind, 0, 0)),
                        struct((2, count, width), HALF),
                    )
                ],
                after=after,
            )(flag, grads2[seq], near_grads[seq])[0]
        )
        far_grads.append(shift(sents[seq], "hi", -1))

    def enter(seq, after):
        one = call(
            f"input{seq}",
            input_kernel,
            (tiles // 2,),
            [
                pl.BlockSpec((2 * tile, width), lambda t: (t, 0)),
            ]
            + [pl.BlockSpec((2, 2 * tile, width), lambda t: (0, t, 0))] * 3
            + [
                pl.BlockSpec(memory_space=pltpu.SMEM),
                whole((3, D, width)),
            ],
            [
                (
                    pl.BlockSpec((2 * tile, D), lambda t: (t, 0)),
                    struct((count, D), HALF),
                )
            ],
            after=after,
        )(query_grads[seq], grads0[seq], near_grads[seq], far_grads[seq], flag, matrices)[0]
        input_parts.append(one)
        input_others.append(swap(one, "tp"))

    input_parts, input_others = [], []
    def send_sums(seq):
        sums[seq], mixed_grads[seq] = lax.optimization_barrier((sums[seq], mixed_grads[seq]))
        sums_other.append(swap(sums[seq], "tp"))

    turn(0)
    send_sums(0)
    attend_back(0)
    couples = [couple_of(0)]
    turn(1)
    send_sums(1)
    send_back(0, (couples[0][1], sums_other[0]))
    attend_back(1)
    enter(0, (query_grads[1], sums_other[1]))
    couples.append(couple_of(1))
    send_back(1, (input_parts[0], couples[1][1]))
    couples.append(couple_of(2))

    def half_map(seq):
        last = 1 if seq == 0 else 0
        return lambda s, t: (jnp.where(s == seq, t, last), 0)

    operands, specs = [], []
    columns = D // 2

    def by_column(rows):
        return pl.BlockSpec((rows, columns), lambda t, *_: (0, t))

    for seq in range(seqs):
        operands += [normed2, normed1, normed0, query_grads[seq], grads2[seq], grads1[seq], grads0[seq]]
        operands += [cots[seq], mixed[seq], talls[seq], routed[seq], extras[seq], earlies[seq]]
        specs += [pl.BlockSpec((1, count, columns), lambda t, *_, seq=seq: (seq, 0, t))] * 3
        specs += [whole((count, width))] + [whole((2, count, width))] * 3
        specs += [by_column(count), whole((count, width)), whole((count, PAIR))]
        specs += [by_column(count), by_column(8), by_column(8)]
    part_shape = (2, D + SMALL, width)
    slots_of = jnp.stack(
        [2 * (lo == place % 2).astype(jnp.int32) + (hi == place // 2) for place in range(4)]
    ).astype(jnp.int32)
    theirs, mine = call(
        "weight",
        functools.partial(weight_kernel, seqs),
        (2,),
        specs + [pl.BlockSpec((3, columns, width), lambda t, *_: (0, t, 0)), by_column(SMALL)],
        [(whole(part_shape), struct(part_shape, HALF))] * 2,
        prefetch=1,
        after=(sents[1],),
    )(slots_of, *operands, matrices, small_rows)
    received = swap(theirs, "lo")
    enter(1, (couples[1][1], couples[2][1], input_others[0], scattered[3]))
    received, input_parts[1] = lax.optimization_barrier((received, input_parts[1]))
    input_others[1] = swap(input_parts[1], "tp")

    rest_shape = (D + 2 * SMALL, width)
    sent, kept = call(
        "fold",
        fold_kernel,
        (1,),
        [whole(part_shape)] * 2,
        [(whole(rest_shape), struct(rest_shape, HALF))] * 2,
    )(mine, received)
    crossed = swap(sent, "hi")
    layer_out = call(
        "layer",
        functools.partial(layer_kernel, seqs),
        (seqs, 2),
        [
            pl.BlockSpec((2 * tile, D), half_map(seq))
            for seq in range(seqs)
            for _ in range(3)
        ],
        [
            (
                pl.BlockSpec((1, 2 * tile, D), lambda s, t: (s, t, 0)),
                struct((seqs, count, D), HALF),
            )
        ],
        after=(input_parts[1],),
    )(*[array for seq in range(seqs) for array in (bases[seq], sums[seq], sums_other[seq])])[0]
    if fsdp_size <= 4:
        block = (deep + SMALL, width)
        blocks = list(
            call(
                "split",
                split_kernel,
                (1,),
                [whole(rest_shape)] * 2,
                [(whole(block), struct(block, HALF))] * fsdp_size,
                prefetch=1,
                after=(layer_out, input_others[1]),
            )(lax.axis_index("fsdp").reshape(1).astype(jnp.int32), kept, crossed)
        )
        blocks[0], scattered[3] = lax.optimization_barrier((blocks[0], scattered[3]))
        own = blocks[0].astype(WIDE)
        for distance in range(1, fsdp_size):
            own = own + ring(blocks[distance], distance).astype(WIDE)
        own = own.astype(HALF)
    else:
        total = kept + crossed
        rest = jnp.concatenate([total[D : D + SMALL], total[D + SMALL :]], axis=1)
        rest = rest.reshape(SMALL, fsdp_size, deep).transpose(1, 0, 2)
        rest = jnp.pad(rest, ((0, 0), (0, 0), (0, width - deep)))
        own = scatter_blocks(
            jnp.concatenate([total[:D].reshape(fsdp_size, deep, width), rest], axis=1)
        )
    couples.append(couple_of(3))

    by_tile = pl.BlockSpec((1, tile, D), lambda s, t: (s, t, 0))
    operands, specs = [block_in, small_rows], [by_tile, whole((SMALL, D))]
    for seq in range(seqs):
        operands += [residual_grads[seq], input_parts[seq], input_others[seq]]
        last = tiles - 1 if seq == 0 else 0
        specs += [
            pl.BlockSpec(
                (tile, D), lambda s, t, seq=seq, last=last: (jnp.where(s == seq, t, last), 0)
            )
        ] * 3
    grad_input = call(
        "final",
        functools.partial(final_kernel, seqs),
        (seqs, tiles),
        specs,
        [
            (by_tile, struct((seqs, count, D), WIDE)),
        ],
    )(*operands)[0]

    own, grad_input = lax.optimization_barrier((own, grad_input))
    small = own[deep:, :deep].astype(WIDE)
    norm_grad = small[14] + swap(small[14], "tp")
    across = swap(own, "hi")
    sources = (own, across, swap(own, "lo"), swap(across, "lo"))

    result = struct((EXPERTS, deep, hidden), WIDE)
    grads = None
    for group in (couples[:2], couples[2:]):
        operands = []
        for couple in group:
            operands += list(couple) + [swap(array, "lo") for array in couple]
        previous = [] if grads is None else list(grads)
        grads = call(
            f"place{len(previous)}",
            place_kernel,
            (1,),
            [whole(array.shape) for array in operands]
            + [pl.BlockSpec(memory_space=pl.ANY)] * len(previous),
            [(fixed((2, deep, hidden), (1 if previous else 0, 0, 0)), result)] * 3,
            prefetch=1,
            aliases={1 + len(operands) + kind: kind for kind in range(3)} if previous else None,
            after=() if previous else (input_parts[1],),
        )(order, *operands, *previous)

    matrix = struct((deep, width), WIDE)
    matrix_grads = call(
        "unpack",
        unpack_kernel,
        (1,),
        [whole(own.shape)] * 4,
        [(whole((deep, width)), matrix)] * 4,
        prefetch=1,
        after=(grads[0],),
    )(slots_of, *sources)

    return (
        layer_out,
        grad_input,
        *matrix_grads,
        *grads,
        small[0:8].T,
        small[8:12].T,
        small[12:14].T,
        norm_grad,
        small[15],
    )


def solution(mesh):
    sizes = mesh.shape
    inner = Mesh(
        mesh.devices.reshape(sizes["fsdp"], sizes["ctx"] // 2, 2, sizes["tp"]),
        ("fsdp", "hi", "lo", "tp"),
    )
    rows = P("fsdp", CTX, None)
    matrix = P("fsdp", "tp")
    experts = P(None, "fsdp", "tp")
    narrow = P("fsdp", None)
    vector = P("fsdp")
    return jax.shard_map(
        shards,
        mesh=inner,
        in_specs=(rows,) * 4
        + (P("fsdp", CTX),)
        + (matrix,) * 4
        + (experts,) * 3
        + (narrow,) * 3
        + (vector,) * 2,
        out_specs=(rows,) * 2
        + (matrix,) * 4
        + (experts,) * 3
        + (narrow,) * 3
        + (vector,) * 2,
        check_vma=False,
    )
```

```python
import functools

import jax
import jax.numpy as jnp
from jax import lax
from jax.experimental import pallas as pl
from jax.experimental.pallas import tpu as pltpu
from jax.sharding import Mesh
from jax.sharding import PartitionSpec as P

D = 768
HEADS = 12
HD = 64
EXPERTS = 4
ALL = 8
WINDOW = 1024
MOST = 192

EPSILON = 1e-06
MASKED = -1e30

CTX = ("hi", "lo")
HALF = jnp.bfloat16
WIDE = jnp.float32
TILE = 256
PAIR = 2 * HD
SMALL = 16
SIDE = 32
MIB = 1 << 20
COSTS = {
    "project": 10,
    "attend": 2,
    "route": 40,
    "expert0": 0,
    "expert1": 10,
    "expert2": 1,
    "expert3": 1,
    "combine0": 20,
    "combine1": 5,
    "turn0": 2,
    "turn1": 40,
    "back0": 10,
    "back1": 1,
    "relay0": 80,
    "relay1": 0,
    "input0": 5,
    "input1": 80,
    "weight": 20,
    "layer": 0,
    "fold": 40,
    "split": 10,
    "final": 20,
    "place0": 0,
    "place3": 5,
    "unpack": 80,
    "dispatch": 5,
}


def nn(a, b):
    return jnp.dot(a, b, preferred_element_type=WIDE)


def nt(a, b):
    return lax.dot_general(a, b, (((1,), (1,)), ((), ())), preferred_element_type=WIDE)


def call(
    tag,
    body,
    grid,
    ins,
    outs,
    scratch=(),
    prefetch=0,
    aliases=None,
    after=(),
    side=(),
):
    operands = [array for job in side for array in job[0]]
    specs = [spec for job in side for spec in job[1]]
    kind = tag.rstrip("0123456789")
    own = prefetch + len(ins)
    first = own + len(operands) + len(after)

    def inner(*refs):
        start, results = own, first + len(outs)
        for place, job in enumerate(side):
            total = refs[start][...].astype(WIDE)
            for ref in refs[start + 1 : start + len(job[0])]:
                total = total + ref[...].astype(WIDE)
            refs[results + place][...] = total.astype(HALF)
            start += len(job[0])
        body(*refs[:own], *refs[first:results], *refs[results + len(side) :])

    all_outs = list(outs) + [job[2] for job in side]
    grid_spec = pltpu.PrefetchScalarGridSpec(
        num_scalar_prefetch=prefetch,
        grid=grid,
        in_specs=list(ins) + specs + [pl.BlockSpec(memory_space=pl.ANY)] * len(after),
        out_specs=[spec for spec, _ in all_outs],
        scratch_shapes=list(scratch),
    )
    kernel = pl.pallas_call(
        inner,
        grid_spec=grid_spec,
        name=tag,
        out_shape=[shape for _, shape in all_outs],
        input_output_aliases=aliases or {},
        compiler_params=pltpu.CompilerParams(
            dimension_semantics=("arbitrary",) * len(grid), vmem_limit_bytes=64 * MIB
        ),
        cost_estimate=pl.CostEstimate(
            flops=int(COSTS.get(tag, COSTS.get(kind, 2)) * 1e9), bytes_accessed=0, transcendentals=0
        ),
    )
    return lambda *arrays: kernel(*arrays, *operands, *after)


def side_sum(steps, stacks, index=None, plain=()):
    flat = [stack.reshape(-1, stack.shape[-1]) for stack in stacks]
    rows, columns = flat[0].shape
    rows = rows if index is None else rows // stacks[0].shape[0]
    start = 0 if index is None else index * steps
    block = (rows // steps, columns)
    out = pl.BlockSpec(block, lambda step, *_: (step, 0))
    specs = [pl.BlockSpec(block, lambda step, *_: (start + step, 0))] * len(flat)
    flat += [array.reshape(rows, columns) for array in plain]
    specs += [out] * len(plain)
    return flat, specs, (out, struct((rows, columns), HALF))


def whole(shape):
    zeros = (0,) * len(shape)
    return pl.BlockSpec(shape, lambda *_: zeros)


def fixed(block, place):
    return pl.BlockSpec(block, lambda *_: place)


def struct(shape, dtype):
    return jax.ShapeDtypeStruct(shape, dtype)


def spread_of(tensor):
    return lax.rsqrt(jnp.mean(tensor * tensor, axis=-1, keepdims=True) + EPSILON)


def partner(tensor):
    lane = lax.broadcasted_iota(jnp.int32, tensor.shape, 1)
    return jnp.where(
        (lane & (HD // 2)) == 0,
        pltpu.roll(tensor, PAIR - HD // 2, 1),
        pltpu.roll(tensor, HD // 2, 1),
    )


def rank_kernel(routes_t, routes, rank_rows, rank_columns):
    count = routes.shape[1]
    down = lax.broadcasted_iota(jnp.int32, (count, count), 0)
    across = lax.broadcasted_iota(jnp.int32, (count, count), 1)
    before = jnp.where(down < across, 1.0, 0.0).astype(HALF)
    after = jnp.where(across < down, 1.0, 0.0).astype(HALF)
    row_target = lax.broadcasted_iota(jnp.int32, (ALL, count), 0)
    names = (routes_t[0, 0:1, :] == row_target) | (routes_t[0, 1:2, :] == row_target)
    ranks = nn(jnp.where(names, 1.0, 0.0).astype(HALF), before)
    rank_rows[0] = jnp.where(names, ranks, -1.0)
    column_target = lax.broadcasted_iota(jnp.int32, (count, ALL), 1)
    named = (routes[0, :, 0:1] == column_target) | (routes[0, :, 1:2] == column_target)
    ranked = nn(after, jnp.where(named, 1.0, 0.0).astype(HALF))
    rank_columns[0] = jnp.where(named, ranked, -1.0)


def project_kernel(with_query, *refs):
    x_ref, rows_ref, cos_ref, sin_ref, weights = refs[:5]
    outs = refs[5:]
    tensor = x_ref[0].astype(WIDE)
    unit = tensor * spread_of(tensor)
    normed = (unit * rows_ref[14:15, :].astype(WIDE)).astype(HALF)
    outs[0][0] = normed
    cosine, sine = cos_ref[0], sin_ref[0]

    def turned(matrix, out, scale):
        flat = nn(normed, weights[matrix])
        for piece in range(flat.shape[1] // PAIR):
            lanes = slice(piece * PAIR, (piece + 1) * PAIR)
            part = flat[:, lanes]
            result = (part * cosine + partner(part) * sine).astype(HALF)
            out[0, :, lanes] = result if scale is None else result * scale

    turned(1, outs[1], None)
    outs[2][0] = nn(normed, weights[2]).astype(HALF)
    if with_query:
        turned(0, outs[3], jnp.asarray(HD ** (-0.5), HALF))


def fill_bias(query_ids, key_ids, bias):
    upper = upper_of()
    for tile in range(2):
        ids = query_ids[0, tile * TILE : (tile + 1) * TILE, :]
        first = key_ids[0, :, tile * TILE : (tile + 1) * TILE]
        last = key_ids[0, :, (tile + 4) * TILE : (tile + 5) * TILE]
        mixed = jnp.where(upper, first, last)
        bias[tile, :, :TILE] = jnp.where(mixed == ids, 0.0, MASKED)
        inner = key_ids[0, :, (tile + 1) * TILE : (tile + 4) * TILE]
        bias[tile, :, TILE:] = jnp.where(inner == ids, 0.0, MASKED)


def upper_of():
    down = lax.broadcasted_iota(jnp.int32, (TILE, TILE), 0)
    across = lax.broadcasted_iota(jnp.int32, (TILE, TILE), 1)
    return across > down


def head_lanes(head, rows):
    lane = lax.broadcasted_iota(jnp.int32, (rows, PAIR), 1)
    return (lane < HD) if head == 0 else (lane >= HD)


def folded(upper, spread):
    span = spread.shape[1]
    return (
        jnp.where(upper, spread[:, :TILE], spread[:, span - TILE :]),
        spread[:, TILE : span - TILE],
    )


def unfolded(upper, ends, middle):
    return jnp.concatenate(
        [jnp.where(upper, ends, 0.0), middle, jnp.where(upper, 0.0, ends)], axis=1
    ).astype(HALF)


def load_window(parts, window):
    rows = parts[0].shape[1]
    for place, part in enumerate(parts):
        window[place * rows : (place + 1) * rows, :] = part[0]


def attend_kernel(
    query, k2, k1, k0, v2, v1, v0, query_ids, key_ids, w_out, mixed, logs, attended, bias, keys, values, total
):
    step = pl.program_id(0)

    @pl.when(step == 0)
    def _():
        fill_bias(query_ids, key_ids, bias)

    load_window((k2, k1, k0), keys)
    load_window((v2, v1, v0), values)
    upper = upper_of()
    span = 5 * TILE
    for tile in range(2):
        rows = slice(tile * TILE, (tile + 1) * TILE)
        window = slice(tile * TILE, tile * TILE + span)
        results, totals = [], []
        for head in range(2):
            chosen = head_lanes(head, TILE)
            own = jnp.where(chosen, query[0, rows, :], jnp.zeros((), HALF))
            ends, middle = folded(upper, nt(own, keys[window, :]))
            ends = ends + bias[tile, :, :TILE]
            middle = middle + bias[tile, :, TILE:]
            highest = jnp.maximum(
                jnp.max(ends, axis=-1, keepdims=True), jnp.max(middle, axis=-1, keepdims=True)
            )
            ends = jnp.exp(ends - highest)
            middle = jnp.exp(middle - highest)
            summed = jnp.sum(ends, axis=-1, keepdims=True) + jnp.sum(middle, axis=-1, keepdims=True)
            out = nn(unfolded(upper, ends, middle), values[window, :]) / summed
            results.append(out)
            totals.append(jnp.broadcast_to(highest + jnp.log(summed), (TILE, PAIR)))
        chosen = head_lanes(0, TILE)
        mixed[rows, :] = jnp.where(chosen, results[0], results[1]).astype(HALF)
        logs[rows, :] = jnp.where(chosen, totals[0], totals[1])
    product = nt(mixed[...], w_out[0])

    @pl.when(step == 0)
    def _():
        total[...] = product

    @pl.when(step > 0)
    def _():
        total[...] += product

    @pl.when(step == pl.num_programs(0) - 1)
    def _():
        attended[...] = total[...].astype(HALF)


def residual_of(x_ref, own, other):
    return x_ref[0].astype(WIDE) + (own[...].astype(WIDE) + other[...].astype(WIDE))


def softmax_two(a, b):
    highest = jnp.maximum(a, b)
    a, b = jnp.exp(a - highest), jnp.exp(b - highest)
    return a / (a + b), b / (a + b)


def mix_back(mix, one, two):
    inner = mix[0] * one + mix[1] * two
    return mix[0] * (one - inner), mix[1] * (two - inner)


def put(total, columns, first):
    lane = lax.broadcasted_iota(jnp.int32, total.shape, 1)
    for place, column in enumerate(columns):
        total = total + jnp.where(lane == first + place, column, 0.0)
    return total


def route_kernel(
    x_ref, own, other, upstream, rows_ref, routes, prev, routed_ref, side_ref, base_ref, small_ref
):
    residual = residual_of(x_ref, own, other)
    unit = residual * spread_of(residual)
    routed = (unit * rows_ref[15:16, :].astype(WIDE)).astype(HALF)
    routed_ref[...] = routed
    routed_wide = routed.astype(WIDE)
    scores = nt(routed, rows_ref[...])
    logits = scores[:, :ALL] + prev[0]
    target = lax.broadcasted_iota(jnp.int32, logits.shape, 1)
    picked = [routes[0, :, place : place + 1] == target for place in range(2)]
    chosen = [jnp.sum(jnp.where(one, logits, 0.0), axis=-1, keepdims=True) for one in picked]
    chosen = softmax_two(*chosen)
    weights = jnp.where(picked[0], chosen[0], 0.0) + jnp.where(picked[1], chosen[1], 0.0)
    copy, one, two = (weights[:, place : place + 1] for place in (5, 6, 7))
    first = softmax_two(scores[:, 8:9], scores[:, 9:10])
    second = softmax_two(scores[:, 10:11], scores[:, 11:12])
    vector = [rows_ref[12 + place : 13 + place, :].astype(WIDE) for place in range(2)]
    direct = copy + one * first[0] + two * second[0]
    base_ref[...] = (
        residual + routed_wide * direct + (one * first[1]) * vector[0] + (two * second[1]) * vector[1]
    )
    up_half = upstream[0]
    up = up_half.astype(WIDE)
    dot = jnp.sum(up * routed_wide, axis=-1, keepdims=True)
    dots = nt(up_half, rows_ref[...])
    dot_one, dot_two = dots[:, 12:13], dots[:, 13:14]
    side = put(
        jnp.zeros(side_ref.shape, WIDE),
        (dot, first[0] * dot + first[1] * dot_one, second[0] * dot + second[1] * dot_two),
        ALL + EXPERTS + 1,
    )
    side = put(side, mix_back(first, one * dot, one * dot_one), 16)
    side = put(side, mix_back(second, two * dot, two * dot_two), 18)
    side = put(side, (direct,), 20)
    side_ref[...] = side
    side_ref[:, :ALL] = weights
    step = pl.program_id(0)
    sums = jnp.concatenate(
        [
            jnp.sum((one * first[1]) * up, axis=0, keepdims=True),
            jnp.sum((two * second[1]) * up, axis=0, keepdims=True),
            jnp.zeros((6, D), WIDE),
        ],
        axis=0,
    )

    @pl.when(step == 0)
    def _():
        small_ref[...] = sums

    @pl.when(step > 0)
    def _():
        small_ref[...] += sums


def dispatch_kernel(routed_a, routed_b, upstream, targets_a, targets_b, ranks, rows, cots):
    expert = pl.program_id(0)
    count = routed_a.shape[0]
    slot = lax.broadcasted_iota(jnp.int32, (MOST, count), 0).astype(WIDE)
    for seq, (routed, targets) in enumerate(((routed_a, targets_a), (routed_b, targets_b))):
        place = slice(seq * MOST, (seq + 1) * MOST)
        spread = jnp.where(slot == ranks[seq, pl.ds(expert, 1), :], 1.0, 0.0).astype(HALF)
        rows[0, place, :] = nn(spread, routed[...]).astype(HALF)
        lane = lax.broadcasted_iota(jnp.int32, targets.shape, 1)
        weight = jnp.sum(jnp.where(lane == expert, targets[...], 0.0), axis=-1, keepdims=True)
        weighted = weight * upstream[seq].astype(WIDE)
        cots[0, place, :] = nn(spread, weighted.astype(HALF)).astype(HALF)


def expert_kernel(
    order, rows, cots, weights, theirs, mine, out_slots, grad_slots, rows_t, cots_t, out_total, grad_total
):
    step = pl.program_id(0)

    @pl.when(step == 0)
    def _():
        rows_t[...] = rows[0].T
        cots_t[...] = cots[0].T

    here = [weights[0, :, kind, 0].reshape(D, weights.shape[-1]) for kind in range(3)]
    gate = nn(rows[0], here[0])
    up = nn(rows[0], here[1])
    sigmoid = 1.0 / (1.0 + jnp.exp(-gate))
    silu = gate * sigmoid
    activated = (silu * up).astype(HALF)
    activated_grad = nn(cots[0], here[2])
    up_grad = (activated_grad * silu).astype(HALF)
    gate_grad = (activated_grad * up * sigmoid * (1.0 + gate * (1.0 - sigmoid))).astype(HALF)
    out_part = nt(activated, here[2])
    grad_part = nt(gate_grad, here[0]) + nt(up_grad, here[1])

    @pl.when(step == 0)
    def _():
        out_total[...] = out_part
        grad_total[...] = grad_part

    @pl.when(step > 0)
    def _():
        out_total[...] += out_part
        grad_total[...] += grad_part

    grads = (nn(rows_t[...], gate_grad), nn(rows_t[...], up_grad), nn(cots_t[...], activated))

    @pl.when(step < 2)
    def _():
        for kind in range(3):
            theirs[0, kind] = grads[kind].astype(HALF)

    @pl.when(step >= 2)
    def _():
        for kind in range(3):
            mine[0, kind] = grads[kind].astype(HALF)

    @pl.when(step == pl.num_programs(0) - 1)
    def _():
        out_slots[...] = out_total[...].astype(HALF)
        grad_slots[...] = grad_total[...].astype(HALF)


def combine_kernel(*refs):
    outs, grads = refs[:EXPERTS], refs[EXPERTS : 2 * EXPERTS]
    ranks, targets, upstream, back_ref, sum_ref = refs[2 * EXPERTS :]
    count = upstream.shape[1]
    slot = lax.broadcasted_iota(jnp.int32, (count, MOST), 1).astype(WIDE)
    wide = upstream[0].astype(WIDE)
    back = total = None
    lane = lax.broadcasted_iota(jnp.int32, (count, PAIR), 1)
    dots = jnp.zeros((count, PAIR), WIDE)
    for expert in range(EXPERTS):
        spread = jnp.where(slot == ranks[0, :, expert : expert + 1], 1.0, 0.0).astype(HALF)
        part = nn(spread, grads[expert][...])
        back = part if back is None else back + part
        part = nn(spread, outs[expert][...])
        dots = dots + jnp.where(lane == expert, jnp.sum(part * wide, axis=-1, keepdims=True), 0.0)
        part = part * targets[:, expert : expert + 1]
        total = part if total is None else total + part
    back_ref[:, :D] = back.astype(HALF)
    main = dots.astype(HALF)
    rest = pltpu.roll(dots - main.astype(WIDE), ALL, 1)
    back_ref[:, D:] = jnp.where(lane < ALL, main.astype(WIDE), rest).astype(HALF)
    sum_ref[...] = total.astype(HALF)


def turn_kernel(
    x_ref, own, other, upstream, back_own, back_other, side, rows_ref, w_out, residual_grad_ref, cot_ref,
    mixed_grad_ref, small_ref, tall_ref
):
    residual = residual_of(x_ref, own, other)
    spread = spread_of(residual)
    unit = residual * spread
    up = upstream[0].astype(WIDE)
    weights = side[:, :ALL]
    halves = back_own[:, D:].astype(WIDE) + back_other[:, D:].astype(WIDE)
    halves = halves[:, :ALL] + halves[:, ALL : 2 * ALL]
    lane = lax.broadcasted_iota(jnp.int32, halves.shape, 1)
    dots = jnp.where(lane < EXPERTS, halves, 0.0) + side[:, ALL : 2 * ALL]
    logit_grad = weights * (dots - jnp.sum(weights * dots, axis=-1, keepdims=True))
    rest = jnp.concatenate([side[:, 16:20], jnp.zeros((up.shape[0], 4), WIDE)], axis=1)
    tall = jnp.concatenate([logit_grad, rest], axis=1).astype(HALF)
    tall_ref[...] = jnp.concatenate(
        [tall, jnp.zeros((up.shape[0], PAIR - SMALL), HALF)], axis=1
    )
    back = back_own[:, :D].astype(WIDE) + back_other[:, :D].astype(WIDE)
    routed_grad = back + nn(tall, rows_ref[...]) + up * side[:, 20:21]
    step = pl.program_id(0)
    sums = jnp.sum(routed_grad * unit, axis=0, keepdims=True)
    sums = jnp.concatenate([jnp.zeros((3, D), WIDE), sums, jnp.zeros((4, D), WIDE)], axis=0)

    @pl.when(step == 0)
    def _():
        small_ref[...] = sums

    @pl.when(step > 0)
    def _():
        small_ref[...] += sums

    scaled = routed_grad * rows_ref[15:16, :].astype(WIDE)
    residual_grad = up + spread * (scaled - unit * jnp.mean(scaled * unit, axis=-1, keepdims=True))
    residual_grad_ref[...] = residual_grad
    cot = residual_grad.astype(HALF)
    cot_ref[...] = cot
    mixed_grad_ref[...] = nn(cot, w_out[0]).astype(HALF)


def attend_back_kernel(
    query, k2, k1, k0, v2, v1, v0, query_ids, key_ids, mixed_grad, logs, cos_ref, sin_ref, query_grad, grad2, grad1,
    grad0, bias, keys, values, key_total, value_total
):
    step = pl.program_id(0)

    @pl.when(step == 0)
    def _():
        fill_bias(query_ids, key_ids, bias)

    load_window((k2, k1, k0), keys)
    load_window((v2, v1, v0), values)
    upper = upper_of()
    span = 5 * TILE
    count = query.shape[1]

    def turned_back(gradient, place, rows):
        cosine, sine = cos_ref[place, rows, :], sin_ref[place, rows, :]
        return (gradient * cosine - partner(gradient) * sine).astype(HALF)

    key_total[...] = jnp.zeros_like(key_total)
    value_total[...] = jnp.zeros_like(value_total)
    for tile in range(2):
        rows = slice(tile * TILE, (tile + 1) * TILE)
        window = slice(tile * TILE, tile * TILE + span)
        results = []
        for head in range(2):
            chosen = head_lanes(head, TILE)
            nothing = jnp.zeros((), HALF)
            own = jnp.where(chosen, query[0, rows, :], nothing)
            out_grad = jnp.where(chosen, mixed_grad[rows, :], nothing)
            level = logs[rows, head * HD : head * HD + 1]
            ends, middle = folded(upper, nt(own, keys[window, :]))
            ends = jnp.exp(ends + bias[tile, :, :TILE] - level)
            middle = jnp.exp(middle + bias[tile, :, TILE:] - level)
            value_total[:, window] += nn(out_grad.T, unfolded(upper, ends, middle))
            ends_grad, middle_grad = folded(upper, nt(out_grad, values[window, :]))
            expected = jnp.sum(ends * ends_grad, axis=-1, keepdims=True) + jnp.sum(
                middle * middle_grad, axis=-1, keepdims=True
            )
            score_grad = unfolded(upper, ends * (ends_grad - expected), middle * (middle_grad - expected))
            key_total[:, window] += nn(own.T, score_grad)
            results.append(nn(score_grad, keys[window, :]))
        gradient = jnp.where(head_lanes(0, TILE), results[0], results[1]) * HD ** (-0.5)
        query_grad[rows, :] = turned_back(gradient, 2, rows)
    for place, grad in enumerate((grad2, grad1, grad0)):
        window = slice(place * count, (place + 1) * count)
        grad[0] = turned_back(key_total[:, window].T, place, slice(0, count))
        grad[1] = value_total[:, window].T.astype(HALF)


def weight_kernel(seqs, slots, *refs):
    each = 13
    groups = [refs[seq * each : (seq + 1) * each] for seq in range(seqs)]
    weights, rows_ref, theirs, mine = refs[seqs * each :]
    step = pl.program_id(0)
    query = key = value = out = small = None

    def plus(a, b):
        return b if a is None else a + b

    for group in groups:
        normed = group[0:3]
        query_grad = group[3]
        pair_grads = group[4:7]
        cot, mixed, tall, routed, extra, early = group[7:13]
        small = plus(small, nn(tall[...].T[:SMALL], routed[...]))
        lower = extra[0:4, :] + early[0:4, :]
        small = small + jnp.concatenate([jnp.zeros((SMALL - 4, lower.shape[1]), WIDE), lower], axis=0)
        for place in range(3):
            flipped = normed[place][0].T
            key = plus(key, nn(flipped, pair_grads[place][0]))
            value = plus(value, nn(flipped, pair_grads[place][1]))
            if place == 2:
                query = plus(query, nn(flipped, query_grad[...]))
        out = plus(out, nn(cot[...].T, mixed[...]))
    norm = None
    deep = out.shape[0]
    rows = pl.ds(pl.multiple_of(step * deep, deep), deep)
    for place, grad in enumerate((query, key, value, out)):
        if place < 3:
            norm = plus(norm, jnp.sum(grad * weights[place].astype(WIDE), axis=-1, keepdims=True))
        half = grad.astype(HALF)
        slot = slots[place]

        @pl.when(slot < 2)
        def _():
            theirs[jnp.minimum(slot, 1), rows, :] = half

        @pl.when(slot >= 2)
        def _():
            mine[jnp.maximum(slot - 2, 0), rows, :] = half

    gain = rows_ref[14:15, :].astype(WIDE)
    norm_row = jnp.broadcast_to(norm, (deep, PAIR)).T[0:1, :] / gain
    row = lax.broadcasted_iota(jnp.int32, small.shape, 0)
    small = jnp.where(row == 14, norm_row, small).astype(HALF)
    theirs[step, D : D + SMALL, :] = small
    mine[step, D : D + SMALL, :] = small


def fold_kernel(mine, received, sent, kept):
    for place, out in ((0, sent), (1, kept)):
        out[:D, :] = (mine[place, :D].astype(WIDE) + received[place, :D].astype(WIDE)).astype(HALF)
        for half in range(2):
            small = mine[half, D:].astype(WIDE) + received[half, D:].astype(WIDE)
            out[D + half * SMALL : D + (half + 1) * SMALL, :] = small.astype(HALF)


def split_kernel(index, kept, received, *outs):
    size = len(outs)
    deep = D // size
    width = kept.shape[1]

    def total(rows):
        return (kept[rows, :].astype(WIDE) + received[rows, :].astype(WIDE)).astype(HALF)

    small = jnp.concatenate(
        [total(slice(D + half * SMALL, D + (half + 1) * SMALL)) for half in range(2)], axis=1
    )
    for distance, out in enumerate(outs):
        place = lax.rem(index[0] + distance, size)
        out[:deep, :] = total(pl.ds(pl.multiple_of(place * deep, deep), deep))
        part = small[:, :deep]
        for other in range(1, size):
            part = jnp.where(place == other, small[:, other * deep : (other + 1) * deep], part)
        out[deep:, :] = jnp.concatenate([part, jnp.zeros((SMALL, width - deep), HALF)], axis=1)


def relay_kernel(flag, far, near, out):
    out[...] = (
        far[...].astype(WIDE) + jnp.where(flag[0] == 1, near[...].astype(WIDE), 0.0)
    ).astype(HALF)


def input_kernel(query_grad, grad0, near, far, flag, weights, out_ref):
    keep = flag[0] == 0
    totals = []
    for kind in range(2):
        total = grad0[kind].astype(WIDE) + far[kind].astype(WIDE)
        total = total + jnp.where(keep, near[kind].astype(WIDE), 0.0)
        totals.append(total.astype(HALF))
    out_ref[...] = (
        nt(query_grad[...], weights[0]) + nt(totals[0], weights[1]) + nt(totals[1], weights[2])
    ).astype(HALF)


def layer_kernel(seqs, *refs):
    step = pl.program_id(0)
    for seq in range(seqs):
        base, own, other = refs[seq * 3 : seq * 3 + 3]

        @pl.when(step == seq)
        def _():
            summed = own[...].astype(WIDE) + other[...].astype(WIDE)
            refs[-1][0] = (base[...] + summed).astype(HALF)


def final_kernel(seqs, *refs):
    x_ref, rows_ref = refs[:2]
    step = pl.program_id(0)
    for seq in range(seqs):
        residual_grad, own, other = refs[2 + seq * 3 : 5 + seq * 3]

        @pl.when(step == seq)
        def _():
            tensor = x_ref[0].astype(WIDE)
            spread = spread_of(tensor)
            unit = tensor * spread
            gradient = own[...].astype(WIDE) + other[...].astype(WIDE)
            scaled = gradient * rows_ref[14:15, :].astype(WIDE)
            refs[-1][0] = residual_grad[...] + spread * (
                scaled - unit * jnp.mean(scaled * unit, axis=-1, keepdims=True)
            )


def pack_kernel(flag, query, key, value, out, *refs):
    packed = refs[-1]
    deep, width = query.shape
    half = deep // 2
    start = pl.multiple_of(flag[0] * half, half)
    for place, matrix in enumerate((query, key, value, out)):
        packed[place * half : (place + 1) * half, :] = matrix[pl.ds(start, half), :].astype(HALF)
    rows = jnp.concatenate([ref[...] for ref in refs[:-1]], axis=0)
    rows = jnp.concatenate([rows, jnp.zeros((SMALL, width - deep), WIDE)], axis=1)
    packed[4 * half :, :] = rows.astype(HALF)


def cast_kernel(order, *refs):
    for kind in range(3):
        refs[-1][kind] = refs[kind][...].astype(HALF)


def order_kernel(index, *refs):
    parts, out = refs[:-1], refs[-1]
    size = len(parts)
    for distance, part in enumerate(parts):
        out[lax.rem(index[0] + size - distance, size)] = part[...]


def join_kernel(flag, own, other, out):
    half = own.shape[1]
    for place in range(own.shape[0]):
        first, second = own[place], other[place]
        start = place * 2 * half
        out[0, start : start + half, :] = jnp.where(flag[0] == 0, first, second)
        out[0, start + half : start + 2 * half, :] = jnp.where(flag[0] == 0, second, first)


def place_kernel(order, *refs):
    outs = refs[-3:]
    part = refs[0].shape[-1]
    for expert in range(2):
        for core, (own, across) in enumerate(
            (refs[4 * expert : 4 * expert + 2], refs[4 * expert + 2 : 4 * expert + 4])
        ):
            for far in range(2):
                lanes = pl.ds(pl.multiple_of(order[3 - far - 2 * core] * part, part), part)
                for kind in range(3):
                    if len(own.shape) == 4:
                        block = own[1 - far, kind].astype(WIDE) + across[far, kind].astype(WIDE)
                    else:
                        block = (across if far else own)[kind].astype(WIDE)
                    outs[kind][expert, :, lanes] = block


def unpack_kernel(slots, own, across, near, far, *outs):
    for place, out in enumerate(outs):
        block = jnp.where(slots[place] == 3, own[...].astype(WIDE), across[...].astype(WIDE))
        block = jnp.where(slots[place] == 1, near[...].astype(WIDE), block)
        block = jnp.where(slots[place] == 0, far[...].astype(WIDE), block)
        out[...] = block[: out.shape[0]]


def swap(block, axis):
    size = lax.axis_size(axis)
    return lax.ppermute(block, axis, [(i, i ^ 1) for i in range(size)])


def shift(block, axis, distance):
    size = lax.axis_size(axis)
    route = [(i, i + distance) for i in range(size) if 0 <= i + distance < size]
    return lax.ppermute(block, axis, route)


def pick(stack, index, axis=0):
    return lax.dynamic_index_in_dim(stack, index, axis, keepdims=False)


def scatter_rows(tensor, dimension):
    return lax.psum_scatter(tensor, "fsdp", scatter_dimension=dimension, tiled=True)


def ring(block, distance):
    size = lax.axis_size("fsdp")
    return lax.ppermute(block, "fsdp", [(i, (i + distance) % size) for i in range(size)])


def gather_blocks(block):
    size = lax.axis_size("fsdp")
    if size > 4:
        return lax.all_gather(block, "fsdp", axis=0)
    blocks = [block] + [ring(block, distance) for distance in range(1, size)]
    if block.shape[0] % 16 == 0:
        parts = whole(block.shape)
        out = (size,) + block.shape
        index = lax.axis_index("fsdp").reshape(1).astype(jnp.int32)
        return call(
            "order",
            order_kernel,
            (1,),
            [parts] * size,
            [(whole(out), struct(out, HALF))],
            prefetch=1,
        )(index, *blocks)[0]
    stacked = jnp.stack(blocks[::-1] * 2)
    start = size - 1 - lax.axis_index("fsdp")
    return lax.dynamic_slice_in_dim(stacked, start, size, axis=0)


def scatter_blocks(blocks):
    size = lax.axis_size("fsdp")
    if size > 4:
        return lax.psum_scatter(blocks, "fsdp", scatter_dimension=0)
    index = lax.axis_index("fsdp")
    total = pick(blocks, index).astype(WIDE)
    for distance in range(1, size):
        sent = pick(blocks, lax.rem(index + distance, size))
        total = total + ring(sent, distance).astype(WIDE)
    return total.astype(blocks.dtype)


def shards(
    block_in,
    cotangent,
    prev_logits,
    routes,
    segments,
    w_query,
    w_key,
    w_value,
    w_out,
    w_gate,
    w_up,
    w_down,
    router,
    const_proj,
    const_vec,
    norm_attn,
    norm_moe,
):
    seqs, count = block_in.shape[:2]
    width = w_query.shape[1]
    pairs = width // PAIR
    deep = w_gate.shape[1]
    hidden = w_gate.shape[2]
    hi, lo = lax.axis_index("hi"), lax.axis_index("lo")
    hi_size = lax.axis_size("hi")
    ctx = hi * 2 + lo
    ctx_size = hi_size * 2
    fsdp_size = lax.axis_size("fsdp")
    part = hidden // ctx_size
    order = jnp.stack([(1 - hi) * 2 + 1 - lo, hi * 2 + 1 - lo, (1 - hi) * 2 + lo, ctx]).astype(
        jnp.int32
    )

    flag = lo.reshape(1).astype(jnp.int32)

    positions = (ctx - 2) * count + jnp.arange(3 * count, dtype=jnp.int32)
    lane = jnp.arange(PAIR, dtype=jnp.int32)
    frequency = 10000.0 ** (-2.0 * (lane % (HD // 2)).astype(WIDE) / HD)
    turned = positions.astype(WIDE)[:, None] * frequency[None, :]
    cosine = jnp.cos(turned).reshape(3, count, PAIR)
    sine = (jnp.sin(turned) * jnp.where((lane & (HD // 2)) == 0, -1.0, 1.0)).reshape(3, count, PAIR)

    rank_rows, rank_columns = call(
        "rank",
        rank_kernel,
        (seqs,),
        [
            pl.BlockSpec((1, 2, count), lambda s: (s, 0, 0)),
            pl.BlockSpec((1, count, 2), lambda s: (s, 0, 0)),
        ],
        [
            (pl.BlockSpec((1, ALL, count), lambda s: (s, 0, 0)), struct((seqs, ALL, count), WIDE)),
            (pl.BlockSpec((1, count, ALL), lambda s: (s, 0, 0)), struct((seqs, count, ALL), WIDE)),
        ],
    )(routes.transpose(0, 2, 1), routes)

    half = deep // 2
    rows = 4 * half + SMALL
    rows = rows + -rows % 16
    narrow = (router.T, const_proj.T, const_vec.T, norm_attn[None, :], norm_moe[None, :])
    if half % 16 == 0:
        operands = (w_query, w_key, w_value, w_out) + narrow
        matrix_own = call(
            "pack",
            pack_kernel,
            (1,),
            [pl.BlockSpec(memory_space=pltpu.SMEM)] + [whole(array.shape) for array in operands],
            [(whole((rows, width)), struct((rows, width), HALF))],
        )(flag, *operands)[0]
    else:
        matrix_own = [
            lax.dynamic_slice_in_dim(w, lo * half, half, axis=0)
            for w in (w_query, w_key, w_value, w_out)
        ]
        small_rows = jnp.concatenate(narrow, axis=0)
        small_rows = jnp.pad(small_rows, ((0, rows - 4 * half - SMALL), (0, width - deep)))
        matrix_own = jnp.concatenate(matrix_own + [small_rows], axis=0).astype(HALF)

    def join_matrices(own):
        other = swap(own, "lo")
        if half % 16 == 0:
            block = pl.BlockSpec((fsdp_size, half, width), lambda kind: (0, kind, 0))
            return call(
                "join",
                join_kernel,
                (4,),
                [pl.BlockSpec(memory_space=pltpu.SMEM), block, block],
                [
                    (
                        pl.BlockSpec((1, D, width), lambda kind: (kind, 0, 0)),
                        struct((4, D, width), HALF),
                    )
                ],
            )(flag, own, other)[0]
        halves = [
            blocks[:, : 4 * half].reshape(fsdp_size, 4, half, width) for blocks in (own, other)
        ]
        halves = jnp.stack(
            [jnp.where(lo == 0, *halves), jnp.where(lo == 0, *halves[::-1])], axis=2
        )
        return halves.transpose(1, 0, 2, 3, 4).reshape(4, D, width)

    expert_own = call(
        "cast",
        cast_kernel,
        (EXPERTS,),
        [pl.BlockSpec((1, deep, part), lambda e, o: (e, 0, o[3]))] * 3,
        [
            (
                pl.BlockSpec((3, 1, deep, part), lambda e, o: (0, e, 0, 0)),
                struct((3, EXPERTS, deep, part), HALF),
            )
        ],
        prefetch=1,
    )(order, w_gate, w_up, w_down)[0]

    far_rows = shift(block_in, "hi", 1)
    matrix_own = gather_blocks(matrix_own)
    matrix_own, expert_own, far_rows, cosine, sine, rank_rows, rank_columns = lax.optimization_barrier(
        (matrix_own, expert_own, far_rows, cosine, sine, rank_rows, rank_columns)
    )
    expert_weights = lax.all_gather(expert_own, CTX + ("fsdp",), axis=0).reshape(
        ctx_size, fsdp_size, 3, EXPERTS, deep, part
    )
    if deep % 16:
        expert_weights = expert_weights.transpose(0, 2, 3, 1, 4, 5).reshape(
            ctx_size, 1, 3, EXPERTS, D, part
        )
    matrices = join_matrices(matrix_own)
    small_rows = matrix_own[:, 4 * half : 4 * half + SMALL, :deep]
    small_rows = small_rows.transpose(1, 0, 2).reshape(SMALL, D)
    near_rows = swap(jnp.where(lo == 1, far_rows, block_in), "lo")
    far_ids = shift(segments, "hi", 1)
    near_ids = swap(jnp.where(lo == 1, far_ids, segments), "lo")
    far_ids = jnp.where(hi == 0, -1, far_ids)
    near_ids = jnp.where(ctx == 0, -1, near_ids)
    key_ids = jnp.concatenate([far_ids, near_ids, segments], axis=1)[:, None, :]
    query_ids = segments[:, :, None]

    def project(rows, place, with_query, after=()):
        spread = struct((seqs, count, width), HALF)
        by_seq = pl.BlockSpec((1, count, width), lambda s: (s, 0, 0))
        by_row = pl.BlockSpec((1, count, D), lambda s: (s, 0, 0))
        kinds = 3 if with_query else 2
        return call(
            f"project{place}",
            functools.partial(project_kernel, with_query),
            (seqs,),
            [
                by_row,
                whole((SMALL, D)),
                fixed((1, count, PAIR), (place, 0, 0)),
                fixed((1, count, PAIR), (place, 0, 0)),
                whole((3, D, width)),
            ],
            [(by_row, struct((seqs, count, D), HALF))] + [(by_seq, spread)] * kinds,
            after=after,
        )(rows, small_rows, cosine, sine, matrices)

    normed0, key0, value0, query = project(block_in, 2, True, (near_rows,))
    normed1, key1, value1 = project(near_rows, 1, False)
    normed2, key2, value2 = project(far_rows, 0, False)

    def pair_block(seq):
        return pl.BlockSpec((1, count, PAIR), lambda p, seq=seq: (seq, 0, p))

    flat_pair = pl.BlockSpec((count, PAIR), lambda p: (0, p))
    window_scratch = [
        pltpu.VMEM((2, TILE, 4 * TILE), WIDE),
        pltpu.VMEM((3 * count, PAIR), HALF),
        pltpu.VMEM((3 * count, PAIR), HALF),
    ]
    product = 2 * 2 * TILE * 5 * TILE * 256 * 2 * pairs

    def attend(seq):
        return call(
            f"attend{seq}",
            attend_kernel,
            (pairs,),
            [pair_block(seq)] * 7
            + [
                fixed((1, count, 1), (seq, 0, 0)),
                fixed((1, 1, 3 * count), (seq, 0, 0)),
                pl.BlockSpec((1, D, PAIR), lambda p: (3, 0, p)),
            ],
            [
                (flat_pair, struct((count, width), HALF)),
                (flat_pair, struct((count, width), WIDE)),
                (whole((count, D)), struct((count, D), HALF)),
            ],
            window_scratch + [pltpu.VMEM((count, D), WIDE)],
        )(query, key2, key1, key0, value2, value1, value0, query_ids, key_ids, matrices)

    mixed, logs, attended, attended_other = [], [], [], []
    for seq in range(seqs):
        one, two, three = attend(seq)
        mixed.append(one)
        logs.append(two)
        attended.append(three)
        attended_other.append(swap(three, "tp"))

    flat = whole((count, D))
    flat_small = whole((count, SIDE))

    def one_seq(seq, columns):
        return fixed((1, count, columns), (seq, 0, 0))

    tiles = 4
    tile = count // tiles

    def tile_rows(columns):
        return pl.BlockSpec((tile, columns), lambda t: (t, 0))

    def tile_seq(seq, columns):
        return pl.BlockSpec((1, tile, columns), lambda t: (seq, t, 0))

    routed, targets, bases, earlies = [], [], [], []
    for seq in range(seqs):
        results = call(
            f"route{seq}",
            route_kernel,
            (tiles,),
            [
                tile_seq(seq, D),
                tile_rows(D),
                tile_rows(D),
                tile_seq(seq, D),
                whole((SMALL, D)),
                tile_seq(seq, 2),
                tile_seq(seq, ALL),
            ],
            [
                (tile_rows(D), struct((count, D), HALF)),
                (tile_rows(SIDE), struct((count, SIDE), WIDE)),
                (tile_rows(D), struct((count, D), WIDE)),
                (whole((8, D)), struct((8, D), WIDE)),
            ],
        )(
            block_in,
            attended[seq],
            attended_other[seq],
            cotangent,
            small_rows,
            routes,
            prev_logits,
        )
        for kept, result in zip((routed, targets, bases, earlies), results, strict=True):
            kept.append(result)

    slots = seqs * MOST
    weight_shape = expert_weights.shape
    weight_block = (1,) + weight_shape[1:2] + (3, 1) + weight_shape[4:]
    piece = (1, 3, D, part)
    out_slots, grad_slots, held, crossing = [], [], [], []
    scattered = [None] * EXPERTS

    def finish(expert, total):
        scattered[expert] = scatter_rows(total, total.ndim - 2)

    slot_out = (
        pl.BlockSpec((1, slots, D), lambda e: (e, 0, 0)),
        struct((EXPERTS, slots, D), HALF),
    )
    slot_rows, slot_cots = call(
        "dispatch",
        dispatch_kernel,
        (EXPERTS,),
        [flat, flat, whole((seqs, count, D)), flat_small, flat_small, whole((seqs, ALL, count))],
        [slot_out, slot_out],
    )(routed[0], routed[1], cotangent, targets[0], targets[1], rank_rows)
    for expert in range(EXPERTS):
        theirs, mine, one, two, *totals = call(
            f"expert{expert}",
            expert_kernel,
            (ctx_size,),
            [
                fixed((1, slots, D), (expert, 0, 0)),
                fixed((1, slots, D), (expert, 0, 0)),
                pl.BlockSpec(
                    weight_block, lambda j, o, expert=expert: (o[j], 0, 0, expert, 0, 0)
                ),
            ],
            [
                (
                    pl.BlockSpec(piece, lambda j, o: (jnp.minimum(j, 1), 0, 0, 0)),
                    struct((2, 3, D, part), HALF),
                ),
                (
                    pl.BlockSpec(piece, lambda j, o: (jnp.maximum(j - 2, 0), 0, 0, 0)),
                    struct((2, 3, D, part), HALF),
                ),
                (whole((slots, D)), struct((slots, D), HALF)),
                (whole((slots, D)), struct((slots, D), HALF)),
            ],
            [
                pltpu.VMEM((D, slots), HALF),
                pltpu.VMEM((D, slots), HALF),
                pltpu.VMEM((slots, D), WIDE),
                pltpu.VMEM((slots, D), WIDE),
            ],
            prefetch=1,
            side=[side_sum(ctx_size, held[expert - 2])] if expert >= 2 else (),
            after=out_slots[-1:],
        )(order, slot_rows, slot_cots, expert_weights)
        out_slots.append(one)
        grad_slots.append(two)
        held.append((mine, swap(theirs, "lo")))
        if totals:
            finish(expert - 2, totals[0].reshape(2, 3, D, part))

    def couple_of(place):
        return scattered[place], swap(scattered[place], "hi")

    back, back_other, sums, sums_other = [], [], [], []
    for seq in range(seqs):
        slot_block = fixed((MOST, D), (seq, 0))
        one, two, sent = call(
            f"combine{seq}",
            combine_kernel,
            (tiles,),
            [slot_block] * (2 * EXPERTS)
            + [tile_seq(seq, ALL), tile_rows(SIDE), tile_seq(seq, D)],
            [
                (tile_rows(D + PAIR), struct((count, D + PAIR), HALF)),
                (tile_rows(D), struct((count, D), HALF)),
            ],
            side=[side_sum(tiles, held[2 + seq], 0)],
        )(*out_slots, *grad_slots, rank_columns, targets[seq], cotangent)
        back.append(one)
        sums.append(two)
        back_other.append(swap(one, "tp"))
        crossing.append(swap(sent, "hi"))

    residual_grads, cots, mixed_grads, extras, talls = [], [], [], [], []
    def turn(seq):
        results = call(
            f"turn{seq}",
            turn_kernel,
            (tiles,),
            [
                tile_seq(seq, D),
                tile_rows(D),
                tile_rows(D),
                tile_seq(seq, D),
                tile_rows(D + PAIR),
                tile_rows(D + PAIR),
                tile_rows(SIDE),
                whole((SMALL, D)),
                fixed((1, D, width), (3, 0, 0)),
            ],
            [
                (tile_rows(D), struct((count, D), WIDE)),
                (tile_rows(D), struct((count, D), HALF)),
                (tile_rows(width), struct((count, width), HALF)),
                (whole((8, D)), struct((8, D), WIDE)),
                (tile_rows(PAIR), struct((count, PAIR), HALF)),
            ],
            side=[side_sum(tiles, held[2], 1, (crossing[0],))] if seq else (),
            after=(query_grads[0],) if seq else (),
        )(
            block_in,
            attended[seq],
            attended_other[seq],
            cotangent,
            back[seq],
            back_other[seq],
            targets[seq],
            small_rows,
            matrices,
        )
        for kept, result in zip(
            (residual_grads, cots, mixed_grads, extras, talls), results[:5], strict=True
        ):
            kept.append(result)
        if seq:
            finish(2, results[5].reshape(3, D, part))

    query_grads, grads2, grads1, grads0 = [], [], [], []
    pair_out = (
        pl.BlockSpec((2, count, PAIR), lambda p: (0, 0, p)),
        struct((2, count, width), HALF),
    )
    table = whole((3, count, PAIR))
    near_grads, far_grads, sents = [], [], []

    def attend_back(seq):
        results = call(
            f"back{seq}",
            attend_back_kernel,
            (pairs,),
            [pair_block(seq)] * 7
            + [
                fixed((1, count, 1), (seq, 0, 0)),
                fixed((1, 1, 3 * count), (seq, 0, 0)),
                flat_pair,
                flat_pair,
                table,
                table,
            ],
            [(flat_pair, struct((count, width), HALF))] + [pair_out] * 3,
            window_scratch
            + [pltpu.VMEM((PAIR, 3 * count), WIDE), pltpu.VMEM((PAIR, 3 * count), WIDE)],
            after=(sents[0], sums_other[0]) if seq else (crossing[0],),
            side=[side_sum(pairs, held[3], 1, (crossing[1],))] if seq else (),
        )(
            query,
            key2,
            key1,
            key0,
            value2,
            value1,
            value0,
            query_ids,
            key_ids,
            mixed_grads[seq],
            logs[seq],
            cosine,
            sine,
        )
        for kept, result in zip((query_grads, grads2, grads1, grads0), results[:4], strict=True):
            kept.append(result)
        near_grads.append(swap(results[2], "lo"))
        if seq:
            finish(3, results[4].reshape(3, D, part))

    def send_back(seq, after):
        sents.append(
            call(
                f"relay{seq}",
                relay_kernel,
                (2,),
                [pl.BlockSpec(memory_space=pltpu.SMEM)]
                + [pl.BlockSpec((1, count, width), lambda kind: (kind, 0, 0))] * 2,
                [
                    (
                        pl.BlockSpec((1, count, width), lambda kind: (kind, 0, 0)),
                        struct((2, count, width), HALF),
                    )
                ],
                after=after,
            )(flag, grads2[seq], near_grads[seq])[0]
        )
        far_grads.append(shift(sents[seq], "hi", -1))

    def enter(seq, after):
        one = call(
            f"input{seq}",
            input_kernel,
            (tiles // 2,),
            [
                pl.BlockSpec((2 * tile, width), lambda t: (t, 0)),
            ]
            + [pl.BlockSpec((2, 2 * tile, width), lambda t: (0, t, 0))] * 3
            + [
                pl.BlockSpec(memory_space=pltpu.SMEM),
                whole((3, D, width)),
            ],
            [
                (
                    pl.BlockSpec((2 * tile, D), lambda t: (t, 0)),
                    struct((count, D), HALF),
                )
            ],
            after=after,
        )(query_grads[seq], grads0[seq], near_grads[seq], far_grads[seq], flag, matrices)[0]
        input_parts.append(one)
        input_others.append(swap(one, "tp"))

    input_parts, input_others = [], []
    def send_sums(seq):
        sums[seq], mixed_grads[seq] = lax.optimization_barrier((sums[seq], mixed_grads[seq]))
        sums_other.append(swap(sums[seq], "tp"))

    turn(0)
    send_sums(0)
    attend_back(0)
    couples = [couple_of(0)]
    turn(1)
    send_sums(1)
    send_back(0, (couples[0][1], sums_other[0]))
    attend_back(1)
    enter(0, (query_grads[1],))
    couples.append(couple_of(1))
    send_back(1, (input_parts[0], couples[1][1]))
    couples.append(couple_of(2))

    def half_map(seq):
        last = 1 if seq == 0 else 0
        return lambda s, t: (jnp.where(s == seq, t, last), 0)

    operands, specs = [], []
    columns = D // 2

    def by_column(rows):
        return pl.BlockSpec((rows, columns), lambda t, *_: (0, t))

    for seq in range(seqs):
        operands += [normed2, normed1, normed0, query_grads[seq], grads2[seq], grads1[seq], grads0[seq]]
        operands += [cots[seq], mixed[seq], talls[seq], routed[seq], extras[seq], earlies[seq]]
        specs += [pl.BlockSpec((1, count, columns), lambda t, *_, seq=seq: (seq, 0, t))] * 3
        specs += [whole((count, width))] + [whole((2, count, width))] * 3
        specs += [by_column(count), whole((count, width)), whole((count, PAIR))]
        specs += [by_column(count), by_column(8), by_column(8)]
    part_shape = (2, D + SMALL, width)
    slots_of = jnp.stack(
        [2 * (lo == place % 2).astype(jnp.int32) + (hi == place // 2) for place in range(4)]
    ).astype(jnp.int32)
    theirs, mine = call(
        "weight",
        functools.partial(weight_kernel, seqs),
        (2,),
        specs + [pl.BlockSpec((3, columns, width), lambda t, *_: (0, t, 0)), by_column(SMALL)],
        [(whole(part_shape), struct(part_shape, HALF))] * 2,
        prefetch=1,
        after=(sents[1],),
    )(slots_of, *operands, matrices, small_rows)
    received = swap(theirs, "lo")
    enter(1, (couples[1][1], couples[2][1], input_others[0], scattered[3]))
    received, input_parts[1] = lax.optimization_barrier((received, input_parts[1]))
    input_others[1] = swap(input_parts[1], "tp")

    rest_shape = (D + 2 * SMALL, width)
    sent, kept = call(
        "fold",
        fold_kernel,
        (1,),
        [whole(part_shape)] * 2,
        [(whole(rest_shape), struct(rest_shape, HALF))] * 2,
    )(mine, received)
    crossed = swap(sent, "hi")
    layer_out = call(
        "layer",
        functools.partial(layer_kernel, seqs),
        (seqs, 2),
        [
            pl.BlockSpec((2 * tile, D), half_map(seq))
            for seq in range(seqs)
            for _ in range(3)
        ],
        [
            (
                pl.BlockSpec((1, 2 * tile, D), lambda s, t: (s, t, 0)),
                struct((seqs, count, D), HALF),
            )
        ],
        after=(input_parts[1],),
    )(*[array for seq in range(seqs) for array in (bases[seq], sums[seq], sums_other[seq])])[0]
    if fsdp_size <= 4:
        block = (deep + SMALL, width)
        blocks = list(
            call(
                "split",
                split_kernel,
                (1,),
                [whole(rest_shape)] * 2,
                [(whole(block), struct(block, HALF))] * fsdp_size,
                prefetch=1,
                after=(layer_out, input_others[1]),
            )(lax.axis_index("fsdp").reshape(1).astype(jnp.int32), kept, crossed)
        )
        blocks[0], scattered[3] = lax.optimization_barrier((blocks[0], scattered[3]))
        own = blocks[0].astype(WIDE)
        for distance in range(1, fsdp_size):
            own = own + ring(blocks[distance], distance).astype(WIDE)
        own = own.astype(HALF)
    else:
        total = kept + crossed
        rest = jnp.concatenate([total[D : D + SMALL], total[D + SMALL :]], axis=1)
        rest = rest.reshape(SMALL, fsdp_size, deep).transpose(1, 0, 2)
        rest = jnp.pad(rest, ((0, 0), (0, 0), (0, width - deep)))
        own = scatter_blocks(
            jnp.concatenate([total[:D].reshape(fsdp_size, deep, width), rest], axis=1)
        )
    couples.append(couple_of(3))

    by_tile = pl.BlockSpec((1, tile, D), lambda s, t: (s, t, 0))
    operands, specs = [block_in, small_rows], [by_tile, whole((SMALL, D))]
    for seq in range(seqs):
        operands += [residual_grads[seq], input_parts[seq], input_others[seq]]
        last = tiles - 1 if seq == 0 else 0
        specs += [
            pl.BlockSpec(
                (tile, D), lambda s, t, seq=seq, last=last: (jnp.where(s == seq, t, last), 0)
            )
        ] * 3
    grad_input = call(
        "final",
        functools.partial(final_kernel, seqs),
        (seqs, tiles),
        specs,
        [
            (by_tile, struct((seqs, count, D), WIDE)),
        ],
    )(*operands)[0]

    own, grad_input = lax.optimization_barrier((own, grad_input))
    small = own[deep:, :deep].astype(WIDE)
    norm_grad = small[14] + swap(small[14], "tp")
    across = swap(own, "hi")
    sources = (own, across, swap(own, "lo"), swap(across, "lo"))

    result = struct((EXPERTS, deep, hidden), WIDE)
    grads = None
    for group in (couples[:2], couples[2:]):
        operands = []
        for couple in group:
            operands += list(couple) + [swap(array, "lo") for array in couple]
        previous = [] if grads is None else list(grads)
        grads = call(
            f"place{len(previous)}",
            place_kernel,
            (1,),
            [whole(array.shape) for array in operands]
            + [pl.BlockSpec(memory_space=pl.ANY)] * len(previous),
            [(fixed((2, deep, hidden), (1 if previous else 0, 0, 0)), result)] * 3,
            prefetch=1,
            aliases={1 + len(operands) + kind: kind for kind in range(3)} if previous else None,
            after=() if previous else (input_parts[1],),
        )(order, *operands, *previous)

    matrix = struct((deep, width), WIDE)
    matrix_grads = call(
        "unpack",
        unpack_kernel,
        (1,),
        [whole(own.shape)] * 4,
        [(whole((deep, width)), matrix)] * 4,
        prefetch=1,
        after=(grads[0],),
    )(slots_of, *sources)

    return (
        layer_out,
        grad_input,
        *matrix_grads,
        *grads,
        small[0:8].T,
        small[8:12].T,
        small[12:14].T,
        norm_grad,
        small[15],
    )


def solution(mesh):
    sizes = mesh.shape
    inner = Mesh(
        mesh.devices.reshape(sizes["fsdp"], sizes["ctx"] // 2, 2, sizes["tp"]),
        ("fsdp", "hi", "lo", "tp"),
    )
    rows = P("fsdp", CTX, None)
    matrix = P("fsdp", "tp")
    experts = P(None, "fsdp", "tp")
    narrow = P("fsdp", None)
    vector = P("fsdp")
    return jax.shard_map(
        shards,
        mesh=inner,
        in_specs=(rows,) * 4
        + (P("fsdp", CTX),)
        + (matrix,) * 4
        + (experts,) * 3
        + (narrow,) * 3
        + (vector,) * 2,
        out_specs=(rows,) * 2
        + (matrix,) * 4
        + (experts,) * 3
        + (narrow,) * 3
        + (vector,) * 2,
        check_vma=False,
    )
```

```python
import functools

import jax
import jax.numpy as jnp
from jax import lax
from jax.experimental import pallas as pl
from jax.experimental.pallas import tpu as pltpu
from jax.sharding import Mesh
from jax.sharding import PartitionSpec as P

D = 768
HEADS = 12
HD = 64
EXPERTS = 4
ALL = 8
WINDOW = 1024
MOST = 192

EPSILON = 1e-06
MASKED = -1e30

CTX = ("hi", "lo")
HALF = jnp.bfloat16
WIDE = jnp.float32
TILE = 256
PAIR = 2 * HD
SMALL = 16
SIDE = 32
MIB = 1 << 20
COSTS = {
    "project": 10,
    "attend": 2,
    "route": 40,
    "expert0": 0,
    "expert1": 10,
    "expert2": 1,
    "expert3": 1,
    "combine0": 20,
    "combine1": 5,
    "turn0": 2,
    "turn1": 40,
    "back0": 10,
    "back1": 1,
    "relay0": 80,
    "relay1": 0,
    "input0": 5,
    "input1": 80,
    "weight": 20,
    "layer": 0,
    "fold": 40,
    "split": 10,
    "final": 20,
    "place0": 0,
    "place3": 0,
    "unpack": 80,
    "dispatch": 5,
    "first": 7,
}


def nn(a, b):
    return jnp.dot(a, b, preferred_element_type=WIDE)


def nt(a, b):
    return lax.dot_general(a, b, (((1,), (1,)), ((), ())), preferred_element_type=WIDE)


def call(
    tag,
    body,
    grid,
    ins,
    outs,
    scratch=(),
    prefetch=0,
    aliases=None,
    after=(),
    side=(),
):
    operands = [array for job in side for array in job[0]]
    specs = [spec for job in side for spec in job[1]]
    kind = tag.rstrip("0123456789")
    own = prefetch + len(ins)
    first = own + len(operands) + len(after)

    def inner(*refs):
        start, results = own, first + len(outs)
        for place, job in enumerate(side):
            total = refs[start][...].astype(WIDE)
            for ref in refs[start + 1 : start + len(job[0])]:
                total = total + ref[...].astype(WIDE)
            refs[results + place][...] = total.astype(HALF)
            start += len(job[0])
        body(*refs[:own], *refs[first:results], *refs[results + len(side) :])

    all_outs = list(outs) + [job[2] for job in side]
    grid_spec = pltpu.PrefetchScalarGridSpec(
        num_scalar_prefetch=prefetch,
        grid=grid,
        in_specs=list(ins) + specs + [pl.BlockSpec(memory_space=pl.ANY)] * len(after),
        out_specs=[spec for spec, _ in all_outs],
        scratch_shapes=list(scratch),
    )
    kernel = pl.pallas_call(
        inner,
        grid_spec=grid_spec,
        name=tag,
        out_shape=[shape for _, shape in all_outs],
        input_output_aliases=aliases or {},
        compiler_params=pltpu.CompilerParams(
            dimension_semantics=("arbitrary",) * len(grid), vmem_limit_bytes=64 * MIB
        ),
        cost_estimate=pl.CostEstimate(
            flops=int(COSTS.get(tag, COSTS.get(kind, 2)) * 1e9), bytes_accessed=0, transcendentals=0
        ),
    )
    return lambda *arrays: kernel(*arrays, *operands, *after)


def side_sum(steps, stacks, index=None, plain=()):
    flat = [stack.reshape(-1, stack.shape[-1]) for stack in stacks]
    rows, columns = flat[0].shape
    rows = rows if index is None else rows // stacks[0].shape[0]
    start = 0 if index is None else index * steps
    block = (rows // steps, columns)
    out = pl.BlockSpec(block, lambda step, *_: (step, 0))
    specs = [pl.BlockSpec(block, lambda step, *_: (start + step, 0))] * len(flat)
    flat += [array.reshape(rows, columns) for array in plain]
    specs += [out] * len(plain)
    return flat, specs, (out, struct((rows, columns), HALF))


def whole(shape):
    zeros = (0,) * len(shape)
    return pl.BlockSpec(shape, lambda *_: zeros)


def fixed(block, place):
    return pl.BlockSpec(block, lambda *_: place)


def struct(shape, dtype):
    return jax.ShapeDtypeStruct(shape, dtype)


def spread_of(tensor):
    return lax.rsqrt(jnp.mean(tensor * tensor, axis=-1, keepdims=True) + EPSILON)


def partner(tensor):
    lane = lax.broadcasted_iota(jnp.int32, tensor.shape, 1)
    return jnp.where(
        (lane & (HD // 2)) == 0,
        pltpu.roll(tensor, PAIR - HD // 2, 1),
        pltpu.roll(tensor, HD // 2, 1),
    )


def rank_kernel(routes_t, routes, rank_rows, rank_columns):
    count = routes.shape[1]
    down = lax.broadcasted_iota(jnp.int32, (count, count), 0)
    across = lax.broadcasted_iota(jnp.int32, (count, count), 1)
    before = jnp.where(down < across, 1.0, 0.0).astype(HALF)
    after = jnp.where(across < down, 1.0, 0.0).astype(HALF)
    row_target = lax.broadcasted_iota(jnp.int32, (ALL, count), 0)
    names = (routes_t[0, 0:1, :] == row_target) | (routes_t[0, 1:2, :] == row_target)
    ranks = nn(jnp.where(names, 1.0, 0.0).astype(HALF), before)
    rank_rows[0] = jnp.where(names, ranks, -1.0)
    column_target = lax.broadcasted_iota(jnp.int32, (count, ALL), 1)
    named = (routes[0, :, 0:1] == column_target) | (routes[0, :, 1:2] == column_target)
    ranked = nn(after, jnp.where(named, 1.0, 0.0).astype(HALF))
    rank_columns[0] = jnp.where(named, ranked, -1.0)


def project_kernel(with_query, *refs):
    x_ref, rows_ref, cos_ref, sin_ref, weights = refs[:5]
    outs = refs[5:]
    tensor = x_ref[0].astype(WIDE)
    unit = tensor * spread_of(tensor)
    normed = (unit * rows_ref[14:15, :].astype(WIDE)).astype(HALF)
    outs[0][0] = normed
    cosine, sine = cos_ref[0], sin_ref[0]

    def turned(matrix, out, scale):
        flat = nn(normed, weights[matrix])
        for piece in range(flat.shape[1] // PAIR):
            lanes = slice(piece * PAIR, (piece + 1) * PAIR)
            part = flat[:, lanes]
            result = (part * cosine + partner(part) * sine).astype(HALF)
            out[0, :, lanes] = result if scale is None else result * scale

    turned(1, outs[1], None)
    outs[2][0] = nn(normed, weights[2]).astype(HALF)
    if with_query:
        turned(0, outs[3], jnp.asarray(HD ** (-0.5), HALF))


def fill_bias(query_ids, key_ids, bias):
    upper = upper_of()
    for tile in range(2):
        ids = query_ids[0, tile * TILE : (tile + 1) * TILE, :]
        first = key_ids[0, :, tile * TILE : (tile + 1) * TILE]
        last = key_ids[0, :, (tile + 4) * TILE : (tile + 5) * TILE]
        mixed = jnp.where(upper, first, last)
        bias[tile, :, :TILE] = jnp.where(mixed == ids, 0.0, MASKED)
        inner = key_ids[0, :, (tile + 1) * TILE : (tile + 4) * TILE]
        bias[tile, :, TILE:] = jnp.where(inner == ids, 0.0, MASKED)


def upper_of():
    down = lax.broadcasted_iota(jnp.int32, (TILE, TILE), 0)
    across = lax.broadcasted_iota(jnp.int32, (TILE, TILE), 1)
    return across > down


def head_lanes(head, rows):
    lane = lax.broadcasted_iota(jnp.int32, (rows, PAIR), 1)
    return (lane < HD) if head == 0 else (lane >= HD)


def folded(upper, spread):
    span = spread.shape[1]
    return (
        jnp.where(upper, spread[:, :TILE], spread[:, span - TILE :]),
        spread[:, TILE : span - TILE],
    )


def unfolded(upper, ends, middle):
    return jnp.concatenate(
        [jnp.where(upper, ends, 0.0), middle, jnp.where(upper, 0.0, ends)], axis=1
    ).astype(HALF)


def load_window(parts, window):
    rows = parts[0].shape[1]
    for place, part in enumerate(parts):
        window[place * rows : (place + 1) * rows, :] = part[0]


def attend_kernel(
    query, k2, k1, k0, v2, v1, v0, query_ids, key_ids, w_out, mixed, logs, attended, bias, keys, values, total
):
    step = pl.program_id(0)

    @pl.when(step == 0)
    def _():
        fill_bias(query_ids, key_ids, bias)

    load_window((k2, k1, k0), keys)
    load_window((v2, v1, v0), values)
    upper = upper_of()
    span = 5 * TILE
    for tile in range(2):
        rows = slice(tile * TILE, (tile + 1) * TILE)
        window = slice(tile * TILE, tile * TILE + span)
        results, totals = [], []
        for head in range(2):
            chosen = head_lanes(head, TILE)
            own = jnp.where(chosen, query[0, rows, :], jnp.zeros((), HALF))
            ends, middle = folded(upper, nt(own, keys[window, :]))
            ends = ends + bias[tile, :, :TILE]
            middle = middle + bias[tile, :, TILE:]
            highest = jnp.maximum(
                jnp.max(ends, axis=-1, keepdims=True), jnp.max(middle, axis=-1, keepdims=True)
            )
            ends = jnp.exp(ends - highest)
            middle = jnp.exp(middle - highest)
            summed = jnp.sum(ends, axis=-1, keepdims=True) + jnp.sum(middle, axis=-1, keepdims=True)
            out = nn(unfolded(upper, ends, middle), values[window, :]) / summed
            results.append(out)
            totals.append(jnp.broadcast_to(highest + jnp.log(summed), (TILE, PAIR)))
        chosen = head_lanes(0, TILE)
        mixed[rows, :] = jnp.where(chosen, results[0], results[1]).astype(HALF)
        logs[rows, :] = jnp.where(chosen, totals[0], totals[1])
    product = nt(mixed[...], w_out[0])

    @pl.when(step == 0)
    def _():
        total[...] = product

    @pl.when(step > 0)
    def _():
        total[...] += product

    @pl.when(step == pl.num_programs(0) - 1)
    def _():
        attended[...] = total[...].astype(HALF)


def residual_of(x_ref, own, other):
    return x_ref[0].astype(WIDE) + (own[...].astype(WIDE) + other[...].astype(WIDE))


def softmax_two(a, b):
    highest = jnp.maximum(a, b)
    a, b = jnp.exp(a - highest), jnp.exp(b - highest)
    return a / (a + b), b / (a + b)


def mix_back(mix, one, two):
    inner = mix[0] * one + mix[1] * two
    return mix[0] * (one - inner), mix[1] * (two - inner)


def put(total, columns, first):
    lane = lax.broadcasted_iota(jnp.int32, total.shape, 1)
    for place, column in enumerate(columns):
        total = total + jnp.where(lane == first + place, column, 0.0)
    return total


def route_kernel(
    x_ref, own, other, upstream, rows_ref, routes, prev, routed_ref, side_ref, base_ref, small_ref
):
    residual = residual_of(x_ref, own, other)
    unit = residual * spread_of(residual)
    routed = (unit * rows_ref[15:16, :].astype(WIDE)).astype(HALF)
    routed_ref[...] = routed
    routed_wide = routed.astype(WIDE)
    scores = nt(routed, rows_ref[...])
    logits = scores[:, :ALL] + prev[0]
    target = lax.broadcasted_iota(jnp.int32, logits.shape, 1)
    picked = [routes[0, :, place : place + 1] == target for place in range(2)]
    chosen = [jnp.sum(jnp.where(one, logits, 0.0), axis=-1, keepdims=True) for one in picked]
    chosen = softmax_two(*chosen)
    weights = jnp.where(picked[0], chosen[0], 0.0) + jnp.where(picked[1], chosen[1], 0.0)
    copy, one, two = (weights[:, place : place + 1] for place in (5, 6, 7))
    first = softmax_two(scores[:, 8:9], scores[:, 9:10])
    second = softmax_two(scores[:, 10:11], scores[:, 11:12])
    vector = [rows_ref[12 + place : 13 + place, :].astype(WIDE) for place in range(2)]
    direct = copy + one * first[0] + two * second[0]
    base_ref[...] = (
        residual + routed_wide * direct + (one * first[1]) * vector[0] + (two * second[1]) * vector[1]
    )
    up_half = upstream[0]
    up = up_half.astype(WIDE)
    dot = jnp.sum(up * routed_wide, axis=-1, keepdims=True)
    dots = nt(up_half, rows_ref[...])
    dot_one, dot_two = dots[:, 12:13], dots[:, 13:14]
    side = put(
        jnp.zeros(side_ref.shape, WIDE),
        (dot, first[0] * dot + first[1] * dot_one, second[0] * dot + second[1] * dot_two),
        ALL + EXPERTS + 1,
    )
    side = put(side, mix_back(first, one * dot, one * dot_one), 16)
    side = put(side, mix_back(second, two * dot, two * dot_two), 18)
    side = put(side, (direct,), 20)
    side_ref[...] = side
    side_ref[:, :ALL] = weights
    step = pl.program_id(0)
    sums = jnp.concatenate(
        [
            jnp.sum((one * first[1]) * up, axis=0, keepdims=True),
            jnp.sum((two * second[1]) * up, axis=0, keepdims=True),
            jnp.zeros((6, D), WIDE),
        ],
        axis=0,
    )

    @pl.when(step == 0)
    def _():
        small_ref[...] = sums

    @pl.when(step > 0)
    def _():
        small_ref[...] += sums


def dispatch_kernel(routed_a, routed_b, upstream, targets_a, targets_b, ranks, rows, cots):
    expert = pl.program_id(0)
    count = routed_a.shape[0]
    slot = lax.broadcasted_iota(jnp.int32, (MOST, count), 0).astype(WIDE)
    for seq, (routed, targets) in enumerate(((routed_a, targets_a), (routed_b, targets_b))):
        place = slice(seq * MOST, (seq + 1) * MOST)
        spread = jnp.where(slot == ranks[seq, pl.ds(expert, 1), :], 1.0, 0.0).astype(HALF)
        rows[0, place, :] = nn(spread, routed[...]).astype(HALF)
        lane = lax.broadcasted_iota(jnp.int32, targets.shape, 1)
        weight = jnp.sum(jnp.where(lane == expert, targets[...], 0.0), axis=-1, keepdims=True)
        weighted = weight * upstream[seq].astype(WIDE)
        cots[0, place, :] = nn(spread, weighted.astype(HALF)).astype(HALF)


def expert_kernel(
    order, rows, cots, weights, theirs, mine, out_slots, grad_slots, rows_t, cots_t, out_total, grad_total
):
    step = pl.program_id(0)

    @pl.when(step == 0)
    def _():
        rows_t[...] = rows[0].T
        cots_t[...] = cots[0].T

    here = [weights[0, :, kind, 0].reshape(D, weights.shape[-1]) for kind in range(3)]
    gate = nn(rows[0], here[0])
    up = nn(rows[0], here[1])
    sigmoid = 1.0 / (1.0 + jnp.exp(-gate))
    silu = gate * sigmoid
    activated = (silu * up).astype(HALF)
    activated_grad = nn(cots[0], here[2])
    up_grad = (activated_grad * silu).astype(HALF)
    gate_grad = (activated_grad * up * sigmoid * (1.0 + gate * (1.0 - sigmoid))).astype(HALF)
    out_part = nt(activated, here[2])
    grad_part = nt(gate_grad, here[0]) + nt(up_grad, here[1])

    @pl.when(step == 0)
    def _():
        out_total[...] = out_part
        grad_total[...] = grad_part

    @pl.when(step > 0)
    def _():
        out_total[...] += out_part
        grad_total[...] += grad_part

    grads = (nn(rows_t[...], gate_grad), nn(rows_t[...], up_grad), nn(cots_t[...], activated))

    @pl.when(step < 2)
    def _():
        for kind in range(3):
            theirs[0, kind] = grads[kind].astype(HALF)

    @pl.when(step >= 2)
    def _():
        for kind in range(3):
            mine[0, kind] = grads[kind].astype(HALF)

    @pl.when(step == pl.num_programs(0) - 1)
    def _():
        out_slots[...] = out_total[...].astype(HALF)
        grad_slots[...] = grad_total[...].astype(HALF)


def combine_kernel(*refs):
    outs, grads = refs[:EXPERTS], refs[EXPERTS : 2 * EXPERTS]
    ranks, targets, upstream, back_ref, sum_ref = refs[2 * EXPERTS :]
    count = upstream.shape[1]
    slot = lax.broadcasted_iota(jnp.int32, (count, MOST), 1).astype(WIDE)
    wide = upstream[0].astype(WIDE)
    back = total = None
    lane = lax.broadcasted_iota(jnp.int32, (count, PAIR), 1)
    dots = jnp.zeros((count, PAIR), WIDE)
    for expert in range(EXPERTS):
        spread = jnp.where(slot == ranks[0, :, expert : expert + 1], 1.0, 0.0).astype(HALF)
        part = nn(spread, grads[expert][...])
        back = part if back is None else back + part
        part = nn(spread, outs[expert][...])
        dots = dots + jnp.where(lane == expert, jnp.sum(part * wide, axis=-1, keepdims=True), 0.0)
        part = part * targets[:, expert : expert + 1]
        total = part if total is None else total + part
    back_ref[:, :D] = back.astype(HALF)
    main = dots.astype(HALF)
    rest = pltpu.roll(dots - main.astype(WIDE), ALL, 1)
    back_ref[:, D:] = jnp.where(lane < ALL, main.astype(WIDE), rest).astype(HALF)
    sum_ref[...] = total.astype(HALF)


def turn_kernel(
    x_ref, own, other, upstream, back_own, back_other, side, rows_ref, w_out, residual_grad_ref, cot_ref,
    mixed_grad_ref, small_ref, tall_ref
):
    residual = residual_of(x_ref, own, other)
    spread = spread_of(residual)
    unit = residual * spread
    up = upstream[0].astype(WIDE)
    weights = side[:, :ALL]
    halves = back_own[:, D:].astype(WIDE) + back_other[:, D:].astype(WIDE)
    halves = halves[:, :ALL] + halves[:, ALL : 2 * ALL]
    lane = lax.broadcasted_iota(jnp.int32, halves.shape, 1)
    dots = jnp.where(lane < EXPERTS, halves, 0.0) + side[:, ALL : 2 * ALL]
    logit_grad = weights * (dots - jnp.sum(weights * dots, axis=-1, keepdims=True))
    rest = jnp.concatenate([side[:, 16:20], jnp.zeros((up.shape[0], 4), WIDE)], axis=1)
    tall = jnp.concatenate([logit_grad, rest], axis=1).astype(HALF)
    tall_ref[...] = jnp.concatenate(
        [tall, jnp.zeros((up.shape[0], PAIR - SMALL), HALF)], axis=1
    )
    back = back_own[:, :D].astype(WIDE) + back_other[:, :D].astype(WIDE)
    routed_grad = back + nn(tall, rows_ref[...]) + up * side[:, 20:21]
    step = pl.program_id(0)
    sums = jnp.sum(routed_grad * unit, axis=0, keepdims=True)
    sums = jnp.concatenate([jnp.zeros((3, D), WIDE), sums, jnp.zeros((4, D), WIDE)], axis=0)

    @pl.when(step == 0)
    def _():
        small_ref[...] = sums

    @pl.when(step > 0)
    def _():
        small_ref[...] += sums

    scaled = routed_grad * rows_ref[15:16, :].astype(WIDE)
    residual_grad = up + spread * (scaled - unit * jnp.mean(scaled * unit, axis=-1, keepdims=True))
    residual_grad_ref[...] = residual_grad
    cot = residual_grad.astype(HALF)
    cot_ref[...] = cot
    mixed_grad_ref[...] = nn(cot, w_out[0]).astype(HALF)


def attend_back_kernel(
    query, k2, k1, k0, v2, v1, v0, query_ids, key_ids, mixed_grad, mixed, logs, cos_ref, sin_ref, query_grad, grad2, grad1,
    grad0, bias, keys, values, key_total, value_total
):
    step = pl.program_id(0)

    @pl.when(step == 0)
    def _():
        fill_bias(query_ids, key_ids, bias)

    load_window((k2, k1, k0), keys)
    load_window((v2, v1, v0), values)
    upper = upper_of()
    span = 5 * TILE
    count = query.shape[1]

    def turned_back(gradient, place, rows):
        cosine, sine = cos_ref[place, rows, :], sin_ref[place, rows, :]
        return (gradient * cosine - partner(gradient) * sine).astype(HALF)

    key_total[...] = jnp.zeros_like(key_total)
    value_total[...] = jnp.zeros_like(value_total)
    for tile in range(2):
        rows = slice(tile * TILE, (tile + 1) * TILE)
        window = slice(tile * TILE, tile * TILE + span)
        results = []
        for head in range(2):
            chosen = head_lanes(head, TILE)
            nothing = jnp.zeros((), HALF)
            own = jnp.where(chosen, query[0, rows, :], nothing)
            out_grad = jnp.where(chosen, mixed_grad[rows, :], nothing)
            level = logs[rows, head * HD : head * HD + 1]
            ends, middle = folded(upper, nt(own, keys[window, :]))
            ends = jnp.exp(ends + bias[tile, :, :TILE] - level)
            middle = jnp.exp(middle + bias[tile, :, TILE:] - level)
            value_total[:, window] += nn(out_grad.T, unfolded(upper, ends, middle))
            ends_grad, middle_grad = folded(upper, nt(out_grad, values[window, :]))
            product = out_grad.astype(WIDE) * mixed[rows, :].astype(WIDE)
            expected = jnp.sum(product, axis=-1, keepdims=True)
            score_grad = unfolded(upper, ends * (ends_grad - expected), middle * (middle_grad - expected))
            key_total[:, window] += nn(own.T, score_grad)
            results.append(nn(score_grad, keys[window, :]))
        gradient = jnp.where(head_lanes(0, TILE), results[0], results[1]) * HD ** (-0.5)
        query_grad[rows, :] = turned_back(gradient, 2, rows)
    for place, grad in enumerate((grad2, grad1, grad0)):
        window = slice(place * count, (place + 1) * count)
        grad[0] = turned_back(key_total[:, window].T, place, slice(0, count))
        grad[1] = value_total[:, window].T.astype(HALF)


def weight_sums(group):
    normed = group[0:3]
    query_grad = group[3]
    pair_grads = group[4:7]
    cot, mixed, tall, routed, extra, early = group[7:13]
    small = nn(tall[...].T[:SMALL], routed[...])
    lower = extra[0:4, :] + early[0:4, :]
    small = small + jnp.concatenate([jnp.zeros((SMALL - 4, lower.shape[1]), WIDE), lower], axis=0)
    key = value = 0.0
    for place in range(3):
        flipped = normed[place][0].T
        key = key + nn(flipped, pair_grads[place][0])
        value = value + nn(flipped, pair_grads[place][1])
    query = nn(flipped, query_grad[...])
    return (query, key, value, nn(cot[...].T, mixed[...])), small


def first_weight_kernel(*refs):
    grads, small = weight_sums(refs[:13])
    for place, grad in enumerate(grads):
        refs[13][place] = grad
    refs[14][...] = small


def weight_kernel(slots, *refs):
    grads, small = weight_sums(refs[:13])
    earlier, earlier_small, weights, rows_ref, theirs, mine = refs[13:]
    query, key, value, out = (grad + earlier[place] for place, grad in enumerate(grads))
    small = small + earlier_small[...]
    step = pl.program_id(0)
    norm = 0.0
    deep = out.shape[0]
    rows = pl.ds(pl.multiple_of(step * deep, deep), deep)
    for place, grad in enumerate((query, key, value, out)):
        if place < 3:
            norm = norm + jnp.sum(grad * weights[place].astype(WIDE), axis=-1, keepdims=True)
        half = grad.astype(HALF)
        slot = slots[place]

        @pl.when(slot < 2)
        def _():
            theirs[jnp.minimum(slot, 1), rows, :] = half

        @pl.when(slot >= 2)
        def _():
            mine[jnp.maximum(slot - 2, 0), rows, :] = half

    gain = rows_ref[14:15, :].astype(WIDE)
    norm_row = jnp.broadcast_to(norm, (deep, PAIR)).T[0:1, :] / gain
    row = lax.broadcasted_iota(jnp.int32, small.shape, 0)
    small = jnp.where(row == 14, norm_row, small).astype(HALF)
    theirs[step, D : D + SMALL, :] = small
    mine[step, D : D + SMALL, :] = small


def fold_kernel(mine, received, sent, kept):
    for place, out in ((0, sent), (1, kept)):
        out[:D, :] = (mine[place, :D].astype(WIDE) + received[place, :D].astype(WIDE)).astype(HALF)
        for half in range(2):
            small = mine[half, D:].astype(WIDE) + received[half, D:].astype(WIDE)
            out[D + half * SMALL : D + (half + 1) * SMALL, :] = small.astype(HALF)


def split_kernel(index, kept, received, *outs):
    size = len(outs)
    deep = D // size
    width = kept.shape[1]

    def total(rows):
        return (kept[rows, :].astype(WIDE) + received[rows, :].astype(WIDE)).astype(HALF)

    small = jnp.concatenate(
        [total(slice(D + half * SMALL, D + (half + 1) * SMALL)) for half in range(2)], axis=1
    )
    for distance, out in enumerate(outs):
        place = lax.rem(index[0] + distance, size)
        out[:deep, :] = total(pl.ds(pl.multiple_of(place * deep, deep), deep))
        part = small[:, :deep]
        for other in range(1, size):
            part = jnp.where(place == other, small[:, other * deep : (other + 1) * deep], part)
        out[deep:, :] = jnp.concatenate([part, jnp.zeros((SMALL, width - deep), HALF)], axis=1)


def relay_kernel(flag, far, near, out):
    out[...] = (
        far[...].astype(WIDE) + jnp.where(flag[0] == 1, near[...].astype(WIDE), 0.0)
    ).astype(HALF)


def input_kernel(query_grad, grad0, near, far, flag, weights, out_ref):
    keep = flag[0] == 0
    totals = []
    for kind in range(2):
        total = grad0[kind].astype(WIDE) + far[kind].astype(WIDE)
        total = total + jnp.where(keep, near[kind].astype(WIDE), 0.0)
        totals.append(total.astype(HALF))
    out_ref[...] = (
        nt(query_grad[...], weights[0]) + nt(totals[0], weights[1]) + nt(totals[1], weights[2])
    ).astype(HALF)


def layer_kernel(seqs, *refs):
    step = pl.program_id(0)
    for seq in range(seqs):
        base, own, other = refs[seq * 3 : seq * 3 + 3]

        @pl.when(step == seq)
        def _():
            summed = own[...].astype(WIDE) + other[...].astype(WIDE)
            refs[-1][0] = (base[...] + summed).astype(HALF)


def final_kernel(seqs, *refs):
    x_ref, rows_ref = refs[:2]
    step = pl.program_id(0)
    for seq in range(seqs):
        residual_grad, own, other = refs[2 + seq * 3 : 5 + seq * 3]

        @pl.when(step == seq)
        def _():
            tensor = x_ref[0].astype(WIDE)
            spread = spread_of(tensor)
            unit = tensor * spread
            gradient = own[...].astype(WIDE) + other[...].astype(WIDE)
            scaled = gradient * rows_ref[14:15, :].astype(WIDE)
            refs[-1][0] = residual_grad[...] + spread * (
                scaled - unit * jnp.mean(scaled * unit, axis=-1, keepdims=True)
            )


def pack_kernel(flag, query, key, value, out, *refs):
    packed = refs[-1]
    deep, width = query.shape
    half = deep // 2
    start = pl.multiple_of(flag[0] * half, half)
    for place, matrix in enumerate((query, key, value, out)):
        packed[place * half : (place + 1) * half, :] = matrix[pl.ds(start, half), :].astype(HALF)
    rows = jnp.concatenate([ref[...] for ref in refs[:-1]], axis=0)
    rows = jnp.concatenate([rows, jnp.zeros((SMALL, width - deep), WIDE)], axis=1)
    packed[4 * half :, :] = rows.astype(HALF)


def cast_kernel(order, *refs):
    for kind in range(3):
        refs[-1][kind] = refs[kind][...].astype(HALF)


def order_kernel(index, *refs):
    parts, out = refs[:-1], refs[-1]
    size = len(parts)
    for distance, part in enumerate(parts):
        out[lax.rem(index[0] + size - distance, size)] = part[...]


def join_kernel(flag, own, other, out):
    half = own.shape[1]
    for place in range(own.shape[0]):
        first, second = own[place], other[place]
        start = place * 2 * half
        out[0, start : start + half, :] = jnp.where(flag[0] == 0, first, second)
        out[0, start + half : start + 2 * half, :] = jnp.where(flag[0] == 0, second, first)


def place_kernel(order, *refs):
    outs = refs[-3:]
    part = refs[0].shape[-1]
    for expert in range(2):
        for core, (own, across) in enumerate(
            (refs[4 * expert : 4 * expert + 2], refs[4 * expert + 2 : 4 * expert + 4])
        ):
            for far in range(2):
                lanes = pl.ds(pl.multiple_of(order[3 - far - 2 * core] * part, part), part)
                for kind in range(3):
                    if len(own.shape) == 4:
                        block = own[1 - far, kind].astype(WIDE) + across[far, kind].astype(WIDE)
                    else:
                        block = (across if far else own)[kind].astype(WIDE)
                    outs[kind][expert, :, lanes] = block


def unpack_kernel(slots, own, across, near, far, *outs):
    for place, out in enumerate(outs):
        block = jnp.where(slots[place] == 3, own[...].astype(WIDE), across[...].astype(WIDE))
        block = jnp.where(slots[place] == 1, near[...].astype(WIDE), block)
        block = jnp.where(slots[place] == 0, far[...].astype(WIDE), block)
        out[...] = block[: out.shape[0]]


def swap(block, axis):
    size = lax.axis_size(axis)
    return lax.ppermute(block, axis, [(i, i ^ 1) for i in range(size)])


def shift(block, axis, distance):
    size = lax.axis_size(axis)
    route = [(i, i + distance) for i in range(size) if 0 <= i + distance < size]
    return lax.ppermute(block, axis, route)


def pick(stack, index, axis=0):
    return lax.dynamic_index_in_dim(stack, index, axis, keepdims=False)


def scatter_rows(tensor, dimension):
    return lax.psum_scatter(tensor, "fsdp", scatter_dimension=dimension, tiled=True)


def ring(block, distance):
    size = lax.axis_size("fsdp")
    return lax.ppermute(block, "fsdp", [(i, (i + distance) % size) for i in range(size)])


def gather_blocks(block):
    size = lax.axis_size("fsdp")
    if size > 4:
        return lax.all_gather(block, "fsdp", axis=0)
    blocks = [block] + [ring(block, distance) for distance in range(1, size)]
    if block.shape[0] % 16 == 0:
        parts = whole(block.shape)
        out = (size,) + block.shape
        index = lax.axis_index("fsdp").reshape(1).astype(jnp.int32)
        return call(
            "order",
            order_kernel,
            (1,),
            [parts] * size,
            [(whole(out), struct(out, HALF))],
            prefetch=1,
        )(index, *blocks)[0]
    stacked = jnp.stack(blocks[::-1] * 2)
    start = size - 1 - lax.axis_index("fsdp")
    return lax.dynamic_slice_in_dim(stacked, start, size, axis=0)


def scatter_blocks(blocks):
    size = lax.axis_size("fsdp")
    if size > 4:
        return lax.psum_scatter(blocks, "fsdp", scatter_dimension=0)
    index = lax.axis_index("fsdp")
    total = pick(blocks, index).astype(WIDE)
    for distance in range(1, size):
        sent = pick(blocks, lax.rem(index + distance, size))
        total = total + ring(sent, distance).astype(WIDE)
    return total.astype(blocks.dtype)


def shards(
    block_in,
    cotangent,
    prev_logits,
    routes,
    segments,
    w_query,
    w_key,
    w_value,
    w_out,
    w_gate,
    w_up,
    w_down,
    router,
    const_proj,
    const_vec,
    norm_attn,
    norm_moe,
):
    seqs, count = block_in.shape[:2]
    width = w_query.shape[1]
    pairs = width // PAIR
    deep = w_gate.shape[1]
    hidden = w_gate.shape[2]
    hi, lo = lax.axis_index("hi"), lax.axis_index("lo")
    hi_size = lax.axis_size("hi")
    ctx = hi * 2 + lo
    ctx_size = hi_size * 2
    fsdp_size = lax.axis_size("fsdp")
    part = hidden // ctx_size
    order = jnp.stack([(1 - hi) * 2 + 1 - lo, hi * 2 + 1 - lo, (1 - hi) * 2 + lo, ctx]).astype(
        jnp.int32
    )

    flag = lo.reshape(1).astype(jnp.int32)

    positions = (ctx - 2) * count + jnp.arange(3 * count, dtype=jnp.int32)
    lane = jnp.arange(PAIR, dtype=jnp.int32)
    frequency = 10000.0 ** (-2.0 * (lane % (HD // 2)).astype(WIDE) / HD)
    turned = positions.astype(WIDE)[:, None] * frequency[None, :]
    cosine = jnp.cos(turned).reshape(3, count, PAIR)
    sine = (jnp.sin(turned) * jnp.where((lane & (HD // 2)) == 0, -1.0, 1.0)).reshape(3, count, PAIR)

    rank_rows, rank_columns = call(
        "rank",
        rank_kernel,
        (seqs,),
        [
            pl.BlockSpec((1, 2, count), lambda s: (s, 0, 0)),
            pl.BlockSpec((1, count, 2), lambda s: (s, 0, 0)),
        ],
        [
            (pl.BlockSpec((1, ALL, count), lambda s: (s, 0, 0)), struct((seqs, ALL, count), WIDE)),
            (pl.BlockSpec((1, count, ALL), lambda s: (s, 0, 0)), struct((seqs, count, ALL), WIDE)),
        ],
    )(routes.transpose(0, 2, 1), routes)

    half = deep // 2
    rows = 4 * half + SMALL
    rows = rows + -rows % 16
    narrow = (router.T, const_proj.T, const_vec.T, norm_attn[None, :], norm_moe[None, :])
    if half % 16 == 0:
        operands = (w_query, w_key, w_value, w_out) + narrow
        matrix_own = call(
            "pack",
            pack_kernel,
            (1,),
            [pl.BlockSpec(memory_space=pltpu.SMEM)] + [whole(array.shape) for array in operands],
            [(whole((rows, width)), struct((rows, width), HALF))],
        )(flag, *operands)[0]
    else:
        matrix_own = [
            lax.dynamic_slice_in_dim(w, lo * half, half, axis=0)
            for w in (w_query, w_key, w_value, w_out)
        ]
        small_rows = jnp.concatenate(narrow, axis=0)
        small_rows = jnp.pad(small_rows, ((0, rows - 4 * half - SMALL), (0, width - deep)))
        matrix_own = jnp.concatenate(matrix_own + [small_rows], axis=0).astype(HALF)

    def join_matrices(own):
        other = swap(own, "lo")
        if half % 16 == 0:
            block = pl.BlockSpec((fsdp_size, half, width), lambda kind: (0, kind, 0))
            return call(
                "join",
                join_kernel,
                (4,),
                [pl.BlockSpec(memory_space=pltpu.SMEM), block, block],
                [
                    (
                        pl.BlockSpec((1, D, width), lambda kind: (kind, 0, 0)),
                        struct((4, D, width), HALF),
                    )
                ],
            )(flag, own, other)[0]
        halves = [
            blocks[:, : 4 * half].reshape(fsdp_size, 4, half, width) for blocks in (own, other)
        ]
        halves = jnp.stack(
            [jnp.where(lo == 0, *halves), jnp.where(lo == 0, *halves[::-1])], axis=2
        )
        return halves.transpose(1, 0, 2, 3, 4).reshape(4, D, width)

    expert_own = call(
        "cast",
        cast_kernel,
        (EXPERTS,),
        [pl.BlockSpec((1, deep, part), lambda e, o: (e, 0, o[3]))] * 3,
        [
            (
                pl.BlockSpec((3, 1, deep, part), lambda e, o: (0, e, 0, 0)),
                struct((3, EXPERTS, deep, part), HALF),
            )
        ],
        prefetch=1,
    )(order, w_gate, w_up, w_down)[0]

    far_rows = shift(block_in, "hi", 1)
    matrix_own = gather_blocks(matrix_own)
    matrix_own, expert_own, far_rows, cosine, sine, rank_rows, rank_columns = lax.optimization_barrier(
        (matrix_own, expert_own, far_rows, cosine, sine, rank_rows, rank_columns)
    )
    expert_weights = lax.all_gather(expert_own, CTX + ("fsdp",), axis=0).reshape(
        ctx_size, fsdp_size, 3, EXPERTS, deep, part
    )
    if deep % 16:
        expert_weights = expert_weights.transpose(0, 2, 3, 1, 4, 5).reshape(
            ctx_size, 1, 3, EXPERTS, D, part
        )
    matrices = join_matrices(matrix_own)
    small_rows = matrix_own[:, 4 * half : 4 * half + SMALL, :deep]
    small_rows = small_rows.transpose(1, 0, 2).reshape(SMALL, D)
    near_rows = swap(jnp.where(lo == 1, far_rows, block_in), "lo")
    far_ids = shift(segments, "hi", 1)
    near_ids = swap(jnp.where(lo == 1, far_ids, segments), "lo")
    far_ids = jnp.where(hi == 0, -1, far_ids)
    near_ids = jnp.where(ctx == 0, -1, near_ids)
    key_ids = jnp.concatenate([far_ids, near_ids, segments], axis=1)[:, None, :]
    query_ids = segments[:, :, None]

    def project(rows, place, with_query, after=()):
        spread = struct((seqs, count, width), HALF)
        by_seq = pl.BlockSpec((1, count, width), lambda s: (s, 0, 0))
        by_row = pl.BlockSpec((1, count, D), lambda s: (s, 0, 0))
        kinds = 3 if with_query else 2
        return call(
            f"project{place}",
            functools.partial(project_kernel, with_query),
            (seqs,),
            [
                by_row,
                whole((SMALL, D)),
                fixed((1, count, PAIR), (place, 0, 0)),
                fixed((1, count, PAIR), (place, 0, 0)),
                whole((3, D, width)),
            ],
            [(by_row, struct((seqs, count, D), HALF))] + [(by_seq, spread)] * kinds,
            after=after,
        )(rows, small_rows, cosine, sine, matrices)

    normed0, key0, value0, query = project(block_in, 2, True, (near_rows,))
    normed1, key1, value1 = project(near_rows, 1, False)
    normed2, key2, value2 = project(far_rows, 0, False)

    def pair_block(seq):
        return pl.BlockSpec((1, count, PAIR), lambda p, seq=seq: (seq, 0, p))

    flat_pair = pl.BlockSpec((count, PAIR), lambda p: (0, p))
    window_scratch = [
        pltpu.VMEM((2, TILE, 4 * TILE), WIDE),
        pltpu.VMEM((3 * count, PAIR), HALF),
        pltpu.VMEM((3 * count, PAIR), HALF),
    ]
    product = 2 * 2 * TILE * 5 * TILE * 256 * 2 * pairs

    def attend(seq):
        return call(
            f"attend{seq}",
            attend_kernel,
            (pairs,),
            [pair_block(seq)] * 7
            + [
                fixed((1, count, 1), (seq, 0, 0)),
                fixed((1, 1, 3 * count), (seq, 0, 0)),
                pl.BlockSpec((1, D, PAIR), lambda p: (3, 0, p)),
            ],
            [
                (flat_pair, struct((count, width), HALF)),
                (flat_pair, struct((count, width), WIDE)),
                (whole((count, D)), struct((count, D), HALF)),
            ],
            window_scratch + [pltpu.VMEM((count, D), WIDE)],
        )(query, key2, key1, key0, value2, value1, value0, query_ids, key_ids, matrices)

    mixed, logs, attended, attended_other = [], [], [], []
    for seq in range(seqs):
        one, two, three = attend(seq)
        mixed.append(one)
        logs.append(two)
        attended.append(three)
        attended_other.append(swap(three, "tp"))

    flat = whole((count, D))
    flat_small = whole((count, SIDE))

    def one_seq(seq, columns):
        return fixed((1, count, columns), (seq, 0, 0))

    tiles = 4
    tile = count // tiles

    def tile_rows(columns):
        return pl.BlockSpec((tile, columns), lambda t: (t, 0))

    def tile_seq(seq, columns):
        return pl.BlockSpec((1, tile, columns), lambda t: (seq, t, 0))

    routed, targets, bases, earlies = [], [], [], []
    for seq in range(seqs):
        results = call(
            f"route{seq}",
            route_kernel,
            (tiles,),
            [
                tile_seq(seq, D),
                tile_rows(D),
                tile_rows(D),
                tile_seq(seq, D),
                whole((SMALL, D)),
                tile_seq(seq, 2),
                tile_seq(seq, ALL),
            ],
            [
                (tile_rows(D), struct((count, D), HALF)),
                (tile_rows(SIDE), struct((count, SIDE), WIDE)),
                (tile_rows(D), struct((count, D), WIDE)),
                (whole((8, D)), struct((8, D), WIDE)),
            ],
        )(
            block_in,
            attended[seq],
            attended_other[seq],
            cotangent,
            small_rows,
            routes,
            prev_logits,
        )
        for kept, result in zip((routed, targets, bases, earlies), results, strict=True):
            kept.append(result)

    slots = seqs * MOST
    weight_shape = expert_weights.shape
    weight_block = (1,) + weight_shape[1:2] + (3, 1) + weight_shape[4:]
    piece = (1, 3, D, part)
    out_slots, grad_slots, held, crossing = [], [], [], []
    scattered = [None] * EXPERTS

    def finish(expert, total):
        scattered[expert] = scatter_rows(total, total.ndim - 2)

    slot_out = (
        pl.BlockSpec((1, slots, D), lambda e: (e, 0, 0)),
        struct((EXPERTS, slots, D), HALF),
    )
    slot_rows, slot_cots = call(
        "dispatch",
        dispatch_kernel,
        (EXPERTS,),
        [flat, flat, whole((seqs, count, D)), flat_small, flat_small, whole((seqs, ALL, count))],
        [slot_out, slot_out],
    )(routed[0], routed[1], cotangent, targets[0], targets[1], rank_rows)
    for expert in range(EXPERTS):
        theirs, mine, one, two, *totals = call(
            f"expert{expert}",
            expert_kernel,
            (ctx_size,),
            [
                fixed((1, slots, D), (expert, 0, 0)),
                fixed((1, slots, D), (expert, 0, 0)),
                pl.BlockSpec(
                    weight_block, lambda j, o, expert=expert: (o[j], 0, 0, expert, 0, 0)
                ),
            ],
            [
                (
                    pl.BlockSpec(piece, lambda j, o: (jnp.minimum(j, 1), 0, 0, 0)),
                    struct((2, 3, D, part), HALF),
                ),
                (
                    pl.BlockSpec(piece, lambda j, o: (jnp.maximum(j - 2, 0), 0, 0, 0)),
                    struct((2, 3, D, part), HALF),
                ),
                (whole((slots, D)), struct((slots, D), HALF)),
                (whole((slots, D)), struct((slots, D), HALF)),
            ],
            [
                pltpu.VMEM((D, slots), HALF),
                pltpu.VMEM((D, slots), HALF),
                pltpu.VMEM((slots, D), WIDE),
                pltpu.VMEM((slots, D), WIDE),
            ],
            prefetch=1,
            side=[side_sum(ctx_size, held[expert - 2])] if expert >= 2 else (),
            after=out_slots[-1:],
        )(order, slot_rows, slot_cots, expert_weights)
        out_slots.append(one)
        grad_slots.append(two)
        held.append((mine, swap(theirs, "lo")))
        if totals:
            finish(expert - 2, totals[0].reshape(2, 3, D, part))

    def couple_of(place):
        return scattered[place], swap(scattered[place], "hi")

    back, back_other, sums, sums_other = [], [], [], []
    for seq in range(seqs):
        slot_block = fixed((MOST, D), (seq, 0))
        one, two, sent = call(
            f"combine{seq}",
            combine_kernel,
            (tiles,),
            [slot_block] * (2 * EXPERTS)
            + [tile_seq(seq, ALL), tile_rows(SIDE), tile_seq(seq, D)],
            [
                (tile_rows(D + PAIR), struct((count, D + PAIR), HALF)),
                (tile_rows(D), struct((count, D), HALF)),
            ],
            side=[side_sum(tiles, held[2 + seq], 0)],
        )(*out_slots, *grad_slots, rank_columns, targets[seq], cotangent)
        back.append(one)
        sums.append(two)
        back_other.append(swap(one, "tp"))
        crossing.append(swap(sent, "hi"))

    residual_grads, cots, mixed_grads, extras, talls = [], [], [], [], []
    def turn(seq):
        results = call(
            f"turn{seq}",
            turn_kernel,
            (tiles,),
            [
                tile_seq(seq, D),
                tile_rows(D),
                tile_rows(D),
                tile_seq(seq, D),
                tile_rows(D + PAIR),
                tile_rows(D + PAIR),
                tile_rows(SIDE),
                whole((SMALL, D)),
                fixed((1, D, width), (3, 0, 0)),
            ],
            [
                (tile_rows(D), struct((count, D), WIDE)),
                (tile_rows(D), struct((count, D), HALF)),
                (tile_rows(width), struct((count, width), HALF)),
                (whole((8, D)), struct((8, D), WIDE)),
                (tile_rows(PAIR), struct((count, PAIR), HALF)),
            ],
            side=[side_sum(tiles, held[2], 1, (crossing[0],))] if seq else (),
            after=(query_grads[0],) if seq else (),
        )(
            block_in,
            attended[seq],
            attended_other[seq],
            cotangent,
            back[seq],
            back_other[seq],
            targets[seq],
            small_rows,
            matrices,
        )
        for kept, result in zip(
            (residual_grads, cots, mixed_grads, extras, talls), results[:5], strict=True
        ):
            kept.append(result)
        if seq:
            finish(2, results[5].reshape(3, D, part))

    query_grads, grads2, grads1, grads0 = [], [], [], []
    pair_out = (
        pl.BlockSpec((2, count, PAIR), lambda p: (0, 0, p)),
        struct((2, count, width), HALF),
    )
    table = whole((3, count, PAIR))
    near_grads, far_grads, sents = [], [], []

    def attend_back(seq):
        results = call(
            f"back{seq}",
            attend_back_kernel,
            (pairs,),
            [pair_block(seq)] * 7
            + [
                fixed((1, count, 1), (seq, 0, 0)),
                fixed((1, 1, 3 * count), (seq, 0, 0)),
                flat_pair,
                flat_pair,
                flat_pair,
                table,
                table,
            ],
            [(flat_pair, struct((count, width), HALF))] + [pair_out] * 3,
            window_scratch
            + [pltpu.VMEM((PAIR, 3 * count), WIDE), pltpu.VMEM((PAIR, 3 * count), WIDE)],
            after=(sents[0], sums_other[0]) if seq else (crossing[0],),
            side=[side_sum(pairs, held[3], 1, (crossing[1],))] if seq else (),
        )(
            query,
            key2,
            key1,
            key0,
            value2,
            value1,
            value0,
            query_ids,
            key_ids,
            mixed_grads[seq],
            mixed[seq],
            logs[seq],
            cosine,
            sine,
        )
        for kept, result in zip((query_grads, grads2, grads1, grads0), results[:4], strict=True):
            kept.append(result)
        near_grads.append(swap(results[2], "lo"))
        if seq:
            finish(3, results[4].reshape(3, D, part))

    def send_back(seq, after):
        sents.append(
            call(
                f"relay{seq}",
                relay_kernel,
                (2,),
                [pl.BlockSpec(memory_space=pltpu.SMEM)]
                + [pl.BlockSpec((1, count, width), lambda kind: (kind, 0, 0))] * 2,
                [
                    (
                        pl.BlockSpec((1, count, width), lambda kind: (kind, 0, 0)),
                        struct((2, count, width), HALF),
                    )
                ],
                after=after,
            )(flag, grads2[seq], near_grads[seq])[0]
        )
        far_grads.append(shift(sents[seq], "hi", -1))

    def enter(seq, after):
        one = call(
            f"input{seq}",
            input_kernel,
            (tiles // 2,),
            [
                pl.BlockSpec((2 * tile, width), lambda t: (t, 0)),
            ]
            + [pl.BlockSpec((2, 2 * tile, width), lambda t: (0, t, 0))] * 3
            + [
                pl.BlockSpec(memory_space=pltpu.SMEM),
                whole((3, D, width)),
            ],
            [
                (
                    pl.BlockSpec((2 * tile, D), lambda t: (t, 0)),
                    struct((count, D), HALF),
                )
            ],
            after=after,
        )(query_grads[seq], grads0[seq], near_grads[seq], far_grads[seq], flag, matrices)[0]
        input_parts.append(one)
        input_others.append(swap(one, "tp"))

    input_parts, input_others = [], []
    def send_sums(seq):
        sums[seq], mixed_grads[seq] = lax.optimization_barrier((sums[seq], mixed_grads[seq]))
        sums_other.append(swap(sums[seq], "tp"))

    turn(0)
    send_sums(0)
    attend_back(0)
    couples = [couple_of(0)]
    turn(1)
    send_sums(1)
    columns = D // 2

    def by_column(rows):
        return pl.BlockSpec((rows, columns), lambda t, *_: (0, t))

    def weight_operands(seq):
        return (
            [normed2, normed1, normed0, query_grads[seq], grads2[seq], grads1[seq], grads0[seq]]
            + [cots[seq], mixed[seq], talls[seq], routed[seq], extras[seq], earlies[seq]]
        )

    def weight_specs(seq):
        return (
            [pl.BlockSpec((1, count, columns), lambda t, *_: (seq, 0, t))] * 3
            + [whole((count, width))]
            + [whole((2, count, width))] * 3
            + [by_column(count), whole((count, width)), whole((count, PAIR))]
            + [by_column(count), by_column(8), by_column(8)]
        )

    first_sums = call(
        "first",
        first_weight_kernel,
        (2,),
        weight_specs(0),
        [
            (
                pl.BlockSpec((4, columns, width), lambda t, *_: (0, t, 0)),
                struct((4, D, width), WIDE),
            ),
            (by_column(SMALL), struct((SMALL, D), WIDE)),
        ],
        after=(extras[1],),
    )(*weight_operands(0))
    send_back(0, (first_sums[1],))
    attend_back(1)
    enter(0, (query_grads[1],))
    couples.append(couple_of(1))
    send_back(1, (input_parts[0],))
    couples.append(couple_of(2))

    def half_map(seq):
        last = 1 if seq == 0 else 0
        return lambda s, t: (jnp.where(s == seq, t, last), 0)

    part_shape = (2, D + SMALL, width)
    slots_of = jnp.stack(
        [2 * (lo == place % 2).astype(jnp.int32) + (hi == place // 2) for place in range(4)]
    ).astype(jnp.int32)
    theirs, mine = call(
        "weight",
        weight_kernel,
        (2,),
        weight_specs(1)
        + [
            pl.BlockSpec((4, columns, width), lambda t, *_: (0, t, 0)),
            by_column(SMALL),
            pl.BlockSpec((3, columns, width), lambda t, *_: (0, t, 0)),
            by_column(SMALL),
        ],
        [(whole(part_shape), struct(part_shape, HALF))] * 2,
        prefetch=1,
        after=(sents[1],),
    )(slots_of, *weight_operands(1), *first_sums, matrices, small_rows)
    received = swap(theirs, "lo")
    enter(1, (input_others[0],))
    received, input_parts[1] = lax.optimization_barrier((received, input_parts[1]))
    input_others[1] = swap(input_parts[1], "tp")

    rest_shape = (D + 2 * SMALL, width)
    sent, kept = call(
        "fold",
        fold_kernel,
        (1,),
        [whole(part_shape)] * 2,
        [(whole(rest_shape), struct(rest_shape, HALF))] * 2,
    )(mine, received)
    crossed = swap(sent, "hi")
    layer_out = call(
        "layer",
        functools.partial(layer_kernel, seqs),
        (seqs, 2),
        [
            pl.BlockSpec((2 * tile, D), half_map(seq))
            for seq in range(seqs)
            for _ in range(3)
        ],
        [
            (
                pl.BlockSpec((1, 2 * tile, D), lambda s, t: (s, t, 0)),
                struct((seqs, count, D), HALF),
            )
        ],
        after=(input_parts[1],),
    )(*[array for seq in range(seqs) for array in (bases[seq], sums[seq], sums_other[seq])])[0]
    if fsdp_size <= 4:
        block = (deep + SMALL, width)
        blocks = list(
            call(
                "split",
                split_kernel,
                (1,),
                [whole(rest_shape)] * 2,
                [(whole(block), struct(block, HALF))] * fsdp_size,
                prefetch=1,
                after=(layer_out, input_others[1]),
            )(lax.axis_index("fsdp").reshape(1).astype(jnp.int32), kept, crossed)
        )
        own = blocks[0].astype(WIDE)
        for distance in range(1, fsdp_size):
            own = own + ring(blocks[distance], distance).astype(WIDE)
        own = own.astype(HALF)
    else:
        total = kept + crossed
        rest = jnp.concatenate([total[D : D + SMALL], total[D + SMALL :]], axis=1)
        rest = rest.reshape(SMALL, fsdp_size, deep).transpose(1, 0, 2)
        rest = jnp.pad(rest, ((0, 0), (0, 0), (0, width - deep)))
        own = scatter_blocks(
            jnp.concatenate([total[:D].reshape(fsdp_size, deep, width), rest], axis=1)
        )
    couples.append(couple_of(3))

    by_tile = pl.BlockSpec((1, tile, D), lambda s, t: (s, t, 0))
    operands, specs = [block_in, small_rows], [by_tile, whole((SMALL, D))]
    for seq in range(seqs):
        operands += [residual_grads[seq], input_parts[seq], input_others[seq]]
        last = tiles - 1 if seq == 0 else 0
        specs += [
            pl.BlockSpec(
                (tile, D), lambda s, t, seq=seq, last=last: (jnp.where(s == seq, t, last), 0)
            )
        ] * 3
    grad_input = call(
        "final",
        functools.partial(final_kernel, seqs),
        (seqs, tiles),
        specs,
        [
            (by_tile, struct((seqs, count, D), WIDE)),
        ],
    )(*operands)[0]

    own, grad_input = lax.optimization_barrier((own, grad_input))
    small = own[deep:, :deep].astype(WIDE)
    norm_grad = small[14] + swap(small[14], "tp")
    across = swap(own, "hi")
    sources = (own, across, swap(own, "lo"), swap(across, "lo"))

    result = struct((EXPERTS, deep, hidden), WIDE)
    grads = None
    for group in (couples[:2], couples[2:]):
        operands = []
        for couple in group:
            operands += list(couple) + [swap(array, "lo") for array in couple]
        previous = [] if grads is None else list(grads)
        grads = call(
            f"place{len(previous)}",
            place_kernel,
            (1,),
            [whole(array.shape) for array in operands]
            + [pl.BlockSpec(memory_space=pl.ANY)] * len(previous),
            [(fixed((2, deep, hidden), (1 if previous else 0, 0, 0)), result)] * 3,
            prefetch=1,
            aliases={1 + len(operands) + kind: kind for kind in range(3)} if previous else None,
            after=() if previous else (input_parts[1],),
        )(order, *operands, *previous)

    matrix = struct((deep, width), WIDE)
    matrix_grads = call(
        "unpack",
        unpack_kernel,
        (1,),
        [whole(own.shape)] * 4,
        [(whole((deep, width)), matrix)] * 4,
        prefetch=1,
        after=(grads[0],),
    )(slots_of, *sources)

    return (
        layer_out,
        grad_input,
        *matrix_grads,
        *grads,
        small[0:8].T,
        small[8:12].T,
        small[12:14].T,
        norm_grad,
        small[15],
    )


def solution(mesh):
    sizes = mesh.shape
    inner = Mesh(
        mesh.devices.reshape(sizes["fsdp"], sizes["ctx"] // 2, 2, sizes["tp"]),
        ("fsdp", "hi", "lo", "tp"),
    )
    rows = P("fsdp", CTX, None)
    matrix = P("fsdp", "tp")
    experts = P(None, "fsdp", "tp")
    narrow = P("fsdp", None)
    vector = P("fsdp")
    return jax.shard_map(
        shards,
        mesh=inner,
        in_specs=(rows,) * 4
        + (P("fsdp", CTX),)
        + (matrix,) * 4
        + (experts,) * 3
        + (narrow,) * 3
        + (vector,) * 2,
        out_specs=(rows,) * 2
        + (matrix,) * 4
        + (experts,) * 3
        + (narrow,) * 3
        + (vector,) * 2,
        check_vma=False,
    )
```

```python
import functools

import jax
import jax.numpy as jnp
from jax import lax
from jax.experimental import pallas as pl
from jax.experimental.pallas import tpu as pltpu
from jax.sharding import Mesh
from jax.sharding import PartitionSpec as P

D = 768
HEADS = 12
HD = 64
EXPERTS = 4
ALL = 8
WINDOW = 1024
MOST = 192

EPSILON = 1e-06
MASKED = -1e30

CTX = ("hi", "lo")
HALF = jnp.bfloat16
WIDE = jnp.float32
TILE = 256
PAIR = 2 * HD
SMALL = 16
SIDE = 32
MIB = 1 << 20
COSTS = {
    "project": 10,
    "attend": 2,
    "route": 40,
    "expert0": 0,
    "expert1": 10,
    "expert2": 1,
    "expert3": 1,
    "combine0": 20,
    "combine1": 5,
    "turn0": 2,
    "turn1": 40,
    "back0": 10,
    "back1": 1,
    "relay0": 80,
    "relay1": 0,
    "input0": 5,
    "input1": 80,
    "weight": 20,
    "layer": 0,
    "fold": 40,
    "split": 10,
    "final": 20,
    "place0": 0,
    "place3": 0,
    "unpack": 80,
    "dispatch": 5,
    "first": 7,
}


def nn(a, b):
    return jnp.dot(a, b, preferred_element_type=WIDE)


def nt(a, b):
    return lax.dot_general(a, b, (((1,), (1,)), ((), ())), preferred_element_type=WIDE)


def call(
    tag,
    body,
    grid,
    ins,
    outs,
    scratch=(),
    prefetch=0,
    aliases=None,
    after=(),
    side=(),
):
    operands = [array for job in side for array in job[0]]
    specs = [spec for job in side for spec in job[1]]
    kind = tag.rstrip("0123456789")
    own = prefetch + len(ins)
    first = own + len(operands) + len(after)

    def inner(*refs):
        start, results = own, first + len(outs)
        for place, job in enumerate(side):
            total = refs[start][...].astype(WIDE)
            for ref in refs[start + 1 : start + len(job[0])]:
                total = total + ref[...].astype(WIDE)
            refs[results + place][...] = total.astype(HALF)
            start += len(job[0])
        body(*refs[:own], *refs[first:results], *refs[results + len(side) :])

    all_outs = list(outs) + [job[2] for job in side]
    grid_spec = pltpu.PrefetchScalarGridSpec(
        num_scalar_prefetch=prefetch,
        grid=grid,
        in_specs=list(ins) + specs + [pl.BlockSpec(memory_space=pl.ANY)] * len(after),
        out_specs=[spec for spec, _ in all_outs],
        scratch_shapes=list(scratch),
    )
    kernel = pl.pallas_call(
        inner,
        grid_spec=grid_spec,
        name=tag,
        out_shape=[shape for _, shape in all_outs],
        input_output_aliases=aliases or {},
        compiler_params=pltpu.CompilerParams(
            dimension_semantics=("arbitrary",) * len(grid), vmem_limit_bytes=64 * MIB
        ),
        cost_estimate=pl.CostEstimate(
            flops=int(COSTS.get(tag, COSTS.get(kind, 2)) * 1e9), bytes_accessed=0, transcendentals=0
        ),
    )
    return lambda *arrays: kernel(*arrays, *operands, *after)


def side_sum(steps, stacks, index=None, plain=()):
    flat = [stack.reshape(-1, stack.shape[-1]) for stack in stacks]
    rows, columns = flat[0].shape
    rows = rows if index is None else rows // stacks[0].shape[0]
    start = 0 if index is None else index * steps
    block = (rows // steps, columns)
    out = pl.BlockSpec(block, lambda step, *_: (step, 0))
    specs = [pl.BlockSpec(block, lambda step, *_: (start + step, 0))] * len(flat)
    flat += [array.reshape(rows, columns) for array in plain]
    specs += [out] * len(plain)
    return flat, specs, (out, struct((rows, columns), HALF))


def whole(shape):
    zeros = (0,) * len(shape)
    return pl.BlockSpec(shape, lambda *_: zeros)


def fixed(block, place):
    return pl.BlockSpec(block, lambda *_: place)


def struct(shape, dtype):
    return jax.ShapeDtypeStruct(shape, dtype)


def spread_of(tensor):
    return lax.rsqrt(jnp.mean(tensor * tensor, axis=-1, keepdims=True) + EPSILON)


def partner(tensor):
    lane = lax.broadcasted_iota(jnp.int32, tensor.shape, 1)
    return jnp.where(
        (lane & (HD // 2)) == 0,
        pltpu.roll(tensor, PAIR - HD // 2, 1),
        pltpu.roll(tensor, HD // 2, 1),
    )


def rank_kernel(routes_t, routes, rank_rows, rank_columns):
    count = routes.shape[1]
    down = lax.broadcasted_iota(jnp.int32, (count, count), 0)
    across = lax.broadcasted_iota(jnp.int32, (count, count), 1)
    before = jnp.where(down < across, 1.0, 0.0).astype(HALF)
    after = jnp.where(across < down, 1.0, 0.0).astype(HALF)
    row_target = lax.broadcasted_iota(jnp.int32, (ALL, count), 0)
    names = (routes_t[0, 0:1, :] == row_target) | (routes_t[0, 1:2, :] == row_target)
    ranks = nn(jnp.where(names, 1.0, 0.0).astype(HALF), before)
    rank_rows[0] = jnp.where(names, ranks, -1.0)
    column_target = lax.broadcasted_iota(jnp.int32, (count, ALL), 1)
    named = (routes[0, :, 0:1] == column_target) | (routes[0, :, 1:2] == column_target)
    ranked = nn(after, jnp.where(named, 1.0, 0.0).astype(HALF))
    rank_columns[0] = jnp.where(named, ranked, -1.0)


def project_kernel(with_query, *refs):
    x_ref, rows_ref, cos_ref, sin_ref, weights = refs[:5]
    outs = refs[5:]
    tensor = x_ref[0].astype(WIDE)
    unit = tensor * spread_of(tensor)
    normed = (unit * rows_ref[14:15, :].astype(WIDE)).astype(HALF)
    outs[0][0] = normed
    cosine, sine = cos_ref[0], sin_ref[0]

    def turned(matrix, out, scale):
        flat = nn(normed, weights[matrix])
        for piece in range(flat.shape[1] // PAIR):
            lanes = slice(piece * PAIR, (piece + 1) * PAIR)
            part = flat[:, lanes]
            result = (part * cosine + partner(part) * sine).astype(HALF)
            out[0, :, lanes] = result if scale is None else result * scale

    turned(1, outs[1], None)
    outs[2][0] = nn(normed, weights[2]).astype(HALF)
    if with_query:
        turned(0, outs[3], jnp.asarray(HD ** (-0.5), HALF))


def fill_bias(query_ids, key_ids, bias):
    upper = upper_of()
    for tile in range(2):
        ids = query_ids[0, tile * TILE : (tile + 1) * TILE, :]
        first = key_ids[0, :, tile * TILE : (tile + 1) * TILE]
        last = key_ids[0, :, (tile + 4) * TILE : (tile + 5) * TILE]
        mixed = jnp.where(upper, first, last)
        bias[tile, :, :TILE] = jnp.where(mixed == ids, 0.0, MASKED)
        inner = key_ids[0, :, (tile + 1) * TILE : (tile + 4) * TILE]
        bias[tile, :, TILE:] = jnp.where(inner == ids, 0.0, MASKED)


def upper_of():
    down = lax.broadcasted_iota(jnp.int32, (TILE, TILE), 0)
    across = lax.broadcasted_iota(jnp.int32, (TILE, TILE), 1)
    return across > down


def head_lanes(head, rows):
    lane = lax.broadcasted_iota(jnp.int32, (rows, PAIR), 1)
    return (lane < HD) if head == 0 else (lane >= HD)


def folded(upper, spread):
    span = spread.shape[1]
    return (
        jnp.where(upper, spread[:, :TILE], spread[:, span - TILE :]),
        spread[:, TILE : span - TILE],
    )


def unfolded(upper, ends, middle):
    return jnp.concatenate(
        [jnp.where(upper, ends, 0.0), middle, jnp.where(upper, 0.0, ends)], axis=1
    ).astype(HALF)


def load_window(parts, window):
    rows = parts[0].shape[1]
    for place, part in enumerate(parts):
        window[place * rows : (place + 1) * rows, :] = part[0]


def attend_kernel(
    query, k2, k1, k0, v2, v1, v0, query_ids, key_ids, w_out, mixed, logs, attended, bias, keys, values, total
):
    step = pl.program_id(0)

    @pl.when(step == 0)
    def _():
        fill_bias(query_ids, key_ids, bias)

    load_window((k2, k1, k0), keys)
    load_window((v2, v1, v0), values)
    upper = upper_of()
    span = 5 * TILE
    for tile in range(2):
        rows = slice(tile * TILE, (tile + 1) * TILE)
        window = slice(tile * TILE, tile * TILE + span)
        results, totals = [], []
        for head in range(2):
            chosen = head_lanes(head, TILE)
            own = jnp.where(chosen, query[0, rows, :], jnp.zeros((), HALF))
            ends, middle = folded(upper, nt(own, keys[window, :]))
            ends = ends + bias[tile, :, :TILE]
            middle = middle + bias[tile, :, TILE:]
            highest = jnp.maximum(
                jnp.max(ends, axis=-1, keepdims=True), jnp.max(middle, axis=-1, keepdims=True)
            )
            ends = jnp.exp(ends - highest)
            middle = jnp.exp(middle - highest)
            summed = jnp.sum(ends, axis=-1, keepdims=True) + jnp.sum(middle, axis=-1, keepdims=True)
            out = nn(unfolded(upper, ends, middle), values[window, :]) / summed
            results.append(out)
            totals.append(jnp.broadcast_to(highest + jnp.log(summed), (TILE, PAIR)))
        chosen = head_lanes(0, TILE)
        mixed[rows, :] = jnp.where(chosen, results[0], results[1]).astype(HALF)
        logs[rows, :] = jnp.where(chosen, totals[0], totals[1])
    product = nt(mixed[...], w_out[0])

    @pl.when(step == 0)
    def _():
        total[...] = product

    @pl.when(step > 0)
    def _():
        total[...] += product

    @pl.when(step == pl.num_programs(0) - 1)
    def _():
        attended[...] = total[...].astype(HALF)


def residual_of(x_ref, own, other):
    return x_ref[0].astype(WIDE) + (own[...].astype(WIDE) + other[...].astype(WIDE))


def softmax_two(a, b):
    highest = jnp.maximum(a, b)
    a, b = jnp.exp(a - highest), jnp.exp(b - highest)
    return a / (a + b), b / (a + b)


def mix_back(mix, one, two):
    inner = mix[0] * one + mix[1] * two
    return mix[0] * (one - inner), mix[1] * (two - inner)


def put(total, columns, first):
    lane = lax.broadcasted_iota(jnp.int32, total.shape, 1)
    for place, column in enumerate(columns):
        total = total + jnp.where(lane == first + place, column, 0.0)
    return total


def route_kernel(
    x_ref, own, other, upstream, rows_ref, routes, prev, routed_ref, side_ref, base_ref, small_ref
):
    residual = residual_of(x_ref, own, other)
    unit = residual * spread_of(residual)
    routed = (unit * rows_ref[15:16, :].astype(WIDE)).astype(HALF)
    routed_ref[...] = routed
    routed_wide = routed.astype(WIDE)
    scores = nt(routed, rows_ref[...])
    logits = scores[:, :ALL] + prev[0]
    target = lax.broadcasted_iota(jnp.int32, logits.shape, 1)
    picked = [routes[0, :, place : place + 1] == target for place in range(2)]
    chosen = [jnp.sum(jnp.where(one, logits, 0.0), axis=-1, keepdims=True) for one in picked]
    chosen = softmax_two(*chosen)
    weights = jnp.where(picked[0], chosen[0], 0.0) + jnp.where(picked[1], chosen[1], 0.0)
    copy, one, two = (weights[:, place : place + 1] for place in (5, 6, 7))
    first = softmax_two(scores[:, 8:9], scores[:, 9:10])
    second = softmax_two(scores[:, 10:11], scores[:, 11:12])
    vector = [rows_ref[12 + place : 13 + place, :].astype(WIDE) for place in range(2)]
    direct = copy + one * first[0] + two * second[0]
    base_ref[...] = (
        residual + routed_wide * direct + (one * first[1]) * vector[0] + (two * second[1]) * vector[1]
    )
    up_half = upstream[0]
    up = up_half.astype(WIDE)
    dot = jnp.sum(up * routed_wide, axis=-1, keepdims=True)
    dots = nt(up_half, rows_ref[...])
    dot_one, dot_two = dots[:, 12:13], dots[:, 13:14]
    side = put(
        jnp.zeros(side_ref.shape, WIDE),
        (dot, first[0] * dot + first[1] * dot_one, second[0] * dot + second[1] * dot_two),
        ALL + EXPERTS + 1,
    )
    side = put(side, mix_back(first, one * dot, one * dot_one), 16)
    side = put(side, mix_back(second, two * dot, two * dot_two), 18)
    side = put(side, (direct,), 20)
    side_ref[...] = side
    side_ref[:, :ALL] = weights
    step = pl.program_id(0)
    sums = jnp.concatenate(
        [
            jnp.sum((one * first[1]) * up, axis=0, keepdims=True),
            jnp.sum((two * second[1]) * up, axis=0, keepdims=True),
            jnp.zeros((6, D), WIDE),
        ],
        axis=0,
    )

    @pl.when(step == 0)
    def _():
        small_ref[...] = sums

    @pl.when(step > 0)
    def _():
        small_ref[...] += sums


def dispatch_kernel(routed_a, routed_b, upstream, targets_a, targets_b, ranks, rows, cots):
    expert = pl.program_id(0)
    count = routed_a.shape[0]
    slot = lax.broadcasted_iota(jnp.int32, (MOST, count), 0).astype(WIDE)
    for seq, (routed, targets) in enumerate(((routed_a, targets_a), (routed_b, targets_b))):
        place = slice(seq * MOST, (seq + 1) * MOST)
        spread = jnp.where(slot == ranks[seq, pl.ds(expert, 1), :], 1.0, 0.0).astype(HALF)
        rows[0, place, :] = nn(spread, routed[...]).astype(HALF)
        lane = lax.broadcasted_iota(jnp.int32, targets.shape, 1)
        weight = jnp.sum(jnp.where(lane == expert, targets[...], 0.0), axis=-1, keepdims=True)
        weighted = weight * upstream[seq].astype(WIDE)
        cots[0, place, :] = nn(spread, weighted.astype(HALF)).astype(HALF)


def expert_kernel(
    order, rows, cots, weights, theirs, mine, out_slots, grad_slots, rows_t, cots_t, out_total, grad_total
):
    step = pl.program_id(0)

    @pl.when(step == 0)
    def _():
        rows_t[...] = rows[0].T
        cots_t[...] = cots[0].T

    here = [weights[0, :, kind, 0].reshape(D, weights.shape[-1]) for kind in range(3)]
    gate = nn(rows[0], here[0])
    up = nn(rows[0], here[1])
    sigmoid = 1.0 / (1.0 + jnp.exp(-gate))
    silu = gate * sigmoid
    activated = (silu * up).astype(HALF)
    activated_grad = nn(cots[0], here[2])
    up_grad = (activated_grad * silu).astype(HALF)
    gate_grad = (activated_grad * up * sigmoid * (1.0 + gate * (1.0 - sigmoid))).astype(HALF)
    out_part = nt(activated, here[2])
    grad_part = nt(gate_grad, here[0]) + nt(up_grad, here[1])

    @pl.when(step == 0)
    def _():
        out_total[...] = out_part
        grad_total[...] = grad_part

    @pl.when(step > 0)
    def _():
        out_total[...] += out_part
        grad_total[...] += grad_part

    grads = (nn(rows_t[...], gate_grad), nn(rows_t[...], up_grad), nn(cots_t[...], activated))

    @pl.when(step < 2)
    def _():
        for kind in range(3):
            theirs[0, kind] = grads[kind].astype(HALF)

    @pl.when(step >= 2)
    def _():
        for kind in range(3):
            mine[0, kind] = grads[kind].astype(HALF)

    @pl.when(step == pl.num_programs(0) - 1)
    def _():
        out_slots[...] = out_total[...].astype(HALF)
        grad_slots[...] = grad_total[...].astype(HALF)


def combine_kernel(*refs):
    outs, grads = refs[:EXPERTS], refs[EXPERTS : 2 * EXPERTS]
    ranks, targets, upstream, back_ref, sum_ref = refs[2 * EXPERTS :]
    count = upstream.shape[1]
    slot = lax.broadcasted_iota(jnp.int32, (count, MOST), 1).astype(WIDE)
    wide = upstream[0].astype(WIDE)
    back = total = None
    lane = lax.broadcasted_iota(jnp.int32, (count, PAIR), 1)
    dots = jnp.zeros((count, PAIR), WIDE)
    for expert in range(EXPERTS):
        spread = jnp.where(slot == ranks[0, :, expert : expert + 1], 1.0, 0.0).astype(HALF)
        part = nn(spread, grads[expert][...])
        back = part if back is None else back + part
        part = nn(spread, outs[expert][...])
        dots = dots + jnp.where(lane == expert, jnp.sum(part * wide, axis=-1, keepdims=True), 0.0)
        part = part * targets[:, expert : expert + 1]
        total = part if total is None else total + part
    back_ref[:, :D] = back.astype(HALF)
    main = dots.astype(HALF)
    rest = pltpu.roll(dots - main.astype(WIDE), ALL, 1)
    back_ref[:, D:] = jnp.where(lane < ALL, main.astype(WIDE), rest).astype(HALF)
    sum_ref[...] = total.astype(HALF)


def turn_kernel(
    x_ref, own, other, upstream, back_own, back_other, side, rows_ref, w_out, residual_grad_ref, cot_ref,
    mixed_grad_ref, small_ref, tall_ref
):
    residual = residual_of(x_ref, own, other)
    spread = spread_of(residual)
    unit = residual * spread
    up = upstream[0].astype(WIDE)
    weights = side[:, :ALL]
    halves = back_own[:, D:].astype(WIDE) + back_other[:, D:].astype(WIDE)
    halves = halves[:, :ALL] + halves[:, ALL : 2 * ALL]
    lane = lax.broadcasted_iota(jnp.int32, halves.shape, 1)
    dots = jnp.where(lane < EXPERTS, halves, 0.0) + side[:, ALL : 2 * ALL]
    logit_grad = weights * (dots - jnp.sum(weights * dots, axis=-1, keepdims=True))
    rest = jnp.concatenate([side[:, 16:20], jnp.zeros((up.shape[0], 4), WIDE)], axis=1)
    tall = jnp.concatenate([logit_grad, rest], axis=1).astype(HALF)
    tall_ref[...] = jnp.concatenate(
        [tall, jnp.zeros((up.shape[0], PAIR - SMALL), HALF)], axis=1
    )
    back = back_own[:, :D].astype(WIDE) + back_other[:, :D].astype(WIDE)
    routed_grad = back + nn(tall, rows_ref[...]) + up * side[:, 20:21]
    step = pl.program_id(0)
    sums = jnp.sum(routed_grad * unit, axis=0, keepdims=True)
    sums = jnp.concatenate([jnp.zeros((3, D), WIDE), sums, jnp.zeros((4, D), WIDE)], axis=0)

    @pl.when(step == 0)
    def _():
        small_ref[...] = sums

    @pl.when(step > 0)
    def _():
        small_ref[...] += sums

    scaled = routed_grad * rows_ref[15:16, :].astype(WIDE)
    residual_grad = up + spread * (scaled - unit * jnp.mean(scaled * unit, axis=-1, keepdims=True))
    residual_grad_ref[...] = residual_grad
    cot = residual_grad.astype(HALF)
    cot_ref[...] = cot
    mixed_grad_ref[...] = nn(cot, w_out[0]).astype(HALF)


def attend_back_kernel(
    query, k2, k1, k0, v2, v1, v0, query_ids, key_ids, mixed_grad, mixed, logs, cos_ref, sin_ref, query_grad, grad2, grad1,
    grad0, bias, keys, values, key_total, value_total
):
    step = pl.program_id(0)

    @pl.when(step == 0)
    def _():
        fill_bias(query_ids, key_ids, bias)

    load_window((k2, k1, k0), keys)
    load_window((v2, v1, v0), values)
    upper = upper_of()
    span = 5 * TILE
    count = query.shape[1]

    def turned_back(gradient, place, rows):
        cosine, sine = cos_ref[place, rows, :], sin_ref[place, rows, :]
        return (gradient * cosine - partner(gradient) * sine).astype(HALF)

    key_total[...] = jnp.zeros_like(key_total)
    value_total[...] = jnp.zeros_like(value_total)
    for tile in range(2):
        rows = slice(tile * TILE, (tile + 1) * TILE)
        window = slice(tile * TILE, tile * TILE + span)
        results = []
        for head in range(2):
            chosen = head_lanes(head, TILE)
            nothing = jnp.zeros((), HALF)
            own = jnp.where(chosen, query[0, rows, :], nothing)
            out_grad = jnp.where(chosen, mixed_grad[rows, :], nothing)
            level = logs[rows, head * HD : head * HD + 1]
            ends, middle = folded(upper, nt(own, keys[window, :]))
            ends = jnp.exp(ends + bias[tile, :, :TILE] - level)
            middle = jnp.exp(middle + bias[tile, :, TILE:] - level)
            value_total[:, window] += nn(out_grad.T, unfolded(upper, ends, middle))
            ends_grad, middle_grad = folded(upper, nt(out_grad, values[window, :]))
            product = out_grad.astype(WIDE) * mixed[rows, :].astype(WIDE)
            expected = jnp.sum(product, axis=-1, keepdims=True)
            score_grad = unfolded(upper, ends * (ends_grad - expected), middle * (middle_grad - expected))
            key_total[:, window] += nn(own.T, score_grad)
            results.append(nn(score_grad, keys[window, :]))
        gradient = jnp.where(head_lanes(0, TILE), results[0], results[1]) * HD ** (-0.5)
        query_grad[rows, :] = turned_back(gradient, 2, rows)
    for place, grad in enumerate((grad2, grad1, grad0)):
        window = slice(place * count, (place + 1) * count)
        grad[0] = turned_back(key_total[:, window].T, place, slice(0, count))
        grad[1] = value_total[:, window].T.astype(HALF)


def weight_sums(group):
    normed = group[0:3]
    query_grad = group[3]
    pair_grads = group[4:7]
    cot, mixed, tall, routed, extra, early = group[7:13]
    small = nn(tall[...].T[:SMALL], routed[...])
    lower = extra[0:4, :] + early[0:4, :]
    small = small + jnp.concatenate([jnp.zeros((SMALL - 4, lower.shape[1]), WIDE), lower], axis=0)
    key = value = 0.0
    for place in range(3):
        flipped = normed[place][0].T
        key = key + nn(flipped, pair_grads[place][0])
        value = value + nn(flipped, pair_grads[place][1])
    query = nn(flipped, query_grad[...])
    return (query, key, value, nn(cot[...].T, mixed[...])), small


def first_weight_kernel(*refs):
    grads, small = weight_sums(refs[:13])
    for place, grad in enumerate(grads):
        refs[13][place] = grad
    refs[14][...] = small


def weight_kernel(slots, *refs):
    grads, small = weight_sums(refs[:13])
    earlier, earlier_small, weights, rows_ref, theirs, mine = refs[13:]
    query, key, value, out = (grad + earlier[place] for place, grad in enumerate(grads))
    small = small + earlier_small[...]
    step = pl.program_id(0)
    norm = 0.0
    deep = out.shape[0]
    rows = pl.ds(pl.multiple_of(step * deep, deep), deep)
    for place, grad in enumerate((query, key, value, out)):
        if place < 3:
            norm = norm + jnp.sum(grad * weights[place].astype(WIDE), axis=-1, keepdims=True)
        half = grad.astype(HALF)
        slot = slots[place]

        @pl.when(slot < 2)
        def _():
            theirs[jnp.minimum(slot, 1), rows, :] = half

        @pl.when(slot >= 2)
        def _():
            mine[jnp.maximum(slot - 2, 0), rows, :] = half

    gain = rows_ref[14:15, :].astype(WIDE)
    norm_row = jnp.broadcast_to(norm, (deep, PAIR)).T[0:1, :] / gain
    row = lax.broadcasted_iota(jnp.int32, small.shape, 0)
    small = jnp.where(row == 14, norm_row, small).astype(HALF)
    theirs[step, D : D + SMALL, :] = small
    mine[step, D : D + SMALL, :] = small


def fold_kernel(mine, received, sent, kept):
    for place, out in ((0, sent), (1, kept)):
        out[:D, :] = (mine[place, :D].astype(WIDE) + received[place, :D].astype(WIDE)).astype(HALF)
        for half in range(2):
            small = mine[half, D:].astype(WIDE) + received[half, D:].astype(WIDE)
            out[D + half * SMALL : D + (half + 1) * SMALL, :] = small.astype(HALF)


def split_kernel(index, kept, received, *outs):
    size = len(outs)
    deep = D // size
    width = kept.shape[1]

    def total(rows):
        return (kept[rows, :].astype(WIDE) + received[rows, :].astype(WIDE)).astype(HALF)

    small = jnp.concatenate(
        [total(slice(D + half * SMALL, D + (half + 1) * SMALL)) for half in range(2)], axis=1
    )
    for distance, out in enumerate(outs):
        place = lax.rem(index[0] + distance, size)
        out[:deep, :] = total(pl.ds(pl.multiple_of(place * deep, deep), deep))
        part = small[:, :deep]
        for other in range(1, size):
            part = jnp.where(place == other, small[:, other * deep : (other + 1) * deep], part)
        out[deep:, :] = jnp.concatenate([part, jnp.zeros((SMALL, width - deep), HALF)], axis=1)


def relay_kernel(flag, far, near, out):
    out[...] = (
        far[...].astype(WIDE) + jnp.where(flag[0] == 1, near[...].astype(WIDE), 0.0)
    ).astype(HALF)


def input_kernel(query_grad, grad0, near, far, flag, weights, out_ref):
    keep = flag[0] == 0
    totals = []
    for kind in range(2):
        total = grad0[kind].astype(WIDE) + far[kind].astype(WIDE)
        total = total + jnp.where(keep, near[kind].astype(WIDE), 0.0)
        totals.append(total.astype(HALF))
    out_ref[...] = (
        nt(query_grad[...], weights[0]) + nt(totals[0], weights[1]) + nt(totals[1], weights[2])
    ).astype(HALF)


def layer_kernel(seqs, *refs):
    step = pl.program_id(0)
    for seq in range(seqs):
        base, own, other = refs[seq * 3 : seq * 3 + 3]

        @pl.when(step == seq)
        def _():
            summed = own[...].astype(WIDE) + other[...].astype(WIDE)
            refs[-1][0] = (base[...] + summed).astype(HALF)


def final_kernel(seqs, *refs):
    x_ref, rows_ref = refs[:2]
    step = pl.program_id(0)
    for seq in range(seqs):
        residual_grad, own, other = refs[2 + seq * 3 : 5 + seq * 3]

        @pl.when(step == seq)
        def _():
            tensor = x_ref[0].astype(WIDE)
            spread = spread_of(tensor)
            unit = tensor * spread
            gradient = own[...].astype(WIDE) + other[...].astype(WIDE)
            scaled = gradient * rows_ref[14:15, :].astype(WIDE)
            refs[-1][0] = residual_grad[...] + spread * (
                scaled - unit * jnp.mean(scaled * unit, axis=-1, keepdims=True)
            )


def pack_kernel(flag, query, key, value, out, *refs):
    packed = refs[-1]
    deep, width = query.shape
    half = deep // 2
    start = pl.multiple_of(flag[0] * half, half)
    for place, matrix in enumerate((query, key, value, out)):
        packed[place * half : (place + 1) * half, :] = matrix[pl.ds(start, half), :].astype(HALF)
    rows = jnp.concatenate([ref[...] for ref in refs[:-1]], axis=0)
    rows = jnp.concatenate([rows, jnp.zeros((SMALL, width - deep), WIDE)], axis=1)
    packed[4 * half :, :] = rows.astype(HALF)


def cast_kernel(order, *refs):
    for kind in range(3):
        refs[-1][kind] = refs[kind][...].astype(HALF)


def order_kernel(index, *refs):
    parts, out = refs[:-1], refs[-1]
    size = len(parts)
    for distance, part in enumerate(parts):
        out[lax.rem(index[0] + size - distance, size)] = part[...]


def join_kernel(flag, own, other, out):
    half = own.shape[1]
    for place in range(own.shape[0]):
        first, second = own[place], other[place]
        start = place * 2 * half
        out[0, start : start + half, :] = jnp.where(flag[0] == 0, first, second)
        out[0, start + half : start + 2 * half, :] = jnp.where(flag[0] == 0, second, first)


def place_kernel(order, *refs):
    outs = refs[-3:]
    part = refs[0].shape[-1]
    for expert in range(2):
        for core, (own, across) in enumerate(
            (refs[4 * expert : 4 * expert + 2], refs[4 * expert + 2 : 4 * expert + 4])
        ):
            for far in range(2):
                lanes = pl.ds(pl.multiple_of(order[3 - far - 2 * core] * part, part), part)
                for kind in range(3):
                    if len(own.shape) == 4:
                        block = own[1 - far, kind].astype(WIDE) + across[far, kind].astype(WIDE)
                    else:
                        block = (across if far else own)[kind].astype(WIDE)
                    outs[kind][expert, :, lanes] = block


def unpack_kernel(slots, own, across, near, far, *outs):
    for place, out in enumerate(outs):
        block = jnp.where(slots[place] == 3, own[...].astype(WIDE), across[...].astype(WIDE))
        block = jnp.where(slots[place] == 1, near[...].astype(WIDE), block)
        block = jnp.where(slots[place] == 0, far[...].astype(WIDE), block)
        out[...] = block[: out.shape[0]]


def swap(block, axis):
    size = lax.axis_size(axis)
    return lax.ppermute(block, axis, [(i, i ^ 1) for i in range(size)])


def shift(block, axis, distance):
    size = lax.axis_size(axis)
    route = [(i, i + distance) for i in range(size) if 0 <= i + distance < size]
    return lax.ppermute(block, axis, route)


def pick(stack, index, axis=0):
    return lax.dynamic_index_in_dim(stack, index, axis, keepdims=False)


def scatter_rows(tensor, dimension):
    return lax.psum_scatter(tensor, "fsdp", scatter_dimension=dimension, tiled=True)


def ring(block, distance):
    size = lax.axis_size("fsdp")
    return lax.ppermute(block, "fsdp", [(i, (i + distance) % size) for i in range(size)])


def gather_blocks(block):
    size = lax.axis_size("fsdp")
    if size > 4:
        return lax.all_gather(block, "fsdp", axis=0)
    blocks = [block] + [ring(block, distance) for distance in range(1, size)]
    if block.shape[0] % 16 == 0:
        parts = whole(block.shape)
        out = (size,) + block.shape
        index = lax.axis_index("fsdp").reshape(1).astype(jnp.int32)
        return call(
            "order",
            order_kernel,
            (1,),
            [parts] * size,
            [(whole(out), struct(out, HALF))],
            prefetch=1,
        )(index, *blocks)[0]
    stacked = jnp.stack(blocks[::-1] * 2)
    start = size - 1 - lax.axis_index("fsdp")
    return lax.dynamic_slice_in_dim(stacked, start, size, axis=0)


def scatter_blocks(blocks):
    size = lax.axis_size("fsdp")
    if size > 4:
        return lax.psum_scatter(blocks, "fsdp", scatter_dimension=0)
    index = lax.axis_index("fsdp")
    total = pick(blocks, index).astype(WIDE)
    for distance in range(1, size):
        sent = pick(blocks, lax.rem(index + distance, size))
        total = total + ring(sent, distance).astype(WIDE)
    return total.astype(blocks.dtype)


def shards(
    block_in,
    cotangent,
    prev_logits,
    routes,
    segments,
    w_query,
    w_key,
    w_value,
    w_out,
    w_gate,
    w_up,
    w_down,
    router,
    const_proj,
    const_vec,
    norm_attn,
    norm_moe,
):
    seqs, count = block_in.shape[:2]
    width = w_query.shape[1]
    pairs = width // PAIR
    deep = w_gate.shape[1]
    hidden = w_gate.shape[2]
    hi, lo = lax.axis_index("hi"), lax.axis_index("lo")
    hi_size = lax.axis_size("hi")
    ctx = hi * 2 + lo
    ctx_size = hi_size * 2
    fsdp_size = lax.axis_size("fsdp")
    part = hidden // ctx_size
    order = jnp.stack([(1 - hi) * 2 + 1 - lo, hi * 2 + 1 - lo, (1 - hi) * 2 + lo, ctx]).astype(
        jnp.int32
    )

    flag = lo.reshape(1).astype(jnp.int32)

    positions = (ctx - 2) * count + jnp.arange(3 * count, dtype=jnp.int32)
    lane = jnp.arange(PAIR, dtype=jnp.int32)
    frequency = 10000.0 ** (-2.0 * (lane % (HD // 2)).astype(WIDE) / HD)
    turned = positions.astype(WIDE)[:, None] * frequency[None, :]
    cosine = jnp.cos(turned).reshape(3, count, PAIR)
    sine = (jnp.sin(turned) * jnp.where((lane & (HD // 2)) == 0, -1.0, 1.0)).reshape(3, count, PAIR)

    rank_rows, rank_columns = call(
        "rank",
        rank_kernel,
        (seqs,),
        [
            pl.BlockSpec((1, 2, count), lambda s: (s, 0, 0)),
            pl.BlockSpec((1, count, 2), lambda s: (s, 0, 0)),
        ],
        [
            (pl.BlockSpec((1, ALL, count), lambda s: (s, 0, 0)), struct((seqs, ALL, count), WIDE)),
            (pl.BlockSpec((1, count, ALL), lambda s: (s, 0, 0)), struct((seqs, count, ALL), WIDE)),
        ],
    )(routes.transpose(0, 2, 1), routes)

    half = deep // 2
    rows = 4 * half + SMALL
    rows = rows + -rows % 16
    narrow = (router.T, const_proj.T, const_vec.T, norm_attn[None, :], norm_moe[None, :])
    if half % 16 == 0:
        operands = (w_query, w_key, w_value, w_out) + narrow
        matrix_own = call(
            "pack",
            pack_kernel,
            (1,),
            [pl.BlockSpec(memory_space=pltpu.SMEM)] + [whole(array.shape) for array in operands],
            [(whole((rows, width)), struct((rows, width), HALF))],
        )(flag, *operands)[0]
    else:
        matrix_own = [
            lax.dynamic_slice_in_dim(w, lo * half, half, axis=0)
            for w in (w_query, w_key, w_value, w_out)
        ]
        small_rows = jnp.concatenate(narrow, axis=0)
        small_rows = jnp.pad(small_rows, ((0, rows - 4 * half - SMALL), (0, width - deep)))
        matrix_own = jnp.concatenate(matrix_own + [small_rows], axis=0).astype(HALF)

    def join_matrices(own):
        other = swap(own, "lo")
        if half % 16 == 0:
            block = pl.BlockSpec((fsdp_size, half, width), lambda kind: (0, kind, 0))
            return call(
                "join",
                join_kernel,
                (4,),
                [pl.BlockSpec(memory_space=pltpu.SMEM), block, block],
                [
                    (
                        pl.BlockSpec((1, D, width), lambda kind: (kind, 0, 0)),
                        struct((4, D, width), HALF),
                    )
                ],
            )(flag, own, other)[0]
        halves = [
            blocks[:, : 4 * half].reshape(fsdp_size, 4, half, width) for blocks in (own, other)
        ]
        halves = jnp.stack(
            [jnp.where(lo == 0, *halves), jnp.where(lo == 0, *halves[::-1])], axis=2
        )
        return halves.transpose(1, 0, 2, 3, 4).reshape(4, D, width)

    expert_own = call(
        "cast",
        cast_kernel,
        (EXPERTS,),
        [pl.BlockSpec((1, deep, part), lambda e, o: (e, 0, o[3]))] * 3,
        [
            (
                pl.BlockSpec((3, 1, deep, part), lambda e, o: (0, e, 0, 0)),
                struct((3, EXPERTS, deep, part), HALF),
            )
        ],
        prefetch=1,
    )(order, w_gate, w_up, w_down)[0]

    far_rows = shift(block_in, "hi", 1)
    matrix_own = gather_blocks(matrix_own)
    matrix_own, expert_own, far_rows, cosine, sine, rank_rows, rank_columns = lax.optimization_barrier(
        (matrix_own, expert_own, far_rows, cosine, sine, rank_rows, rank_columns)
    )
    expert_weights = lax.all_gather(expert_own, CTX + ("fsdp",), axis=0).reshape(
        ctx_size, fsdp_size, 3, EXPERTS, deep, part
    )
    if deep % 16:
        expert_weights = expert_weights.transpose(0, 2, 3, 1, 4, 5).reshape(
            ctx_size, 1, 3, EXPERTS, D, part
        )
    matrices = join_matrices(matrix_own)
    small_rows = matrix_own[:, 4 * half : 4 * half + SMALL, :deep]
    small_rows = small_rows.transpose(1, 0, 2).reshape(SMALL, D)
    near_rows = swap(jnp.where(lo == 1, far_rows, block_in), "lo")
    far_ids = shift(segments, "hi", 1)
    near_ids = swap(jnp.where(lo == 1, far_ids, segments), "lo")
    far_ids = jnp.where(hi == 0, -1, far_ids)
    near_ids = jnp.where(ctx == 0, -1, near_ids)
    key_ids = jnp.concatenate([far_ids, near_ids, segments], axis=1)[:, None, :]
    query_ids = segments[:, :, None]

    def project(rows, place, with_query, after=()):
        spread = struct((seqs, count, width), HALF)
        by_seq = pl.BlockSpec((1, count, width), lambda s: (s, 0, 0))
        by_row = pl.BlockSpec((1, count, D), lambda s: (s, 0, 0))
        kinds = 3 if with_query else 2
        return call(
            f"project{place}",
            functools.partial(project_kernel, with_query),
            (seqs,),
            [
                by_row,
                whole((SMALL, D)),
                fixed((1, count, PAIR), (place, 0, 0)),
                fixed((1, count, PAIR), (place, 0, 0)),
                whole((3, D, width)),
            ],
            [(by_row, struct((seqs, count, D), HALF))] + [(by_seq, spread)] * kinds,
            after=after,
        )(rows, small_rows, cosine, sine, matrices)

    normed0, key0, value0, query = project(block_in, 2, True, (near_rows,))
    normed1, key1, value1 = project(near_rows, 1, False)
    normed2, key2, value2 = project(far_rows, 0, False)

    def pair_block(seq):
        return pl.BlockSpec((1, count, PAIR), lambda p, seq=seq: (seq, 0, p))

    flat_pair = pl.BlockSpec((count, PAIR), lambda p: (0, p))
    window_scratch = [
        pltpu.VMEM((2, TILE, 4 * TILE), WIDE),
        pltpu.VMEM((3 * count, PAIR), HALF),
        pltpu.VMEM((3 * count, PAIR), HALF),
    ]
    product = 2 * 2 * TILE * 5 * TILE * 256 * 2 * pairs

    def attend(seq):
        return call(
            f"attend{seq}",
            attend_kernel,
            (pairs,),
            [pair_block(seq)] * 7
            + [
                fixed((1, count, 1), (seq, 0, 0)),
                fixed((1, 1, 3 * count), (seq, 0, 0)),
                pl.BlockSpec((1, D, PAIR), lambda p: (3, 0, p)),
            ],
            [
                (flat_pair, struct((count, width), HALF)),
                (flat_pair, struct((count, width), WIDE)),
                (whole((count, D)), struct((count, D), HALF)),
            ],
            window_scratch + [pltpu.VMEM((count, D), WIDE)],
        )(query, key2, key1, key0, value2, value1, value0, query_ids, key_ids, matrices)

    mixed, logs, attended, attended_other = [], [], [], []
    for seq in range(seqs):
        one, two, three = attend(seq)
        mixed.append(one)
        logs.append(two)
        attended.append(three)
        attended_other.append(swap(three, "tp"))

    flat = whole((count, D))
    flat_small = whole((count, SIDE))

    def one_seq(seq, columns):
        return fixed((1, count, columns), (seq, 0, 0))

    tiles = 4
    tile = count // tiles

    def tile_rows(columns):
        return pl.BlockSpec((tile, columns), lambda t: (t, 0))

    def tile_seq(seq, columns):
        return pl.BlockSpec((1, tile, columns), lambda t: (seq, t, 0))

    routed, targets, bases, earlies = [], [], [], []
    for seq in range(seqs):
        results = call(
            f"route{seq}",
            route_kernel,
            (tiles,),
            [
                tile_seq(seq, D),
                tile_rows(D),
                tile_rows(D),
                tile_seq(seq, D),
                whole((SMALL, D)),
                tile_seq(seq, 2),
                tile_seq(seq, ALL),
            ],
            [
                (tile_rows(D), struct((count, D), HALF)),
                (tile_rows(SIDE), struct((count, SIDE), WIDE)),
                (tile_rows(D), struct((count, D), WIDE)),
                (whole((8, D)), struct((8, D), WIDE)),
            ],
        )(
            block_in,
            attended[seq],
            attended_other[seq],
            cotangent,
            small_rows,
            routes,
            prev_logits,
        )
        for kept, result in zip((routed, targets, bases, earlies), results, strict=True):
            kept.append(result)

    slots = seqs * MOST
    weight_shape = expert_weights.shape
    weight_block = (1,) + weight_shape[1:2] + (3, 1) + weight_shape[4:]
    piece = (1, 3, D, part)
    out_slots, grad_slots, held, crossing = [], [], [], []
    scattered = [None] * EXPERTS

    def finish(expert, total):
        scattered[expert] = scatter_rows(total, total.ndim - 2)

    slot_out = (
        pl.BlockSpec((1, slots, D), lambda e: (e, 0, 0)),
        struct((EXPERTS, slots, D), HALF),
    )
    slot_rows, slot_cots = call(
        "dispatch",
        dispatch_kernel,
        (EXPERTS,),
        [flat, flat, whole((seqs, count, D)), flat_small, flat_small, whole((seqs, ALL, count))],
        [slot_out, slot_out],
    )(routed[0], routed[1], cotangent, targets[0], targets[1], rank_rows)
    for expert in range(EXPERTS):
        theirs, mine, one, two, *totals = call(
            f"expert{expert}",
            expert_kernel,
            (ctx_size,),
            [
                fixed((1, slots, D), (expert, 0, 0)),
                fixed((1, slots, D), (expert, 0, 0)),
                pl.BlockSpec(
                    weight_block, lambda j, o, expert=expert: (o[j], 0, 0, expert, 0, 0)
                ),
            ],
            [
                (
                    pl.BlockSpec(piece, lambda j, o: (jnp.minimum(j, 1), 0, 0, 0)),
                    struct((2, 3, D, part), HALF),
                ),
                (
                    pl.BlockSpec(piece, lambda j, o: (jnp.maximum(j - 2, 0), 0, 0, 0)),
                    struct((2, 3, D, part), HALF),
                ),
                (whole((slots, D)), struct((slots, D), HALF)),
                (whole((slots, D)), struct((slots, D), HALF)),
            ],
            [
                pltpu.VMEM((D, slots), HALF),
                pltpu.VMEM((D, slots), HALF),
                pltpu.VMEM((slots, D), WIDE),
                pltpu.VMEM((slots, D), WIDE),
            ],
            prefetch=1,
            side=[side_sum(ctx_size, held[expert - 2])] if expert >= 2 else (),
            after=out_slots[-1:],
        )(order, slot_rows, slot_cots, expert_weights)
        out_slots.append(one)
        grad_slots.append(two)
        held.append((mine, swap(theirs, "lo")))
        if totals:
            finish(expert - 2, totals[0].reshape(2, 3, D, part))

    def couple_of(place):
        return scattered[place], swap(scattered[place], "hi")

    back, back_other, sums, sums_other = [], [], [], []
    for seq in range(seqs):
        slot_block = fixed((MOST, D), (seq, 0))
        one, two, sent = call(
            f"combine{seq}",
            combine_kernel,
            (tiles,),
            [slot_block] * (2 * EXPERTS)
            + [tile_seq(seq, ALL), tile_rows(SIDE), tile_seq(seq, D)],
            [
                (tile_rows(D + PAIR), struct((count, D + PAIR), HALF)),
                (tile_rows(D), struct((count, D), HALF)),
            ],
            side=[side_sum(tiles, held[2 + seq], 0)],
        )(*out_slots, *grad_slots, rank_columns, targets[seq], cotangent)
        back.append(one)
        sums.append(two)
        back_other.append(swap(one, "tp"))
        crossing.append(swap(sent, "hi"))

    residual_grads, cots, mixed_grads, extras, talls = [], [], [], [], []
    def turn(seq):
        results = call(
            f"turn{seq}",
            turn_kernel,
            (tiles,),
            [
                tile_seq(seq, D),
                tile_rows(D),
                tile_rows(D),
                tile_seq(seq, D),
                tile_rows(D + PAIR),
                tile_rows(D + PAIR),
                tile_rows(SIDE),
                whole((SMALL, D)),
                fixed((1, D, width), (3, 0, 0)),
            ],
            [
                (tile_rows(D), struct((count, D), WIDE)),
                (tile_rows(D), struct((count, D), HALF)),
                (tile_rows(width), struct((count, width), HALF)),
                (whole((8, D)), struct((8, D), WIDE)),
                (tile_rows(PAIR), struct((count, PAIR), HALF)),
            ],
            side=[side_sum(tiles, held[2], 1, (crossing[0],))] if seq else (),
            after=(query_grads[0],) if seq else (),
        )(
            block_in,
            attended[seq],
            attended_other[seq],
            cotangent,
            back[seq],
            back_other[seq],
            targets[seq],
            small_rows,
            matrices,
        )
        for kept, result in zip(
            (residual_grads, cots, mixed_grads, extras, talls), results[:5], strict=True
        ):
            kept.append(result)
        if seq:
            finish(2, results[5].reshape(3, D, part))

    query_grads, grads2, grads1, grads0 = [], [], [], []
    pair_out = (
        pl.BlockSpec((2, count, PAIR), lambda p: (0, 0, p)),
        struct((2, count, width), HALF),
    )
    table = whole((3, count, PAIR))
    near_grads, far_grads, sents = [], [], []

    def attend_back(seq):
        results = call(
            f"back{seq}",
            attend_back_kernel,
            (pairs,),
            [pair_block(seq)] * 7
            + [
                fixed((1, count, 1), (seq, 0, 0)),
                fixed((1, 1, 3 * count), (seq, 0, 0)),
                flat_pair,
                flat_pair,
                flat_pair,
                table,
                table,
            ],
            [(flat_pair, struct((count, width), HALF))] + [pair_out] * 3,
            window_scratch
            + [pltpu.VMEM((PAIR, 3 * count), WIDE), pltpu.VMEM((PAIR, 3 * count), WIDE)],
            after=(sents[0], sums_other[0]) if seq else (crossing[0],),
            side=[side_sum(pairs, held[3], 1, (crossing[1],))] if seq else (),
        )(
            query,
            key2,
            key1,
            key0,
            value2,
            value1,
            value0,
            query_ids,
            key_ids,
            mixed_grads[seq],
            mixed[seq],
            logs[seq],
            cosine,
            sine,
        )
        for kept, result in zip((query_grads, grads2, grads1, grads0), results[:4], strict=True):
            kept.append(result)
        near_grads.append(swap(results[2], "lo"))
        if seq:
            finish(3, results[4].reshape(3, D, part))

    def send_back(seq, after):
        sents.append(
            call(
                f"relay{seq}",
                relay_kernel,
                (2,),
                [pl.BlockSpec(memory_space=pltpu.SMEM)]
                + [pl.BlockSpec((1, count, width), lambda kind: (kind, 0, 0))] * 2,
                [
                    (
                        pl.BlockSpec((1, count, width), lambda kind: (kind, 0, 0)),
                        struct((2, count, width), HALF),
                    )
                ],
                after=after,
            )(flag, grads2[seq], near_grads[seq])[0]
        )
        far_grads.append(shift(sents[seq], "hi", -1))

    def enter(seq, after):
        one = call(
            f"input{seq}",
            input_kernel,
            (tiles // 2,),
            [
                pl.BlockSpec((2 * tile, width), lambda t: (t, 0)),
            ]
            + [pl.BlockSpec((2, 2 * tile, width), lambda t: (0, t, 0))] * 3
            + [
                pl.BlockSpec(memory_space=pltpu.SMEM),
                whole((3, D, width)),
            ],
            [
                (
                    pl.BlockSpec((2 * tile, D), lambda t: (t, 0)),
                    struct((count, D), HALF),
                )
            ],
            after=after,
        )(query_grads[seq], grads0[seq], near_grads[seq], far_grads[seq], flag, matrices)[0]
        input_parts.append(one)
        input_others.append(swap(one, "tp"))

    input_parts, input_others = [], []
    def send_sums(seq):
        sums[seq], mixed_grads[seq] = lax.optimization_barrier((sums[seq], mixed_grads[seq]))
        sums_other.append(swap(sums[seq], "tp"))

    turn(0)
    send_sums(0)
    attend_back(0)
    couples = [couple_of(0)]
    turn(1)
    send_sums(1)
    columns = D // 2

    def by_column(rows):
        return pl.BlockSpec((rows, columns), lambda t, *_: (0, t))

    def weight_operands(seq):
        return (
            [normed2, normed1, normed0, query_grads[seq], grads2[seq], grads1[seq], grads0[seq]]
            + [cots[seq], mixed[seq], talls[seq], routed[seq], extras[seq], earlies[seq]]
        )

    def weight_specs(seq):
        return (
            [pl.BlockSpec((1, count, columns), lambda t, *_: (seq, 0, t))] * 3
            + [whole((count, width))]
            + [whole((2, count, width))] * 3
            + [by_column(count), whole((count, width)), whole((count, PAIR))]
            + [by_column(count), by_column(8), by_column(8)]
        )

    first_sums = call(
        "first",
        first_weight_kernel,
        (2,),
        weight_specs(0),
        [
            (
                pl.BlockSpec((4, columns, width), lambda t, *_: (0, t, 0)),
                struct((4, D, width), WIDE),
            ),
            (by_column(SMALL), struct((SMALL, D), WIDE)),
        ],
        after=(extras[1],),
    )(*weight_operands(0))
    send_back(0, (first_sums[1],))
    attend_back(1)
    enter(0, (query_grads[1],))
    couples.append(couple_of(1))
    send_back(1, (input_parts[0],))
    couples.append(couple_of(2))

    def half_map(seq):
        last = 1 if seq == 0 else 0
        return lambda s, t: (jnp.where(s == seq, t, last), 0)

    part_shape = (2, D + SMALL, width)
    slots_of = jnp.stack(
        [2 * (lo == place % 2).astype(jnp.int32) + (hi == place // 2) for place in range(4)]
    ).astype(jnp.int32)
    theirs, mine = call(
        "weight",
        weight_kernel,
        (2,),
        weight_specs(1)
        + [
            pl.BlockSpec((4, columns, width), lambda t, *_: (0, t, 0)),
            by_column(SMALL),
            pl.BlockSpec((3, columns, width), lambda t, *_: (0, t, 0)),
            by_column(SMALL),
        ],
        [(whole(part_shape), struct(part_shape, HALF))] * 2,
        prefetch=1,
        after=(sents[1],),
    )(slots_of, *weight_operands(1), *first_sums, matrices, small_rows)
    received = swap(theirs, "lo")
    enter(1, (input_others[0],))
    received, input_parts[1] = lax.optimization_barrier((received, input_parts[1]))
    input_others[1] = swap(input_parts[1], "tp")

    rest_shape = (D + 2 * SMALL, width)
    sent, kept = call(
        "fold",
        fold_kernel,
        (1,),
        [whole(part_shape)] * 2,
        [(whole(rest_shape), struct(rest_shape, HALF))] * 2,
    )(mine, received)
    crossed = swap(sent, "hi")
    layer_out = call(
        "layer",
        functools.partial(layer_kernel, seqs),
        (seqs, 2),
        [
            pl.BlockSpec((2 * tile, D), half_map(seq))
            for seq in range(seqs)
            for _ in range(3)
        ],
        [
            (
                pl.BlockSpec((1, 2 * tile, D), lambda s, t: (s, t, 0)),
                struct((seqs, count, D), HALF),
            )
        ],
        after=(input_parts[1],),
    )(*[array for seq in range(seqs) for array in (bases[seq], sums[seq], sums_other[seq])])[0]
    if fsdp_size <= 4:
        block = (deep + SMALL, width)
        blocks = list(
            call(
                "split",
                split_kernel,
                (1,),
                [whole(rest_shape)] * 2,
                [(whole(block), struct(block, HALF))] * fsdp_size,
                prefetch=1,
                after=(layer_out, input_others[1]),
            )(lax.axis_index("fsdp").reshape(1).astype(jnp.int32), kept, crossed)
        )
        own = blocks[0].astype(WIDE)
        for distance in range(1, fsdp_size):
            own = own + ring(blocks[distance], distance).astype(WIDE)
        own = own.astype(HALF)
    else:
        total = kept + crossed
        rest = jnp.concatenate([total[D : D + SMALL], total[D + SMALL :]], axis=1)
        rest = rest.reshape(SMALL, fsdp_size, deep).transpose(1, 0, 2)
        rest = jnp.pad(rest, ((0, 0), (0, 0), (0, width - deep)))
        own = scatter_blocks(
            jnp.concatenate([total[:D].reshape(fsdp_size, deep, width), rest], axis=1)
        )
    couples.append(couple_of(3))

    by_tile = pl.BlockSpec((1, tile, D), lambda s, t: (s, t, 0))
    operands, specs = [block_in, small_rows], [by_tile, whole((SMALL, D))]
    for seq in range(seqs):
        operands += [residual_grads[seq], input_parts[seq], input_others[seq]]
        last = tiles - 1 if seq == 0 else 0
        specs += [
            pl.BlockSpec(
                (tile, D), lambda s, t, seq=seq, last=last: (jnp.where(s == seq, t, last), 0)
            )
        ] * 3
    grad_input = call(
        "final",
        functools.partial(final_kernel, seqs),
        (seqs, tiles),
        specs,
        [
            (by_tile, struct((seqs, count, D), WIDE)),
        ],
    )(*operands)[0]

    own, grad_input = lax.optimization_barrier((own, grad_input))
    small = own[deep:, :deep].astype(WIDE)
    norm_grad = small[14] + swap(small[14], "tp")
    across = swap(own, "hi")
    sources = (own, across, swap(own, "lo"), swap(across, "lo"))

    result = struct((EXPERTS, deep, hidden), WIDE)
    steps = 3 if deep % 48 == 0 else 1

    def by_rows(shape):
        lead = (0,) * (len(shape) - 2)
        return pl.BlockSpec(
            shape[:-2] + (shape[-2] // steps, shape[-1]), lambda t, *_: lead + (t, 0)
        )

    grads = None
    for group in (couples[:2], couples[2:]):
        operands = []
        for couple in group:
            operands += list(couple) + [swap(array, "lo") for array in couple]
        previous = [] if grads is None else list(grads)
        grads = call(
            f"place{len(previous)}",
            place_kernel,
            (steps,),
            [by_rows(array.shape) for array in operands]
            + [pl.BlockSpec(memory_space=pl.ANY)] * len(previous),
            [
                (
                    pl.BlockSpec(
                        (2, deep // steps, hidden),
                        lambda t, *_, half=1 if previous else 0: (half, t, 0),
                    ),
                    result,
                )
            ]
            * 3,
            prefetch=1,
            aliases={1 + len(operands) + kind: kind for kind in range(3)} if previous else None,
            after=() if previous else (input_parts[1],),
        )(order, *operands, *previous)

    matrix = struct((deep, width), WIDE)
    matrix_grads = call(
        "unpack",
        unpack_kernel,
        (1,),
        [whole(own.shape)] * 4,
        [(whole((deep, width)), matrix)] * 4,
        prefetch=1,
        after=(grads[0],),
    )(slots_of, *sources)

    return (
        layer_out,
        grad_input,
        *matrix_grads,
        *grads,
        small[0:8].T,
        small[8:12].T,
        small[12:14].T,
        norm_grad,
        small[15],
    )


def solution(mesh):
    sizes = mesh.shape
    inner = Mesh(
        mesh.devices.reshape(sizes["fsdp"], sizes["ctx"] // 2, 2, sizes["tp"]),
        ("fsdp", "hi", "lo", "tp"),
    )
    rows = P("fsdp", CTX, None)
    matrix = P("fsdp", "tp")
    experts = P(None, "fsdp", "tp")
    narrow = P("fsdp", None)
    vector = P("fsdp")
    return jax.shard_map(
        shards,
        mesh=inner,
        in_specs=(rows,) * 4
        + (P("fsdp", CTX),)
        + (matrix,) * 4
        + (experts,) * 3
        + (narrow,) * 3
        + (vector,) * 2,
        out_specs=(rows,) * 2
        + (matrix,) * 4
        + (experts,) * 3
        + (narrow,) * 3
        + (vector,) * 2,
        check_vma=False,
    )
```
